32 devices in a mesh: fsdp: 4 (over x, core), ctx: 2 (over y), tp: 4 (over z).
Axes of the slice: x: 2, y: 2, z: 4, core: 2. Of those that a mesh axis runs over, the one named last changes fastest.
Arguments:
- inputs: bfloat16 [8, 1536, 1536], P('fsdp', 'ctx'), may hold values from -6 to 6
- cotangent: bfloat16 [8, 1536, 1536], P('fsdp', 'ctx'), may hold values from -6 to 6
- positions: int32 [8, 1536], P('fsdp', 'ctx'), may hold values from 0 to 3070, as said below
- attn_gain: bfloat16 [1536], P('fsdp'), may hold values from 0.5 to 1.5
- query_weight: bfloat16 [1536, 1536], P('fsdp', 'tp'), may hold values from -0.15625 to 0.15625
- query_bias: bfloat16 [12, 128], P('tp', 'fsdp'), may hold values from -3 to 3
- key_weight: bfloat16 [1536, 256], P('fsdp'), may hold values from -0.15625 to 0.15625
- key_bias: bfloat16 [2, 128], P(None, 'fsdp'), may hold values from -3 to 3
- value_weight: bfloat16 [1536, 256], P('fsdp'), may hold values from -0.15625 to 0.15625
- value_bias: bfloat16 [2, 128], P(None, 'fsdp'), may hold values from -3 to 3
- output_weight: bfloat16 [1536, 1536], P('tp', 'fsdp'), may hold values from -0.3125 to 0.3125
- mlp_gain: bfloat16 [1536], P('fsdp'), may hold values from 0.5 to 1.5
- gate_weight: bfloat16 [1536, 8960], P('fsdp', 'tp'), may hold values from -0.15625 to 0.15625
- up_weight: bfloat16 [1536, 8960], P('fsdp', 'tp'), may hold values from -0.15625 to 0.15625
- down_weight: bfloat16 [8960, 1536], P('tp', 'fsdp'), may hold values from -0.0625 to 0.0625
Outputs:
- outputs: bfloat16 [8, 1536, 1536], P('fsdp', 'ctx')
- input_grad: float32 [8, 1536, 1536], P('fsdp', 'ctx')
- attn_gain_grad: float32 [1536], P('fsdp')
- query_weight_grad: float32 [1536, 1536], P('fsdp', 'tp')
- query_bias_grad: float32 [12, 128], P('tp', 'fsdp')
- key_weight_grad: float32 [1536, 256], P('fsdp')
- key_bias_grad: float32 [2, 128], P(None, 'fsdp')
- value_weight_grad: float32 [1536, 256], P('fsdp')
- value_bias_grad: float32 [2, 128], P(None, 'fsdp')
- output_weight_grad: float32 [1536, 1536], P('tp', 'fsdp')
- mlp_gain_grad: float32 [1536], P('fsdp')
- gate_weight_grad: float32 [1536, 8960], P('fsdp', 'tp')
- up_weight_grad: float32 [1536, 8960], P('fsdp', 'tp')
- down_weight_grad: float32 [8960, 1536], P('tp', 'fsdp')
The draws below stay inside these ranges and needn't reach their ends.
Inputs may be any that keep to these rules, and one draw needn't show every extreme that they name: `positions`: each row starts at 0 and rises by 1 or 2 from one token to the next.
All inputs are finite; a program needn't handle non-finite values.
Results may differ from the reference program's by a relative error of at most 0.025.
Values may be sent and summed in bfloat16 or wider, within the bound.
No kernel may reach another device: no remote copies, remote signals or barrier semaphores. Data moves between devices by JAX's collectives and lax.ppermute only.
A program may use at most 320 MiB of HBM per device.

```python
import math
import jax
import jax.numpy as jnp
from jax import lax

D = 1536
H = 12
KV = 2
HD = 128
FF = 8960
LEN = 1536
SEQS = 8


def draw_positions(key, part):
    key = jax.random.fold_in(key, 3)
    steps = jax.random.randint(key, (SEQS, LEN - 1), 1, 3).astype(jnp.int32)
    steps = steps.at[SEQS - 1].set(2)
    zeros = jnp.zeros((SEQS, 1), jnp.int32)
    return jnp.concatenate([zeros, jnp.cumsum(steps, axis=1).astype(jnp.int32)], axis=1).astype(jnp.int32)


def levels(key, dims, pieces, low, top_value):
    loudness, own = 1.0, jax.random.fold_in(key, 6)
    for axis_at, parts in pieces:
        steps = jnp.exp(jax.random.uniform(jax.random.fold_in(own, axis_at), (parts,), jnp.float32, low / len(pieces), top_value / len(pieces)))
        loudness = loudness * jnp.repeat(steps, dims[axis_at] // parts).reshape([-1 if axis == axis_at else 1 for axis in range(len(dims))])
    return loudness


def noise(own_key, dims, deviation, bound, cuts=(), kind=jnp.bfloat16):
    drawn = jax.random.normal(own_key, dims, jnp.float32) * deviation
    if len(cuts) > 0:
        drawn = levels(own_key, dims, cuts, -0.22, 0.18) * drawn
    return jnp.clip(drawn, min=-bound, max=bound).astype(kind)


def setup_inputs(seed: int = 0) -> dict:
    arg_keys = jax.random.split(jax.random.key(seed), 16)
    inputs = noise(arg_keys[0], (SEQS, LEN, D), 1.0, 6.0, ((0, 4), (1, 2)))
    cotangent = noise(arg_keys[1], (SEQS, LEN, D), 1.0, 6.0, ((0, 4), (1, 2)))
    positions = draw_positions(jax.random.fold_in(arg_keys[15], 71), 0)
    attn_gain = jnp.clip(1.0 + 0.1 * jax.random.normal(arg_keys[3], (D,), jnp.float32), 0.5, 1.5).astype(jnp.bfloat16)
    query_weight = noise(arg_keys[4], (D, H * HD), D ** -0.5, 0.15625, ((0, 4), (1, 4)))
    query_bias = noise(arg_keys[5], (H, HD), 0.5, 3.0, ((0, 4), (1, 4)))
    key_weight = noise(arg_keys[6], (D, KV * HD), D ** -0.5, 0.15625, ((0, 4),))
    key_bias = noise(arg_keys[7], (KV, HD), 0.5, 3.0, ((1, 4),))
    value_weight = noise(arg_keys[8], (D, KV * HD), D ** -0.5, 0.15625, ((0, 4),))
    value_bias = noise(arg_keys[9], (KV, HD), 0.5, 3.0, ((1, 4),))
    output_weight = noise(arg_keys[10], (H * HD, D), (H * HD // 4) ** -0.5, 0.3125, ((0, 4), (1, 4)))
    mlp_gain = jnp.clip(1.0 + 0.1 * jax.random.normal(arg_keys[11], (D,), jnp.float32), 0.5, 1.5).astype(jnp.bfloat16)
    gate_weight = noise(arg_keys[12], (D, FF), D ** -0.5, 0.15625, ((0, 4), (1, 4)))
    up_weight = noise(arg_keys[13], (D, FF), D ** -0.5, 0.15625, ((0, 4), (1, 4)))
    down_weight = noise(arg_keys[14], (FF, D), FF ** -0.5, 0.0625, ((0, 4), (1, 4)))
    return {"inputs": inputs, "cotangent": cotangent, "positions": positions, "attn_gain": attn_gain, "query_weight": query_weight, "query_bias": query_bias, "key_weight": key_weight, "key_bias": key_bias, "value_weight": value_weight, "value_bias": value_bias, "output_weight": output_weight, "mlp_gain": mlp_gain, "gate_weight": gate_weight, "up_weight": up_weight, "down_weight": down_weight}


EPS = 1e-06
THETA = 1000000.0

@jax.custom_vjp
def low(v):
    return lax.optimization_barrier(v.astype(jnp.bfloat16)).astype(jnp.float32)

@jax.custom_vjp
def low_back(v):
    return v

def low_keep(v):
    return (low(v), None)

def low_pass(kept, grad):
    return (grad,)

def back_keep(v):
    return (v, None)

def back_low(kept, grad):
    return (low(grad),)
low.defvjp(low_keep, low_pass)
low_back.defvjp(back_keep, back_low)

def matmul_high(left, right):
    return jnp.dot(left, right, precision=lax.Precision.HIGHEST, preferred_element_type=jnp.float32)

def rope_tables(position, width):
    half = width // 2
    freqs = jnp.exp(jnp.arange(half, dtype=jnp.float32) * (-2.0 * math.log(THETA) / width))
    angle = position.astype(jnp.float32)[..., None] * freqs
    angle = jnp.concatenate([angle, angle], axis=-1)
    return (jnp.cos(angle), jnp.sin(angle))

def rotate(values):
    half = values.shape[-1] // 2
    return jnp.concatenate([-values[..., half:], values[..., :half]], axis=-1)

def rms_scale(values, gain):
    return values * lax.rsqrt(lax.optimization_barrier(jnp.mean(values * values, axis=-1, keepdims=True)) + EPS) * gain

def decoder_layer(seq_in, seq_pos, params):
    attn_gain, query_weight, query_bias, key_weight, key_bias, value_weight, value_bias, output_weight, mlp_gain, gate_weight, up_weight, down_weight = params
    normed_one = low(rms_scale(seq_in, attn_gain))
    cosine, sine = rope_tables(seq_pos, HD)
    query_lin = low_back(matmul_high(normed_one, query_weight) + query_bias.reshape(-1)).reshape(LEN, H, HD)
    queries = low(query_lin * cosine[:, None] + rotate(query_lin) * sine[:, None])
    key_lin = low_back(matmul_high(normed_one, key_weight) + key_bias.reshape(-1)).reshape(LEN, KV, HD)
    keys = low(key_lin * cosine[:, None] + rotate(key_lin) * sine[:, None])
    values = low_back(low(matmul_high(normed_one, value_weight) + value_bias.reshape(-1))).reshape(LEN, KV, HD)
    key_rep = jnp.repeat(keys, H // KV, axis=1)
    value_rep = jnp.repeat(values, H // KV, axis=1)
    block = min(512, LEN)
    scale = 1.0 / math.sqrt(HD)

    def one_block(index):
        start = (index * block).astype(jnp.int32)
        query_blk = lax.dynamic_slice_in_dim(queries, start, block, 0)
        pos_blk = lax.dynamic_slice_in_dim(seq_pos, start, block, 0)
        logits = low_back(jnp.einsum('ihd,jhd->hij', query_blk, key_rep, precision=lax.Precision.HIGHEST) * scale)
        visible = seq_pos[None, :] <= pos_blk[:, None]
        logits = jnp.where(visible[None], logits, -1e+30)
        peak = lax.optimization_barrier(jnp.max(logits, axis=-1, keepdims=True))
        log_total = peak + jnp.log(lax.optimization_barrier(jnp.sum(jnp.exp(logits - peak), axis=-1, keepdims=True)))
        probs = low(jnp.exp(logits - log_total))
        return jnp.einsum('hij,jhd->ihd', probs, value_rep, precision=lax.Precision.HIGHEST)
    attended = lax.map(jax.checkpoint(one_block), jnp.arange(LEN // block, dtype=jnp.int32))
    attended = low_back(low(attended.reshape(LEN, H * HD)))
    branch = low_back(matmul_high(attended, output_weight))
    hidden_state = seq_in + branch
    normed_two = low(rms_scale(hidden_state, mlp_gain))
    gate = low_back(matmul_high(normed_two, gate_weight))
    up_part = low_back(matmul_high(normed_two, up_weight))
    act = low(jax.nn.silu(gate) * up_part)
    mixed = low_back(matmul_high(act, down_weight))
    return hidden_state + mixed

def reference(inputs, cotangent, positions, attn_gain, query_weight, query_bias, key_weight, key_bias, value_weight, value_bias, output_weight, mlp_gain, gate_weight, up_weight, down_weight):
    params = tuple((w.astype(jnp.float32) for w in (attn_gain, query_weight, query_bias, key_weight, key_bias, value_weight, value_bias, output_weight, mlp_gain, gate_weight, up_weight, down_weight)))

    def per_sequence(carry, item):
        seq_in, seq_cot, seq_pos = item
        result, pull = jax.vjp(lambda first, second: decoder_layer(first, seq_pos, second), seq_in.astype(jnp.float32), params)
        seq_grad, param_grads = pull(seq_cot.astype(jnp.float32))
        carry = jax.tree.map(lambda total, term: total + term, carry, param_grads)
        return (carry, (result.astype(jnp.bfloat16), seq_grad))
    zeros = jax.tree.map(jnp.zeros_like, params)
    grads, (outputs, input_grad) = lax.scan(per_sequence, zeros, (inputs, cotangent, positions))
    return (outputs, input_grad, grads[0], grads[1], grads[2], grads[3], grads[4], grads[5], grads[6], grads[7], grads[8], grads[9], grads[10], grads[11])
```

```python
import functools
import math

import jax
import jax.numpy as jnp
from jax import lax
from jax.experimental import pallas as pl
from jax.experimental.pallas import tpu as pltpu
from jax.sharding import PartitionSpec as P

EPS = 1e-06
THETA = 1000000.0
LOG2E = 1.0 / math.log(2.0)
LOW = jnp.bfloat16
MASKED = -1e30
MIB = 1024 * 1024


def rope_tables(position, width):
    half = width // 2
    freqs = jnp.exp(jnp.arange(half, dtype=jnp.float32) * (-2.0 * math.log(THETA) / width))
    angle = position.astype(jnp.float32)[..., None] * freqs
    cosine, sine = jnp.cos(angle), jnp.sin(angle)
    return (
        jnp.concatenate([cosine, cosine], axis=-1),
        jnp.concatenate([-sine, sine], axis=-1),
    )


def dot(left, right):
    return jnp.dot(left, right, preferred_element_type=jnp.float32)


def inner_rows(left, right):
    return lax.dot_general(
        left, right, (((0,), (0,)), ((), ())), preferred_element_type=jnp.float32
    )


def inner_cols(left, right):
    return lax.dot_general(
        left, right, (((1,), (1,)), ((), ())), preferred_element_type=jnp.float32
    )


def add_low(left, right):
    return (left.astype(jnp.float32) + right.astype(jnp.float32)).astype(LOW)


def root_of(values):
    return lax.rsqrt(jnp.mean(values * values, axis=-1, keepdims=True) + EPS)


FSDP, TP, BEFORE, PLACE = 0, 1, 2, 3


def shard_at(meta, flip, size):
    return pl.multiple_of(jnp.bitwise_xor(meta[FSDP], flip) * size, size)


def tp_at(meta, hop, tps, size):
    return pl.multiple_of(lax.rem(meta[TP] + tps - hop, tps) * size, size)


def call(kernel, grid, in_specs, out_specs, out_shape, scratch=(), cost=None, name=None, vmem=48):
    return pl.pallas_call(
        kernel,
        grid_spec=pltpu.PrefetchScalarGridSpec(
            num_scalar_prefetch=1,
            grid=grid,
            in_specs=in_specs,
            out_specs=out_specs,
            scratch_shapes=list(scratch),
        ),
        out_shape=out_shape,
        compiler_params=pltpu.CompilerParams(vmem_limit_bytes=vmem * MIB),
        cost_estimate=cost,
        name=name,
    )


def whole(array):
    return pl.BlockSpec(array.shape, lambda *_: (0,) * array.ndim)


def shape(dims, kind):
    return jax.ShapeDtypeStruct(dims, kind)


def project_kernel(
    local_heads, kv_heads, head_dim, meta, x_ref, gain_ref, bias_ref, w_ref, wx_ref, wc_ref,
    cos_ref, sin_ref, n_ref, q_ref, kv_ref,
):
    rows = x_ref.shape[1]
    size = n_ref.shape[1] // 4
    height = w_ref.shape[0]
    values = x_ref[...].reshape(rows, -1).astype(jnp.float32)
    n_ref[...] = (values * root_of(values) * gain_ref[...]).astype(LOW)
    lin = bias_ref[...]
    for flip, weight in enumerate(
        (w_ref[:size, :], wc_ref[:size, :], wx_ref[:size, :], wc_ref[height : height + size, :])
    ):
        lin = lin + dot(n_ref[:, pl.ds(shard_at(meta, flip, size), size)], weight)
    cosine, sine = cos_ref[...], sin_ref[...]
    for head in range(local_heads + 2 * kv_heads):
        part = lin[:, head * head_dim : (head + 1) * head_dim]
        if head < local_heads + kv_heads:
            part = part * cosine + pltpu.roll(part, head_dim // 2, 1) * sine
        if head < local_heads:
            q_ref[0, :, head * head_dim : (head + 1) * head_dim] = part.astype(LOW)
        else:
            at = (head - local_heads) * head_dim
            kv_ref[:, at : at + head_dim] = part.astype(LOW)


def project(meta, inputs, gain, bias, weights, cosine, sine, sizes):
    seq_count, block_len, width = inputs.shape
    local_heads, kv_heads, head_dim, tps = sizes
    own = block_len // tps
    q_cols, kv_cols = local_heads * head_dim, 2 * kv_heads * head_dim

    def row(i, m):
        return (i, 0)

    def device(i, m):
        seq, place = i // tps, i % tps
        return jnp.where(seq % 2 == 0, place, tps - 1 - place), seq, 0

    tokens = seq_count * block_len
    return call(
        functools.partial(project_kernel, local_heads, kv_heads, head_dim),
        (seq_count * tps,),
        [
            pl.BlockSpec((1, own, width), lambda i, m: (i // tps, i % tps, 0)),
            whole(gain), whole(bias), *(whole(w) for w in weights),
            pl.BlockSpec((own, head_dim), row), pl.BlockSpec((own, head_dim), row),
        ],
        [
            pl.BlockSpec((own, width), row),
            pl.BlockSpec((1, own, q_cols), device),
            pl.BlockSpec((own, kv_cols), row),
        ],
        [
            shape((tokens, width), LOW),
            shape((tps, seq_count * own, q_cols), LOW),
            shape((tokens, kv_cols), LOW),
        ],
        cost=pl.CostEstimate(
            flops=2 * tokens * width * (q_cols + kv_cols), bytes_accessed=8 * tokens * width, transcendentals=0
        ),
        name="project",
    )(meta, inputs, gain, bias, *weights, cosine, sine)


def fwd_kernel(
    heads, block, parts, meta, *refs
):
    q_refs, (kb_ref, vb_ref, k_ref, v_ref, order_ref, o_ref, lse_ref, qg_ref, acc_ref, m_ref, l_ref) = (
        refs[:parts], refs[parts:]
    )
    own, cols = q_refs[0].shape[1:]
    head_dim = acc_ref.shape[0]
    scale = LOG2E / math.sqrt(head_dim)
    each = cols // head_dim
    for head in range(heads):
        qg_ref[head * own : (head + 1) * own, :] = q_refs[head // each][
            0, :, (head % each) * head_dim : (head % each + 1) * head_dim
        ]
    acc_ref[...] = jnp.zeros_like(acc_ref)
    m_ref[...] = jnp.full_like(m_ref, MASKED)
    l_ref[...] = jnp.zeros_like(l_ref)
    first = meta[PLACE + pl.program_id(0)] * own
    last = first // block

    def step(key_ref, value_ref, index, masked):
        start = pl.multiple_of(index * block, block)
        keys = key_ref[pl.ds(start, block), :]
        values = value_ref[pl.ds(start, block), :]
        logits = inner_cols(keys, qg_ref[...]) * scale
        if masked:
            key_order = (start - first) + lax.broadcasted_iota(jnp.int32, logits.shape, 0)
            logits = jnp.where(key_order <= order_ref[...], logits, MASKED)
        before = m_ref[...]
        peak = jnp.maximum(before, jnp.max(logits, axis=0, keepdims=True))
        weights = jnp.exp2(logits - peak)
        fade = jnp.exp2(before - peak)
        m_ref[...] = peak
        l_ref[...] = l_ref[...] * fade + jnp.sum(weights, axis=0, keepdims=True)
        acc_ref[...] = acc_ref[...] * fade + inner_rows(values, weights.astype(LOW))

    def early(index, carry):
        step(kb_ref, vb_ref, index, False)
        return carry

    def late(index, carry):
        step(k_ref, v_ref, index, False)
        return carry

    lax.fori_loop(0, meta[BEFORE], early, 0)
    lax.fori_loop(0, last, late, 0)
    step(k_ref, v_ref, last, True)
    total = l_ref[...]
    lse_ref[...] = (m_ref[...] + jnp.log2(total)).reshape(lse_ref.shape)
    mixed = jnp.transpose(acc_ref[...] / total)
    for head in range(heads):
        o_ref[:, head * head_dim : (head + 1) * head_dim] = mixed[
            head * own : (head + 1) * own, :
        ].astype(LOW)


def bwd_kernel(heads, block, parts, meta, *refs):
    q_refs, (
        kb_ref, vb_ref, k_ref, v_ref, order_ref, o_ref, g_ref, lse_ref, cos_ref, sin_ref,
        dq_ref, db_ref, dd_ref, qg_ref, gg_ref, acc_ref,
    ) = refs[:parts], refs[parts:]
    own, cols = q_refs[0].shape[1:]
    head_dim = acc_ref.shape[1]
    scale = 1.0 / math.sqrt(head_dim)
    each = cols // head_dim
    for head in range(heads):
        rows = slice(head * own, (head + 1) * own)
        at = slice(head * head_dim, (head + 1) * head_dim)
        qg_ref[rows, :] = q_refs[head // each][
            0, :, (head % each) * head_dim : (head % each + 1) * head_dim
        ]
        gg_ref[rows, :] = g_ref[:, at]
        acc_ref[rows, :] = g_ref[:, at].astype(jnp.float32) * o_ref[:, at].astype(jnp.float32)
    center = jnp.sum(jnp.transpose(acc_ref[...]), axis=0, keepdims=True)
    acc_ref[...] = jnp.zeros_like(acc_ref)
    lse = lse_ref[...].reshape(order_ref.shape)
    first = meta[PLACE + pl.program_id(0)] * own
    last = first // block

    def step(key_ref, value_ref, out_ref, index, masked):
        start = pl.multiple_of(index * block, block)
        keys = key_ref[pl.ds(start, block), :]
        values = value_ref[pl.ds(start, block), :]
        logits = inner_cols(keys, qg_ref[...]) * (scale * LOG2E)
        if masked:
            key_order = (start - first) + lax.broadcasted_iota(jnp.int32, logits.shape, 0)
            logits = jnp.where(key_order <= order_ref[...], logits, MASKED)
        probs = jnp.exp2(logits - lse)
        out_ref[1, 0, pl.ds(start, block), :] = dot(probs.astype(LOW), gg_ref[...]).astype(LOW)
        prob_grad = inner_cols(values, gg_ref[...])
        logit_grad = (probs * (prob_grad - center)).astype(LOW)
        out_ref[0, 0, pl.ds(start, block), :] = (dot(logit_grad, qg_ref[...]) * scale).astype(LOW)
        acc_ref[...] += inner_rows(logit_grad, keys)

    def early(index, carry):
        step(kb_ref, vb_ref, db_ref, index, False)
        return carry

    def late(index, carry):
        step(k_ref, v_ref, dd_ref, index, False)
        return carry

    def clear(ref):
        def body(index, carry):
            start = pl.multiple_of(index * block, block)
            ref[:, :, pl.ds(start, block), :] = jnp.zeros((2, 1, block, head_dim), LOW)
            return carry

        return body

    lax.fori_loop(0, meta[BEFORE], early, 0)
    lax.fori_loop(meta[BEFORE], kb_ref.shape[0] // block, clear(db_ref), 0)
    lax.fori_loop(0, last, late, 0)
    step(k_ref, v_ref, dd_ref, last, True)
    lax.fori_loop(last + 1, k_ref.shape[0] // block, clear(dd_ref), 0)
    for head in range(heads):
        grad = acc_ref[head * own : (head + 1) * own, :] * scale
        grad = grad * cos_ref[...] - pltpu.roll(grad, head_dim // 2, 1) * sin_ref[...]
        dq_ref[:, head * head_dim : (head + 1) * head_dim] = grad.astype(LOW)


def attention_specs(queries, kv_before, kv_own, sizes):
    seq_count, kv_heads, head_dim, tps = sizes
    rows = queries.shape[1] // seq_count
    parts = tps // kv_heads
    heads = queries.shape[2] * parts // head_dim
    before, block_len = kv_before.shape[0] // seq_count, kv_own.shape[0] // seq_count

    def piece(index):
        return pl.BlockSpec(
            (1, rows, queries.shape[2]),
            lambda s, g, m: (lax.rem(m[TP] + tps - (g * parts + index), tps), s, 0),
        )

    specs = [piece(index) for index in range(parts)] + [
        pl.BlockSpec((before, head_dim), lambda s, g, m: (s, g)),
        pl.BlockSpec((before, head_dim), lambda s, g, m: (s, kv_heads + g)),
        pl.BlockSpec((block_len, head_dim), lambda s, g, m: (s, g)),
        pl.BlockSpec((block_len, head_dim), lambda s, g, m: (s, kv_heads + g)),
        pl.BlockSpec((1, heads * rows), lambda s, g, m: (0, 0)),
    ]
    return specs, rows, parts, heads, before, block_len


def attend(meta, queries, kv_before, kv_own, order, block, sizes):
    seq_count, kv_heads, head_dim, tps = sizes
    specs, rows, parts, heads, before, block_len = attention_specs(queries, kv_before, kv_own, sizes)
    width, wide = kv_heads * heads * head_dim, heads * rows
    work = seq_count * rows * width * (before + block_len)
    return call(
        functools.partial(fwd_kernel, heads, block, parts),
        (seq_count, kv_heads),
        specs,
        [
            pl.BlockSpec((rows, heads * head_dim), lambda s, g, m: (s, g)),
            pl.BlockSpec((1, 1, 1, wide), lambda s, g, m: (s, g, 0, 0)),
        ],
        [shape((seq_count * rows, width), LOW), shape((seq_count, kv_heads, 1, wide), jnp.float32)],
        [
            pltpu.VMEM((wide, head_dim), LOW),
            pltpu.VMEM((head_dim, wide), jnp.float32),
            pltpu.VMEM((1, wide), jnp.float32),
            pltpu.VMEM((1, wide), jnp.float32),
        ],
        cost=pl.CostEstimate(flops=8 * work, bytes_accessed=1 << 22, transcendentals=0),
        name="attend",
    )(meta, *([queries] * parts), kv_before, kv_before, kv_own, kv_own, order)


def attend_back(meta, queries, kv_before, kv_own, order, mixed, grads, lse, cosine, sine, block, sizes):
    seq_count, kv_heads, head_dim, tps = sizes
    specs, rows, parts, heads, before, block_len = attention_specs(queries, kv_before, kv_own, sizes)
    width, wide = kv_heads * heads * head_dim, heads * rows
    work = seq_count * rows * width * (before + block_len)
    wide_spec = pl.BlockSpec((rows, heads * head_dim), lambda s, g, m: (s, g))
    table_spec = pl.BlockSpec((rows, head_dim), lambda s, g, m: (s * tps + m[PLACE + s], 0))
    return call(
        functools.partial(bwd_kernel, heads, block, parts),
        (seq_count, kv_heads),
        specs
        + [
            wide_spec,
            wide_spec,
            pl.BlockSpec((1, 1, 1, wide), lambda s, g, m: (s, g, 0, 0)),
            table_spec,
            table_spec,
        ],
        [
            wide_spec,
            pl.BlockSpec((2, 1, before, head_dim), lambda s, g, m: (0, g, s, 0)),
            pl.BlockSpec((2, 1, block_len, head_dim), lambda s, g, m: (0, g, s, 0)),
        ],
        [
            shape((seq_count * rows, width), LOW),
            shape((2, kv_heads, seq_count * before, head_dim), LOW),
            shape((2, kv_heads, seq_count * block_len, head_dim), LOW),
        ],
        [
            pltpu.VMEM((wide, head_dim), LOW),
            pltpu.VMEM((wide, head_dim), LOW),
            pltpu.VMEM((wide, head_dim), jnp.float32),
        ],
        cost=pl.CostEstimate(flops=16 * work, bytes_accessed=1 << 23, transcendentals=0),
        name="attend_back",
    )(
        meta, *([queries] * parts), kv_before, kv_before, kv_own, kv_own, order,
        mixed, grads, lse, cosine, sine,
    )


def merge_kernel(tps, meta, o_ref, x_ref, w_ref, wx_ref, wc_ref, gain_ref, h_ref, n_ref, turned_ref):
    rows, width = h_ref.shape
    size, depth = width // 4, o_ref.shape[1]
    part = depth // tps
    for hop in range(tps):
        turned_ref[:, hop * part : (hop + 1) * part] = o_ref[:, pl.ds(tp_at(meta, hop, tps, part), part)]
    turned = turned_ref[...]
    for flip, weight in enumerate((w_ref[...], wc_ref[:depth, :], wx_ref[...], wc_ref[depth:, :])):
        at = pl.ds(shard_at(meta, flip, size), size)
        h_ref[:, at] = x_ref[0, :, at].astype(jnp.float32) + dot(turned, weight)
    hidden = h_ref[...]
    n_ref[...] = (hidden * root_of(hidden) * gain_ref[...]).astype(LOW)


def merge(meta, mixed, inputs, weights, gain, tps):
    seq_count, block_len, width = inputs.shape
    own = block_len // tps
    depth = mixed.shape[1]
    row = pl.BlockSpec((own, width), lambda s, m: (s, 0))
    return call(
        functools.partial(merge_kernel, tps),
        (seq_count,),
        [
            pl.BlockSpec((own, depth), lambda s, m: (s, 0)),
            pl.BlockSpec((1, own, width), lambda s, m: (s, m[PLACE + s], 0)),
            *(whole(w) for w in weights),
            whole(gain),
        ],
        [row, row],
        [shape((seq_count * own, width), jnp.float32), shape((seq_count * own, width), LOW)],
        [pltpu.VMEM((own, depth), LOW)],
        cost=pl.CostEstimate(
            flops=2 * seq_count * own * depth * width, bytes_accessed=1 << 23, transcendentals=0
        ),
        name="merge",
    )(meta, mixed, inputs, *weights, gain)


def turn_kernel(
    tps, meta, a_ref, b_ref, h_ref, c_ref, w_ref, wx_ref, wc_ref, gain_ref,
    hg_ref, bg_ref, ag_ref, term_ref, turned_ref,
):
    rows, width = h_ref.shape
    size, depth = width // 4, ag_ref.shape[1]
    part = depth // tps
    two_grad = a_ref[...].astype(jnp.float32) + b_ref[...].astype(jnp.float32)
    hidden = h_ref[...]
    root = root_of(hidden)
    term_ref[...] = jnp.sum(two_grad * hidden * root, axis=0, keepdims=True).reshape(term_ref.shape)
    scaled = gain_ref[...] * two_grad
    grad = (
        c_ref[...].reshape(rows, width).astype(jnp.float32)
        + root * scaled
        - hidden * root**3 * jnp.mean(scaled * hidden, axis=-1, keepdims=True)
    )
    hg_ref[...] = grad
    bg_ref[...] = grad.astype(LOW)
    turned_ref[...] = jnp.zeros_like(turned_ref)
    for flip, weight in enumerate((w_ref[...], wc_ref[:depth, :], wx_ref[...], wc_ref[depth:, :])):
        turned_ref[...] += inner_cols(bg_ref[:, pl.ds(shard_at(meta, flip, size), size)], weight)
    for hop in range(tps):
        ag_ref[:, pl.ds(tp_at(meta, hop, tps, part), part)] = turned_ref[
            :, hop * part : (hop + 1) * part
        ].astype(LOW)


def turn(meta, two_own, two_got, hidden, cotangent, weights, gain, depth, tps):
    seq_count, block_len, width = cotangent.shape
    own = block_len // tps
    row = pl.BlockSpec((own, width), lambda s, m: (s, 0))
    tokens = seq_count * own
    return call(
        functools.partial(turn_kernel, tps),
        (seq_count,),
        [
            row, row, row,
            pl.BlockSpec((1, own, width), lambda s, m: (s, m[PLACE + s], 0)),
            *(whole(w) for w in weights),
            whole(gain),
        ],
        [
            row, row,
            pl.BlockSpec((own, depth), lambda s, m: (s, 0)),
            pl.BlockSpec((1, 1, width), lambda s, m: (s, 0, 0)),
        ],
        [
            shape((tokens, width), jnp.float32),
            shape((tokens, width), LOW),
            shape((tokens, depth), LOW),
            shape((seq_count, 1, width), jnp.float32),
        ],
        [pltpu.VMEM((own, depth), jnp.float32)],
        cost=pl.CostEstimate(flops=2 * tokens * depth * width, bytes_accessed=1 << 23, transcendentals=0),
        name="turn",
    )(meta, two_own, two_got, hidden, cotangent, *weights, gain)


def finish_kernel(
    kv_heads, head_dim, meta, g_ref, a_ref, b_ref, cos_ref, sin_ref, q_ref, w_ref, wx_ref, wc_ref,
    x_ref, hg_ref, gain_ref, out_ref, kv_ref, term_ref, one_ref,
):
    rows, width = hg_ref.shape
    size, height = width // 4, w_ref.shape[0]
    cosine, sine = cos_ref[...], sin_ref[...]
    for kind in range(2):
        for head in range(kv_heads):
            grad = (
                a_ref[kind, head, 0].astype(jnp.float32) + b_ref[kind, head, 0].astype(jnp.float32)
            )
            if kind == 0:
                grad = grad * cosine - pltpu.roll(grad, head_dim // 2, 1) * sine
            at = (kind * kv_heads + head) * head_dim
            kv_ref[:, at : at + head_dim] = grad.astype(LOW)
    one_ref[...] = inner_cols(g_ref[...], q_ref[...])
    skip = w_ref.shape[1] - kv_ref.shape[1]
    for flip, weight in enumerate(
        (
            w_ref[:size, skip:], wc_ref[:size, skip:], wx_ref[:size, skip:],
            wc_ref[height : height + size, skip:],
        )
    ):
        one_ref[:, pl.ds(shard_at(meta, flip, size), size)] += inner_cols(kv_ref[...], weight)
    one = one_ref[...]
    values = x_ref[...].reshape(rows, width).astype(jnp.float32)
    root = root_of(values)
    term_ref[...] = jnp.sum(one * values * root, axis=0, keepdims=True).reshape(term_ref.shape)
    scaled = gain_ref[...] * one
    out_ref[...] = (
        hg_ref[...]
        + root * scaled
        - values * root**3 * jnp.mean(scaled * values, axis=-1, keepdims=True)
    ).astype(LOW)


def finish(meta, q_grad, kv_mine, kv_got, cosine, sine, q_full, weights, inputs, hidden_grad, gain, tps):
    seq_count, block_len, width = inputs.shape
    own = block_len // tps
    kv_heads, head_dim = kv_mine.shape[1], kv_mine.shape[4]
    kv_cols = 2 * kv_heads * head_dim
    tokens = seq_count * own
    row = pl.BlockSpec((own, width), lambda s, m: (s, 0))
    kv_spec = pl.BlockSpec((2, kv_heads, 1, own, head_dim), lambda s, m: (0, 0, s, 0, 0))
    table_spec = pl.BlockSpec((own, head_dim), lambda s, m: (s * tps + m[PLACE + s], 0))
    return call(
        functools.partial(finish_kernel, kv_heads, head_dim),
        (seq_count,),
        [
            pl.BlockSpec((own, q_grad.shape[1]), lambda s, m: (s, 0)),
            kv_spec, kv_spec, table_spec, table_spec,
            whole(q_full),
            *(whole(w) for w in weights),
            pl.BlockSpec((1, own, width), lambda s, m: (s, m[PLACE + s], 0)),
            row,
            whole(gain),
        ],
        [
            row,
            pl.BlockSpec((own, kv_cols), lambda s, m: (s, 0)),
            pl.BlockSpec((1, 1, width), lambda s, m: (s, 0, 0)),
        ],
        [
            shape((tokens, width), LOW),
            shape((tokens, kv_cols), LOW),
            shape((seq_count, 1, width), jnp.float32),
        ],
        [pltpu.VMEM((own, width), jnp.float32)],
        cost=pl.CostEstimate(
            flops=2 * tokens * (q_grad.shape[1] + kv_cols) * width, bytes_accessed=1 << 23, transcendentals=0
        ),
        name="finish",
    )(meta, q_grad, kv_mine, kv_got, cosine, sine, q_full, *weights, inputs, hidden_grad, gain)


class Links:
    def __init__(self):
        self.tp, self.ctx, self.fsdp = (lax.axis_index(a) for a in ("tp", "ctx", "fsdp"))
        self.tps, self.ctxs, self.fsdps = (lax.axis_size(a) for a in ("tp", "ctx", "fsdp"))
        self.core, self.x = self.fsdp % 2, self.fsdp // 2
        assert self.fsdps == 4

    def to_core(self, value):
        return lax.ppermute(value, "fsdp", [(0, 1), (1, 0), (2, 3), (3, 2)])

    def to_x(self, value):
        return lax.ppermute(value, "fsdp", [(0, 2), (2, 0), (1, 3), (3, 1)])

    def to_y(self, value):
        return lax.ppermute(value, "ctx", [(0, 1), (1, 0)])

    def hop_tp(self, value, hop=1):
        return lax.ppermute(value, "tp", [(i, (i + hop) % self.tps) for i in range(self.tps)])

    def gather_fsdp(self, shard):
        across = self.to_x(shard)
        return shard, across, self.to_core(jnp.concatenate([shard, across], axis=0))

    def gather_tp(self, block):
        blocks = [block]
        for _ in range(1, self.tps):
            blocks.append(self.hop_tp(blocks[-1]))
        return blocks

    def scatter_tp(self, blocks):
        total = blocks[1]
        for hop in range(1, self.tps):
            got = self.hop_tp(total)
            if hop < self.tps - 1:
                total = add_low(blocks[hop + 1], got)
        return blocks[0], got

    def at(self, hop):
        return (self.tp - hop + self.tps) % self.tps

    def scatter_fsdp(self, value, axis):
        size = value.shape[axis] // 4

        def pair(core):
            return jnp.concatenate(
                [
                    lax.dynamic_slice_in_dim(value, (2 * x + core) * size, size, axis)
                    for x in range(2)
                ],
                axis,
            )

        both = add_low(pair(self.core), self.to_core(pair(1 - self.core)))
        away = lax.dynamic_slice_in_dim(both, (1 - self.x) * size, size, axis)
        keep = lax.dynamic_slice_in_dim(both, self.x * size, size, axis)
        return add_low(keep, self.to_x(away))

    def sum_ctx(self, value):
        value = lax.optimization_barrier(value.astype(LOW))
        if self.ctxs == 2:
            return value.astype(jnp.float32) + self.to_y(value).astype(jnp.float32)
        return lax.psum(value.astype(jnp.float32), "ctx")

    def reduce_weight(self, term, axis):
        part = lax.psum_scatter(
            term.astype(LOW), ("fsdp", "ctx"), scatter_dimension=axis, tiled=True
        )
        if self.ctxs == 2:
            part = lax.optimization_barrier(part)
            got = self.to_y(part)
            low = jnp.where(self.ctx == 0, part, got)
            high = jnp.where(self.ctx == 0, got, part)
            full = jnp.concatenate([low, high], axis)
        else:
            full = lax.all_gather(part, "ctx", axis=axis, tiled=True)
        return full.astype(jnp.float32)


def local(
    inputs,
    cotangent,
    positions,
    attn_gain,
    query_weight,
    query_bias,
    key_weight,
    key_bias,
    value_weight,
    value_bias,
    output_weight,
    mlp_gain,
    gate_weight,
    up_weight,
    down_weight,
):
    links = Links()
    seq_count, block_len, width = inputs.shape
    tp, tps, ctx, ctxs = links.tp, links.tps, links.ctx, links.ctxs
    fsdp, fsdps = links.fsdp, links.fsdps
    own = block_len // tps
    local_heads, kv_heads = query_bias.shape[0], key_bias.shape[0]
    head_dim = key_weight.shape[1] // kv_heads
    q_cols = local_heads * head_dim
    kv_cols = 2 * kv_heads * head_dim
    depth = q_cols * tps
    shard = width // fsdps
    tokens = seq_count * block_len
    key_block = block_len // 2 if block_len % (2 * own) == 0 else block_len
    seqs = range(seq_count)

    def place(seq, device):
        return device if seq % 2 == 0 else tps - 1 - device

    def block_rows(value, hop):
        return jnp.concatenate(
            [
                lax.dynamic_slice_in_dim(value[s], place(s, links.at(hop)) * own, own, 0)
                for s in seqs
            ],
            axis=0,
        )

    meta = jnp.stack(
        [fsdp, tp, ctx * (block_len // key_block)] + [place(s, tp) for s in seqs]
    ).astype(jnp.int32)

    down_full = lax.all_gather(down_weight, "fsdp", axis=1, tiled=True)
    gate_full = lax.all_gather(gate_weight, "fsdp", axis=0, tiled=True)
    up_full = lax.all_gather(up_weight, "fsdp", axis=0, tiled=True)
    q_full = lax.all_gather(
        lax.all_gather(query_weight, "tp", axis=1, tiled=True), "fsdp", axis=0, tiled=True
    )

    lanes = q_cols + kv_cols
    smalls = jnp.concatenate([b.reshape(-1) for b in (query_bias, key_bias, value_bias)])
    extra = jnp.stack(
        [jnp.pad(row, (0, lanes - row.shape[0])) for row in (attn_gain, mlp_gain, smalls)]
    )
    extra = jnp.pad(extra, ((0, 13), (0, 0)))
    qkv = links.gather_fsdp(
        jnp.concatenate(
            [jnp.concatenate([query_weight, key_weight, value_weight], axis=1), extra], axis=0
        )
    )
    height = shard + 16
    rows = jnp.stack(
        [p[shard : shard + 3] for p in (qkv[0], qkv[2][:height], qkv[1], qkv[2][height:])]
    )
    rows = [
        lax.dynamic_index_in_dim(rows, jnp.bitwise_xor(fsdp, j), 0, keepdims=False) for j in range(4)
    ]
    attn_gamma = jnp.concatenate([r[0, :shard] for r in rows])[None].astype(jnp.float32)
    mlp_gamma = jnp.concatenate([r[1, :shard] for r in rows])[None].astype(jnp.float32)
    bias = jnp.concatenate(
        [r[2, : smalls.shape[0]].reshape(-1, head_dim // fsdps) for r in rows], axis=1
    ).reshape(1, lanes).astype(jnp.float32)

    o_wide = jnp.concatenate(links.gather_tp(output_weight), axis=0)
    o_parts = links.gather_fsdp(o_wide)

    cosine, sine = rope_tables(positions.reshape(tokens), head_dim)
    normed_one, query_blocks, kv_own = project(
        meta, inputs, attn_gamma, bias, qkv, cosine, sine, (local_heads, kv_heads, head_dim, tps)
    )
    if ctxs == 2:
        kv_before = lax.ppermute(kv_own, "ctx", [(0, 1)])
    else:
        kv_before = lax.all_gather(
            kv_own.reshape(seq_count, block_len, kv_cols), "ctx", axis=1, tiled=True
        ).reshape(seq_count * block_len * ctxs, kv_cols)

    def swap(block_of):
        return [block_of(tp)] + [
            links.hop_tp(block_of((tp + hop) % tps), hop) for hop in range(1, tps)
        ]

    queries = jnp.stack(swap(lambda d: lax.dynamic_index_in_dim(query_blocks, d, 0, keepdims=False)))
    order = jnp.tile(jnp.arange(own, dtype=jnp.int32), depth // head_dim // kv_heads)[None]
    sizes = (seq_count, kv_heads, head_dim, tps)
    mixed, lse = attend(meta, queries, kv_before, kv_own, order, key_block, sizes)
    hidden, normed_two = merge(meta, mixed, inputs, o_parts, mlp_gamma, tps)

    two_blocks = links.gather_tp(normed_two)
    acts, gate_grads, up_grads, two_parts, mixed_parts = [], [], [], [], []
    cots = [block_rows(cotangent, hop) for hop in range(tps)]
    for hop in range(tps):
        act_grad = inner_cols(cots[hop], down_full)
        gate = dot(two_blocks[hop], gate_full)
        up_part = dot(two_blocks[hop], up_full)
        sigma = jax.nn.sigmoid(gate)
        act = (gate * sigma * up_part).astype(LOW)
        gate_grad = (act_grad * up_part * (sigma * (1.0 + gate * (1.0 - sigma)))).astype(LOW)
        up_grad = (act_grad * (gate * sigma)).astype(LOW)
        two_parts.append((inner_cols(gate_grad, gate_full) + inner_cols(up_grad, up_full)).astype(LOW))
        mixed_parts.append(dot(act, down_full).astype(LOW))
        acts.append(act)
        gate_grads.append(gate_grad)
        up_grads.append(up_grad)
    two_own, two_got = links.scatter_tp(two_parts)

    act_all, cot_all, two_all, gate_all, up_all = (
        jnp.concatenate(item, axis=0) for item in (acts, cots, two_blocks, gate_grads, up_grads)
    )
    down_weight_grad = links.reduce_weight(inner_rows(act_all, cot_all), 1)
    gate_weight_grad = links.reduce_weight(inner_rows(two_all, gate_all), 0)
    up_weight_grad = links.reduce_weight(inner_rows(two_all, up_all), 0)

    def spread(block):
        blocks = links.gather_tp(lax.optimization_barrier(block.astype(LOW)))
        full = jnp.zeros((seq_count, block_len, width), LOW)
        for hop, item in enumerate(blocks):
            for s in seqs:
                full = lax.dynamic_update_slice(
                    full, item[None, s * own : (s + 1) * own], (s, place(s, links.at(hop)) * own, 0)
                )
        return full

    hidden_grad, branch_grad, attended_grad, mlp_term = turn(
        meta, two_own, two_got, hidden, cotangent, o_parts, mlp_gamma, depth, tps
    )
    q_grad, kv_grad_before, kv_grad_own = attend_back(
        meta, queries, kv_before, kv_own, order, mixed, attended_grad, lse, cosine, sine, key_block, sizes
    )
    kv_shape = (2, kv_heads, seq_count, block_len, head_dim)
    if ctxs == 2:
        kv_part = add_low(
            kv_grad_own, lax.ppermute(kv_grad_before, "ctx", [(1, 0)])
        ).reshape(kv_shape)
    else:
        wide_grad = kv_grad_before.reshape(2, kv_heads, seq_count, ctxs * block_len, head_dim)
        wide_grad = lax.dynamic_update_slice_in_dim(
            wide_grad, kv_grad_own.reshape(kv_shape), ctx * block_len, 3
        )
        kv_part = lax.psum_scatter(wide_grad, "ctx", scatter_dimension=3, tiled=True)

    def kv_rows(hop):
        return jnp.concatenate(
            [
                lax.dynamic_slice_in_dim(kv_part[:, :, s : s + 1], place(s, links.at(hop)) * own, own, 3)
                for s in seqs
            ],
            axis=2,
        )

    kv_mine, kv_got = links.scatter_tp([kv_rows(hop) for hop in range(tps)])
    input_low, kv_grad, attn_term = finish(
        meta, q_grad, kv_mine, kv_got, cosine, sine, q_full, qkv, inputs, hidden_grad, attn_gamma, tps
    )
    input_grad = spread(input_low).astype(jnp.float32)

    kv_each = kv_cols // tps
    attn_sum = jnp.sum(attn_term, axis=0)
    mlp_sum = jnp.sum(mlp_term, axis=0)

    def share(device):
        grads = jnp.concatenate(
            [
                lax.dynamic_slice_in_dim(q_grad, device * q_cols, q_cols, 1),
                lax.dynamic_slice_in_dim(kv_grad, device * kv_each, kv_each, 1),
            ],
            axis=1,
        )
        gains = jnp.concatenate(
            [lax.dynamic_slice_in_dim(item, device * shard, shard, 1) for item in (attn_sum, mlp_sum)], axis=0
        )
        gains = jnp.pad(gains, ((0, 14), (0, q_cols + kv_each - shard))).astype(LOW)
        return jnp.concatenate([grads, gains], axis=0)

    shares = swap(share)
    own_tokens = seq_count * own
    grads_all = jnp.concatenate([item[:own_tokens] for item in shares], axis=0)
    one_all = jnp.concatenate(
        [block_rows(normed_one.reshape(seq_count, block_len, width), hop) for hop in range(tps)], axis=0
    )
    gain_rows = sum(item[own_tokens : own_tokens + 2].astype(jnp.float32) for item in shares)
    bias_row = jnp.sum(grads_all.astype(jnp.float32), axis=0, keepdims=True)
    below = jnp.pad(jnp.concatenate([gain_rows, bias_row], axis=0), ((0, 13), (0, 0))).astype(LOW)
    term = inner_rows(one_all, grads_all).astype(LOW)
    term = jnp.concatenate(
        [item for j in range(fsdps) for item in (term[j * shard : (j + 1) * shard], below)], axis=0
    )
    total = links.sum_ctx(links.scatter_fsdp(term, 0))
    query_weight_grad = total[:shard, :q_cols]
    below = total[shard:]
    part = head_dim // fsdps
    query_bias_grad = lax.dynamic_slice_in_dim(
        below[2, :q_cols].reshape(local_heads, head_dim), fsdp * part, part, 1
    )
    kv_low = jnp.concatenate(
        [total[:shard, q_cols:], below[:, :q_cols].reshape(-1, kv_each), below[:, q_cols:]], axis=0
    ).astype(LOW)
    kv_low = lax.optimization_barrier(kv_low)
    all_low = jnp.stack(links.gather_tp(kv_low))
    by_device = [
        lax.dynamic_index_in_dim(all_low, links.at(j), 0, keepdims=False) for j in range(tps)
    ]
    kv_weight = jnp.concatenate([item[:shard] for item in by_device], axis=1).astype(jnp.float32)
    mine = lax.dynamic_index_in_dim(all_low, (tp - fsdp + tps) % tps, 0, keepdims=False)
    gains = mine[shard : shard + 16 * (q_cols // kv_each)].reshape(16, q_cols).astype(jnp.float32)
    kv_bias = jnp.stack([item[-14] for item in by_device]).reshape(2, kv_heads, head_dim)
    kv_bias = lax.dynamic_slice_in_dim(kv_bias, fsdp * part, part, 2).astype(jnp.float32)
    half = kv_cols // 2

    output_part = links.scatter_fsdp(inner_rows(mixed, branch_grad).astype(LOW), 1)
    output_mine, output_got = links.scatter_tp(
        [
            lax.dynamic_slice_in_dim(output_part, links.at(hop) * q_cols, q_cols, 0)
            for hop in range(tps)
        ]
    )
    output_weight_grad = links.sum_ctx(add_low(output_mine, output_got))

    mixed_mine, mixed_got = links.scatter_tp(mixed_parts)
    outputs = spread(hidden + mixed_mine.astype(jnp.float32) + mixed_got.astype(jnp.float32))

    return (
        outputs,
        input_grad,
        gains[0],
        query_weight_grad,
        query_bias_grad,
        kv_weight[:, :half],
        kv_bias[0],
        kv_weight[:, half:],
        kv_bias[1],
        output_weight_grad,
        gains[1],
        gate_weight_grad,
        up_weight_grad,
        down_weight_grad,
    )


def solution(mesh):
    in_specs = (
        P("fsdp", "ctx", None),
        P("fsdp", "ctx", None),
        P("fsdp", "ctx"),
        P("fsdp"),
        P("fsdp", "tp"),
        P("tp", "fsdp"),
        P("fsdp", None),
        P(None, "fsdp"),
        P("fsdp", None),
        P(None, "fsdp"),
        P("tp", "fsdp"),
        P("fsdp"),
        P("fsdp", "tp"),
        P("fsdp", "tp"),
        P("tp", "fsdp"),
    )
    out_specs = (
        P("fsdp", "ctx", None),
        P("fsdp", "ctx", None),
        P("fsdp"),
        P("fsdp", "tp"),
        P("tp", "fsdp"),
        P("fsdp", None),
        P(None, "fsdp"),
        P("fsdp", None),
        P(None, "fsdp"),
        P("tp", "fsdp"),
        P("fsdp"),
        P("fsdp", "tp"),
        P("fsdp", "tp"),
        P("tp", "fsdp"),
    )
    return jax.shard_map(local, mesh=mesh, in_specs=in_specs, out_specs=out_specs, check_vma=False)
```

```python
import functools
import math

import jax
import jax.numpy as jnp
from jax import lax
from jax.experimental import pallas as pl
from jax.experimental.pallas import tpu as pltpu
from jax.sharding import PartitionSpec as P

EPS = 1e-06
THETA = 1000000.0
LOG2E = 1.0 / math.log(2.0)
LOW = jnp.bfloat16
MASKED = -1e30
MIB = 1024 * 1024


def rope_tables(position, width):
    half = width // 2
    freqs = jnp.exp(jnp.arange(half, dtype=jnp.float32) * (-2.0 * math.log(THETA) / width))
    angle = position.astype(jnp.float32)[..., None] * freqs
    cosine, sine = jnp.cos(angle), jnp.sin(angle)
    return (
        jnp.concatenate([cosine, cosine], axis=-1),
        jnp.concatenate([-sine, sine], axis=-1),
    )


def dot(left, right):
    return jnp.dot(left, right, preferred_element_type=jnp.float32)


def inner_rows(left, right):
    return lax.dot_general(
        left, right, (((0,), (0,)), ((), ())), preferred_element_type=jnp.float32
    )


def inner_cols(left, right):
    return lax.dot_general(
        left, right, (((1,), (1,)), ((), ())), preferred_element_type=jnp.float32
    )


def add_low(left, right):
    return (left.astype(jnp.float32) + right.astype(jnp.float32)).astype(LOW)


def after(value, token):
    return lax.optimization_barrier((value, token))[0]


def root_of(values):
    return lax.rsqrt(jnp.mean(values * values, axis=-1, keepdims=True) + EPS)


FSDP, TP, CTX, BEFORE, PLACE = 0, 1, 2, 3, 4


def shard_at(meta, flip, size):
    return pl.multiple_of(jnp.bitwise_xor(meta[FSDP], flip) * size, size)


def tp_at(meta, hop, tps, size):
    return pl.multiple_of(lax.rem(meta[TP] + tps - hop, tps) * size, size)


def call(kernel, grid, in_specs, out_specs, out_shape, scratch=(), cost=None, name=None, vmem=48):
    return pl.pallas_call(
        kernel,
        grid_spec=pltpu.PrefetchScalarGridSpec(
            num_scalar_prefetch=1,
            grid=grid,
            in_specs=in_specs,
            out_specs=out_specs,
            scratch_shapes=list(scratch),
        ),
        out_shape=out_shape,
        compiler_params=pltpu.CompilerParams(vmem_limit_bytes=vmem * MIB),
        cost_estimate=cost,
        name=name,
    )


def whole(array):
    return pl.BlockSpec(array.shape, lambda *_: (0,) * array.ndim)


def shape(dims, kind):
    return jax.ShapeDtypeStruct(dims, kind)


def project_kernel(
    local_heads, kv_heads, head_dim, meta, x_ref, gain_ref, bias_ref, *refs
):
    weights, (cos_ref, sin_ref, n_ref, q_ref, kv_ref) = refs[:4], refs[4:]
    rows = x_ref.shape[1]
    size = n_ref.shape[1] // 4
    values = x_ref[...].reshape(rows, -1).astype(jnp.float32)
    n_ref[...] = (values * root_of(values) * gain_ref[...]).astype(LOW)
    lin = bias_ref[...]
    for flip, weight in enumerate(weights):
        lin = lin + dot(n_ref[:, pl.ds(shard_at(meta, flip, size), size)], weight[:size, :])
    cosine, sine = cos_ref[...], sin_ref[...]
    for head in range(local_heads + 2 * kv_heads):
        part = lin[:, head * head_dim : (head + 1) * head_dim]
        if head < local_heads + kv_heads:
            part = part * cosine + pltpu.roll(part, head_dim // 2, 1) * sine
        if head < local_heads:
            q_ref[0, :, head * head_dim : (head + 1) * head_dim] = part.astype(LOW)
        else:
            at = (head - local_heads) * head_dim
            kv_ref[:, at : at + head_dim] = part.astype(LOW)


def project(meta, inputs, gain, bias, weights, cosine, sine, sizes):
    seq_count, block_len, width = inputs.shape
    local_heads, kv_heads, head_dim, tps = sizes
    own = block_len // tps
    q_cols, kv_cols = local_heads * head_dim, 2 * kv_heads * head_dim

    def row(i, m):
        return (i, 0)

    def device(i, m):
        seq, place = i // tps, i % tps
        return jnp.where(seq % 2 == 0, place, tps - 1 - place), seq, 0

    tokens = seq_count * block_len
    return call(
        functools.partial(project_kernel, local_heads, kv_heads, head_dim),
        (seq_count * tps,),
        [
            pl.BlockSpec((1, own, width), lambda i, m: (i // tps, i % tps, 0)),
            whole(gain), whole(bias), *(whole(w) for w in weights),
            pl.BlockSpec((own, head_dim), row), pl.BlockSpec((own, head_dim), row),
        ],
        [
            pl.BlockSpec((own, width), row),
            pl.BlockSpec((1, own, q_cols), device),
            pl.BlockSpec((own, kv_cols), row),
        ],
        [
            shape((tokens, width), LOW),
            shape((tps, seq_count * own, q_cols), LOW),
            shape((tokens, kv_cols), LOW),
        ],
        cost=pl.CostEstimate(
            flops=2 * tokens * width * (q_cols + kv_cols), bytes_accessed=8 * tokens * width, transcendentals=0
        ),
        name="project",
    )(meta, inputs, gain, bias, *weights, cosine, sine)


def fwd_kernel(
    heads, block, parts, meta, *refs
):
    q_refs, (kb_ref, vb_ref, k_ref, v_ref, order_ref, o_ref, lse_ref, qg_ref, acc_ref, m_ref, l_ref) = (
        refs[:parts], refs[parts:]
    )
    own, cols = q_refs[0].shape[1:]
    head_dim = acc_ref.shape[0]
    scale = LOG2E / math.sqrt(head_dim)
    each = cols // head_dim
    for head in range(heads):
        qg_ref[head * own : (head + 1) * own, :] = q_refs[head // each][
            0, :, (head % each) * head_dim : (head % each + 1) * head_dim
        ]
    acc_ref[...] = jnp.zeros_like(acc_ref)
    m_ref[...] = jnp.full_like(m_ref, MASKED)
    l_ref[...] = jnp.zeros_like(l_ref)
    first = meta[PLACE + pl.program_id(0)] * own
    last = first // block

    def step(key_ref, value_ref, index, masked):
        start = pl.multiple_of(index * block, block)
        keys = key_ref[pl.ds(start, block), :]
        values = value_ref[pl.ds(start, block), :]
        logits = inner_cols(keys, qg_ref[...]) * scale
        if masked:
            key_order = (start - first) + lax.broadcasted_iota(jnp.int32, logits.shape, 0)
            logits = jnp.where(key_order <= order_ref[...], logits, MASKED)
        before = m_ref[...]
        peak = jnp.maximum(before, jnp.max(logits, axis=0, keepdims=True))
        weights = jnp.exp2(logits - peak)
        fade = jnp.exp2(before - peak)
        m_ref[...] = peak
        l_ref[...] = l_ref[...] * fade + jnp.sum(weights, axis=0, keepdims=True)
        acc_ref[...] = acc_ref[...] * fade + inner_rows(values, weights.astype(LOW))

    def early(index, carry):
        step(kb_ref, vb_ref, index, False)
        return carry

    def late(index, carry):
        step(k_ref, v_ref, index, False)
        return carry

    lax.fori_loop(0, meta[BEFORE], early, 0)
    lax.fori_loop(0, last, late, 0)
    step(k_ref, v_ref, last, True)
    total = l_ref[...]
    lse_ref[...] = (m_ref[...] + jnp.log2(total)).reshape(lse_ref.shape)
    mixed = jnp.transpose(acc_ref[...] / total)
    for head in range(heads):
        o_ref[:, head * head_dim : (head + 1) * head_dim] = mixed[
            head * own : (head + 1) * own, :
        ].astype(LOW)


def bwd_kernel(heads, block, parts, seq, meta, *refs):
    q_refs, (
        kb_ref, vb_ref, k_ref, v_ref, order_ref, o_ref, g_ref, lse_ref, cos_ref, sin_ref,
        dq_ref, db_ref, dd_ref, qg_ref, gg_ref, acc_ref,
    ) = refs[:parts], refs[parts:]
    own, cols = q_refs[0].shape[1:]
    head_dim = acc_ref.shape[1]
    scale = 1.0 / math.sqrt(head_dim)
    each = cols // head_dim
    for head in range(heads):
        rows = slice(head * own, (head + 1) * own)
        at = slice(head * head_dim, (head + 1) * head_dim)
        qg_ref[rows, :] = q_refs[head // each][
            0, :, (head % each) * head_dim : (head % each + 1) * head_dim
        ]
        gg_ref[rows, :] = g_ref[:, at]
        acc_ref[rows, :] = g_ref[:, at].astype(jnp.float32) * o_ref[:, at].astype(jnp.float32)
    center = jnp.sum(jnp.transpose(acc_ref[...]), axis=0, keepdims=True)
    acc_ref[...] = jnp.zeros_like(acc_ref)
    lse = lse_ref[...].reshape(order_ref.shape)
    first = meta[PLACE + seq] * own
    last = first // block

    def step(key_ref, value_ref, out_ref, index, masked):
        start = pl.multiple_of(index * block, block)
        keys = key_ref[pl.ds(start, block), :]
        values = value_ref[pl.ds(start, block), :]
        logits = inner_cols(keys, qg_ref[...]) * (scale * LOG2E)
        if masked:
            key_order = (start - first) + lax.broadcasted_iota(jnp.int32, logits.shape, 0)
            logits = jnp.where(key_order <= order_ref[...], logits, MASKED)
        probs = jnp.exp2(logits - lse)
        out_ref[1, 0, pl.ds(start, block), :] = dot(probs.astype(LOW), gg_ref[...]).astype(LOW)
        prob_grad = inner_cols(values, gg_ref[...])
        logit_grad = (probs * (prob_grad - center)).astype(LOW)
        out_ref[0, 0, pl.ds(start, block), :] = (dot(logit_grad, qg_ref[...]) * scale).astype(LOW)
        acc_ref[...] += inner_rows(logit_grad, keys)

    def early(index, carry):
        step(kb_ref, vb_ref, db_ref, index, False)
        return carry

    def late(index, carry):
        step(k_ref, v_ref, dd_ref, index, False)
        return carry

    def clear(ref):
        def body(index, carry):
            start = pl.multiple_of(index * block, block)
            ref[:, :, pl.ds(start, block), :] = jnp.zeros((2, 1, block, head_dim), LOW)
            return carry

        return body

    lax.fori_loop(0, meta[BEFORE], early, 0)
    lax.fori_loop(meta[BEFORE], kb_ref.shape[0] // block, clear(db_ref), 0)
    lax.fori_loop(0, last, late, 0)
    step(k_ref, v_ref, dd_ref, last, True)
    lax.fori_loop(last + 1, k_ref.shape[0] // block, clear(dd_ref), 0)
    for head in range(heads):
        grad = acc_ref[head * own : (head + 1) * own, :] * scale
        grad = grad * cos_ref[...] - pltpu.roll(grad, head_dim // 2, 1) * sin_ref[...]
        dq_ref[:, head * head_dim : (head + 1) * head_dim] = grad.astype(LOW)


def attention_specs(queries, kv_before, kv_own, sizes, seq=None):
    seq_count, kv_heads, head_dim, tps = sizes
    rows = queries.shape[1] // seq_count
    parts = tps // kv_heads
    heads = queries.shape[2] * parts // head_dim
    before, block_len = kv_before.shape[0] // seq_count, kv_own.shape[0] // seq_count

    def spec(dims, index):
        if seq is None:
            return pl.BlockSpec(dims, index)
        return pl.BlockSpec(dims, lambda g, m: index(seq, g, m))

    def piece(part):
        return spec(
            (1, rows, queries.shape[2]),
            lambda s, g, m: (lax.rem(m[TP] + tps - (g * parts + part), tps), s, 0),
        )

    specs = [piece(part) for part in range(parts)] + [
        spec((before, head_dim), lambda s, g, m: (s, g)),
        spec((before, head_dim), lambda s, g, m: (s, kv_heads + g)),
        spec((block_len, head_dim), lambda s, g, m: (s, g)),
        spec((block_len, head_dim), lambda s, g, m: (s, kv_heads + g)),
        spec((1, heads * rows), lambda s, g, m: (0, 0)),
    ]
    return specs, rows, parts, heads, before, block_len


def attend(meta, queries, kv_before, kv_own, order, block, sizes):
    seq_count, kv_heads, head_dim, tps = sizes
    specs, rows, parts, heads, before, block_len = attention_specs(queries, kv_before, kv_own, sizes)
    width, wide = kv_heads * heads * head_dim, heads * rows
    work = seq_count * rows * width * (before + block_len)
    return call(
        functools.partial(fwd_kernel, heads, block, parts),
        (seq_count, kv_heads),
        specs,
        [
            pl.BlockSpec((rows, heads * head_dim), lambda s, g, m: (s, g)),
            pl.BlockSpec((1, 1, 1, wide), lambda s, g, m: (s, g, 0, 0)),
        ],
        [shape((seq_count * rows, width), LOW), shape((seq_count, kv_heads, 1, wide), jnp.float32)],
        [
            pltpu.VMEM((wide, head_dim), LOW),
            pltpu.VMEM((head_dim, wide), jnp.float32),
            pltpu.VMEM((1, wide), jnp.float32),
            pltpu.VMEM((1, wide), jnp.float32),
        ],
        cost=pl.CostEstimate(flops=8 * work, bytes_accessed=1 << 22, transcendentals=0),
        name="attend",
    )(meta, *([queries] * parts), kv_before, kv_before, kv_own, kv_own, order)


def attend_back(
    meta, seq, queries, kv_before, kv_own, order, mixed, grads, lse, cosine, sine, block, sizes
):
    seq_count, kv_heads, head_dim, tps = sizes
    specs, rows, parts, heads, before, block_len = attention_specs(
        queries, kv_before, kv_own, sizes, seq
    )
    width, wide = kv_heads * heads * head_dim, heads * rows
    work = rows * width * (before + block_len)
    wide_spec = pl.BlockSpec((rows, heads * head_dim), lambda g, m: (seq, g))
    table_spec = pl.BlockSpec((rows, head_dim), lambda g, m: (seq * tps + m[PLACE + seq], 0))
    return call(
        functools.partial(bwd_kernel, heads, block, parts, seq),
        (kv_heads,),
        specs
        + [
            wide_spec,
            wide_spec,
            pl.BlockSpec((1, 1, 1, wide), lambda g, m: (seq, g, 0, 0)),
            table_spec,
            table_spec,
        ],
        [
            pl.BlockSpec((rows, heads * head_dim), lambda g, m: (0, g)),
            pl.BlockSpec((2, 1, before, head_dim), lambda g, m: (0, g, 0, 0)),
            pl.BlockSpec((2, 1, block_len, head_dim), lambda g, m: (0, g, 0, 0)),
        ],
        [
            shape((rows, width), LOW),
            shape((2, kv_heads, before, head_dim), LOW),
            shape((2, kv_heads, block_len, head_dim), LOW),
        ],
        [
            pltpu.VMEM((wide, head_dim), LOW),
            pltpu.VMEM((wide, head_dim), LOW),
            pltpu.VMEM((wide, head_dim), jnp.float32),
        ],
        cost=pl.CostEstimate(flops=16 * work, bytes_accessed=1 << 22, transcendentals=0),
        name="attend_back",
    )(
        meta, *([queries] * parts), kv_before, kv_before, kv_own, kv_own, order,
        mixed, grads, lse, cosine, sine,
    )


def merge_kernel(tps, meta, o_ref, x_ref, *refs):
    weights, (gain_ref, h_ref, n_ref) = refs[:4], refs[4:]
    rows, width = h_ref.shape
    size, depth = width // 4, o_ref.shape[1]
    turned = o_ref[...]
    for flip, weight in enumerate(weights):
        at = pl.ds(shard_at(meta, flip, size), size)
        h_ref[:, at] = x_ref[0, :, at].astype(jnp.float32) + dot(turned, weight[...])
    hidden = h_ref[...]
    n_ref[...] = (hidden * root_of(hidden) * gain_ref[...]).astype(LOW)


def merge(meta, mixed, inputs, weights, gain, tps):
    seq_count, block_len, width = inputs.shape
    own = block_len // tps
    depth = mixed.shape[1]
    row = pl.BlockSpec((own, width), lambda s, m: (s, 0))
    return call(
        functools.partial(merge_kernel, tps),
        (seq_count,),
        [
            pl.BlockSpec((own, depth), lambda s, m: (s, 0)),
            pl.BlockSpec((1, own, width), lambda s, m: (s, m[PLACE + s], 0)),
            *(whole(w) for w in weights),
            whole(gain),
        ],
        [row, row],
        [shape((seq_count * own, width), jnp.float32), shape((seq_count * own, width), LOW)],
        cost=pl.CostEstimate(
            flops=2 * seq_count * own * depth * width, bytes_accessed=1 << 23, transcendentals=0
        ),
        name="merge",
    )(meta, mixed, inputs, *weights, gain)


def turn_kernel(
    tps, meta, a_ref, b_ref, h_ref, c_ref, *refs,
):
    weights, (gain_ref, hg_ref, bg_ref, ag_ref, term_ref, turned_ref) = refs[:4], refs[4:]
    rows, width = h_ref.shape
    size, depth = width // 4, ag_ref.shape[1]
    two_grad = a_ref[...].astype(jnp.float32) + b_ref[...].astype(jnp.float32)
    hidden = h_ref[...]
    root = root_of(hidden)
    term_ref[...] = jnp.sum(two_grad * hidden * root, axis=0, keepdims=True).reshape(term_ref.shape)
    scaled = gain_ref[...] * two_grad
    grad = (
        c_ref[...].reshape(rows, width).astype(jnp.float32)
        + root * scaled
        - hidden * root**3 * jnp.mean(scaled * hidden, axis=-1, keepdims=True)
    )
    hg_ref[...] = grad
    bg_ref[...] = grad.astype(LOW)
    turned_ref[...] = jnp.zeros_like(turned_ref)
    for flip, weight in enumerate(weights):
        turned_ref[...] += inner_cols(bg_ref[:, pl.ds(shard_at(meta, flip, size), size)], weight[...])
    ag_ref[...] = turned_ref[...].astype(LOW)


def turn(meta, two_own, two_got, hidden, cotangent, weights, gain, depth, tps):
    seq_count, block_len, width = cotangent.shape
    own = block_len // tps
    row = pl.BlockSpec((own, width), lambda s, m: (s, 0))
    tokens = seq_count * own
    return call(
        functools.partial(turn_kernel, tps),
        (seq_count,),
        [
            row, row, row,
            pl.BlockSpec((1, own, width), lambda s, m: (s, m[PLACE + s], 0)),
            *(whole(w) for w in weights),
            whole(gain),
        ],
        [
            row, row,
            pl.BlockSpec((own, depth), lambda s, m: (s, 0)),
            pl.BlockSpec((1, 1, width), lambda s, m: (s, 0, 0)),
        ],
        [
            shape((tokens, width), jnp.float32),
            shape((tokens, width), LOW),
            shape((tokens, depth), LOW),
            shape((seq_count, 1, width), jnp.float32),
        ],
        [pltpu.VMEM((own, depth), jnp.float32)],
        cost=pl.CostEstimate(flops=2 * tokens * depth * width, bytes_accessed=1 << 23, transcendentals=0),
        name="turn",
    )(meta, two_own, two_got, hidden, cotangent, *weights, gain)


def finish_kernel(
    kv_heads, head_dim, meta, g_ref, a_ref, b_ref, cos_ref, sin_ref, q_ref, *refs
):
    weights = refs[:4]
    x_ref, hg_ref, gain_ref, out_ref, kv_ref, term_ref, one_ref = refs[4:]
    rows, width = hg_ref.shape
    size = width // 4
    cosine, sine = cos_ref[...], sin_ref[...]
    for kind in range(2):
        for head in range(kv_heads):
            grad = (
                a_ref[kind, head, 0].astype(jnp.float32) + b_ref[kind, head, 0].astype(jnp.float32)
            )
            if kind == 0:
                grad = grad * cosine - pltpu.roll(grad, head_dim // 2, 1) * sine
            at = (kind * kv_heads + head) * head_dim
            kv_ref[:, at : at + head_dim] = grad.astype(LOW)
    one_ref[...] = inner_cols(g_ref[...], q_ref[...])
    skip = weights[0].shape[1] - kv_ref.shape[1]
    for flip, weight in enumerate(weights):
        one_ref[:, pl.ds(shard_at(meta, flip, size), size)] += inner_cols(
            kv_ref[...], weight[:size, skip:]
        )
    one = one_ref[...]
    values = x_ref[...].reshape(rows, width).astype(jnp.float32)
    root = root_of(values)
    term_ref[...] = jnp.sum(one * values * root, axis=0, keepdims=True).reshape(term_ref.shape)
    scaled = gain_ref[...] * one
    out_ref[...] = (
        hg_ref[...]
        + root * scaled
        - values * root**3 * jnp.mean(scaled * values, axis=-1, keepdims=True)
    ).astype(LOW)


def finish(meta, q_grad, kv_mine, kv_got, cosine, sine, q_full, weights, inputs, hidden_grad, gain, tps):
    seq_count, block_len, width = inputs.shape
    own = block_len // tps
    kv_heads, head_dim = kv_mine.shape[1], kv_mine.shape[4]
    kv_cols = 2 * kv_heads * head_dim
    tokens = seq_count * own
    row = pl.BlockSpec((own, width), lambda s, m: (s, 0))
    kv_spec = pl.BlockSpec((2, kv_heads, 1, own, head_dim), lambda s, m: (0, 0, s, 0, 0))
    table_spec = pl.BlockSpec((own, head_dim), lambda s, m: (s * tps + m[PLACE + s], 0))
    return call(
        functools.partial(finish_kernel, kv_heads, head_dim),
        (seq_count,),
        [
            pl.BlockSpec((own, q_grad.shape[1]), lambda s, m: (s, 0)),
            kv_spec, kv_spec, table_spec, table_spec,
            whole(q_full),
            *(whole(w) for w in weights),
            pl.BlockSpec((1, own, width), lambda s, m: (s, m[PLACE + s], 0)),
            row,
            whole(gain),
        ],
        [
            row,
            pl.BlockSpec((own, kv_cols), lambda s, m: (s, 0)),
            pl.BlockSpec((1, 1, width), lambda s, m: (s, 0, 0)),
        ],
        [
            shape((tokens, width), LOW),
            shape((tokens, kv_cols), LOW),
            shape((seq_count, 1, width), jnp.float32),
        ],
        [pltpu.VMEM((own, width), jnp.float32)],
        cost=pl.CostEstimate(
            flops=2 * tokens * (q_grad.shape[1] + kv_cols) * width, bytes_accessed=1 << 23, transcendentals=0
        ),
        name="finish",
    )(meta, q_grad, kv_mine, kv_got, cosine, sine, q_full, *weights, inputs, hidden_grad, gain)


def feed_kernel(first, hidden, *refs):
    n_ref, c_ref, wg_ref, wu_ref, wd_ref = refs[1:6]
    act_ref, gg_ref, ug_ref, two_ref, mix_ref, two_acc, mix_acc = refs[6 if first else 9 :]
    step, tile = pl.program_id(0), wg_ref.shape[0]
    steps = -(-hidden // tile)

    def body(count):
        gate = inner_cols(n_ref[...], wg_ref[:count, :])
        up_part = inner_cols(n_ref[...], wu_ref[:count, :])
        act_grad = inner_cols(c_ref[...], wd_ref[:count, :])
        sigma = jax.nn.sigmoid(gate)
        silu = gate * sigma
        act = (silu * up_part).astype(LOW)
        gate_grad = (act_grad * up_part * (sigma * (1.0 + gate * (1.0 - sigma)))).astype(LOW)
        up_grad = (act_grad * silu).astype(LOW)
        act_ref[:, :count], gg_ref[:, :count], ug_ref[:, :count] = act, gate_grad, up_grad
        return (
            dot(gate_grad, wg_ref[:count, :]) + dot(up_grad, wu_ref[:count, :]),
            dot(act, wd_ref[:count, :]),
        )

    @pl.when(step == 0)
    def _():
        two_acc[...], mix_acc[...] = body(tile)

    @pl.when(jnp.logical_and(step > 0, step < steps - 1))
    def _():
        two, mix = body(tile)
        two_acc[...] += two
        mix_acc[...] += mix

    @pl.when(step == steps - 1)
    def _():
        two, mix = body(hidden - (steps - 1) * tile)
        two_ref[...] = (two_acc[...] + two).astype(LOW)
        mix_ref[...] = (mix_acc[...] + mix).astype(LOW)


def feed(meta, normed, cots, gate, up, down, hop, tps, kept):
    rows, width = normed.shape
    hidden = down.shape[0]
    tile = 768
    assert hidden > tile
    weight = pl.BlockSpec((tile, width), lambda j, m: (j, 0))
    column = pl.BlockSpec((rows, tile), lambda j, m: (hop, j))
    fixed = pl.BlockSpec((rows, width), lambda j, m: (0, 0))
    first = hop == 0
    wide = shape((tps * rows, hidden), LOW)
    *hiddens, two_part, mixed_part = pl.pallas_call(
        functools.partial(feed_kernel, first, hidden),
        grid_spec=pltpu.PrefetchScalarGridSpec(
            num_scalar_prefetch=1,
            grid=(-(-hidden // tile),),
            in_specs=[fixed, pl.BlockSpec((rows, width), lambda j, m: (hop, 0)), weight, weight, weight]
            + ([] if first else [pl.BlockSpec(memory_space=pl.ANY)] * 3),
            out_specs=[column, column, column, fixed, fixed],
            scratch_shapes=[pltpu.VMEM((rows, width), jnp.float32)] * 2,
        ),
        out_shape=[wide, wide, wide, shape((rows, width), LOW), shape((rows, width), LOW)],
        input_output_aliases={} if first else {6: 0, 7: 1, 8: 2},
        compiler_params=pltpu.CompilerParams(vmem_limit_bytes=56 * MIB),
        cost_estimate=pl.CostEstimate(
            flops=12 * rows * width * hidden, bytes_accessed=6 * width * hidden, transcendentals=rows * hidden
        ),
        name="feed",
    )(meta, normed, cots, gate, up, down, *(() if first else kept))
    return hiddens, two_part, mixed_part


def assemble_kernel(tiles, meta, own_ref, near_ref, far_ref, o_own_ref, o_near_ref, o_far_ref, out_ref):
    size = own_ref.shape[1]
    is_near = (pl.program_id(0) // tiles) == meta[CTX]
    out_ref[:, pl.ds(shard_at(meta, 0, size), size)] = own_ref[...]
    out_ref[:, pl.ds(shard_at(meta, 1, size), size)] = o_own_ref[...]

    @pl.when(is_near)
    def _():
        out_ref[:, pl.ds(shard_at(meta, 2, size), size)] = near_ref[...]
        out_ref[:, pl.ds(shard_at(meta, 3, size), size)] = o_near_ref[...]

    @pl.when(jnp.logical_not(is_near))
    def _():
        out_ref[:, pl.ds(shard_at(meta, 2, size), size)] = far_ref[...]
        out_ref[:, pl.ds(shard_at(meta, 3, size), size)] = o_far_ref[...]


def assemble(meta, own, near, far, other, other_near, other_far):
    rows, size = own.shape
    tiles = 2 if rows % 64 == 0 else 1
    tile = rows // (2 * tiles)
    every = pl.BlockSpec((tile, size), lambda i, m: (i, 0))
    half = pl.BlockSpec((tile, size), lambda i, m: (i % tiles, 0))
    return call(
        functools.partial(assemble_kernel, tiles),
        (2 * tiles,),
        [every, half, half, every, half, half],
        pl.BlockSpec((tile, 4 * size), lambda i, m: (i, 0)),
        shape((rows, 4 * size), LOW),
        cost=pl.CostEstimate(flops=0, bytes_accessed=16 * rows * size, transcendentals=0),
        name="assemble",
    )(meta, own, near, far, other, other_near, other_far)


def lay_kernel(low_ref, high_ref, out_ref):
    both = jnp.concatenate([low_ref[...], high_ref[...]], axis=0)
    out_ref[...] = jnp.transpose(both.astype(jnp.float32))


def lay(low, high):
    rows, cols = low.shape
    return pl.pallas_call(
        lay_kernel,
        in_specs=[pl.BlockSpec(memory_space=pltpu.VMEM)] * 2,
        out_specs=pl.BlockSpec(memory_space=pltpu.VMEM),
        out_shape=shape((cols, 2 * rows), jnp.float32),
        compiler_params=pltpu.CompilerParams(vmem_limit_bytes=48 * MIB),
        cost_estimate=pl.CostEstimate(flops=0, bytes_accessed=12 * rows * cols, transcendentals=0),
        name="lay",
    )(low, high)


def spread_kernel(tps, meta, *refs):
    out_ref = refs[tps]
    seq_count = out_ref.shape[0]
    own = refs[0].shape[0] // seq_count
    for hop in range(tps):
        device = lax.rem(meta[TP] + tps - hop, tps)
        for s in range(seq_count):
            place = device if s % 2 == 0 else tps - 1 - device
            at = pl.ds(pl.multiple_of(place * own, own), own)
            out_ref[s, at, :] = refs[hop][s * own : (s + 1) * own, :].astype(out_ref.dtype)


def spread_out(meta, blocks, seq_count, kind):
    tps = len(blocks)
    rows, width = blocks[0].shape
    dims = (seq_count, rows // seq_count * tps, width)
    return call(
        functools.partial(spread_kernel, tps),
        (1,),
        [whole(item) for item in blocks],
        pl.BlockSpec(dims, lambda *_: (0, 0, 0)),
        shape(dims, kind),
        cost=pl.CostEstimate(flops=0, bytes_accessed=8 * rows * tps * width, transcendentals=0),
        name="spread",
    )(meta, *blocks)


class Links:
    def __init__(self):
        self.tp, self.ctx, self.fsdp = (lax.axis_index(a) for a in ("tp", "ctx", "fsdp"))
        self.tps, self.ctxs, self.fsdps = (lax.axis_size(a) for a in ("tp", "ctx", "fsdp"))
        self.core, self.x = self.fsdp % 2, self.fsdp // 2
        assert self.fsdps == 4

    def to_core(self, value):
        return lax.ppermute(value, "fsdp", [(0, 1), (1, 0), (2, 3), (3, 2)])

    def to_x(self, value):
        return lax.ppermute(value, "fsdp", [(0, 2), (2, 0), (1, 3), (3, 1)])

    def to_y(self, value):
        return lax.ppermute(value, "ctx", [(0, 1), (1, 0)])

    def hop_tp(self, value, hop=1):
        return lax.ppermute(value, "tp", [(i, (i + hop) % self.tps) for i in range(self.tps)])

    def gather_fsdp(self, shard):
        across = self.to_x(shard)
        return shard, across, self.to_core(jnp.concatenate([shard, across], axis=0))

    def gather_tp(self, block):
        blocks = [block]
        for _ in range(1, self.tps):
            blocks.append(self.hop_tp(blocks[-1]))
        return blocks

    def scatter_tp(self, blocks):
        total = blocks[1]
        for hop in range(1, self.tps):
            got = self.hop_tp(total)
            if hop < self.tps - 1:
                total = add_low(blocks[hop + 1], got)
        return blocks[0], got

    def at(self, hop):
        return (self.tp - hop + self.tps) % self.tps

    def scatter_fsdp(self, value, axis):
        size = value.shape[axis] // 4

        def pair(core):
            return jnp.concatenate(
                [
                    lax.dynamic_slice_in_dim(value, (2 * x + core) * size, size, axis)
                    for x in range(2)
                ],
                axis,
            )

        both = add_low(pair(self.core), self.to_core(pair(1 - self.core)))
        away = lax.dynamic_slice_in_dim(both, (1 - self.x) * size, size, axis)
        keep = lax.dynamic_slice_in_dim(both, self.x * size, size, axis)
        return add_low(keep, self.to_x(away))

    def sum_ctx(self, value):
        value = lax.optimization_barrier(value.astype(LOW))
        if self.ctxs == 2:
            return value.astype(jnp.float32) + self.to_y(value).astype(jnp.float32)
        return lax.psum(value.astype(jnp.float32), "ctx")

    def reduce_weight(self, term):
        part = lax.psum_scatter(term, ("fsdp", "ctx"), scatter_dimension=0, tiled=True)
        if self.ctxs != 2:
            return lax.all_gather(part, "ctx", axis=0, tiled=True).astype(jnp.float32).T
        part = lax.optimization_barrier(part)
        got = self.to_y(part)
        return lay(jnp.where(self.ctx == 0, part, got), jnp.where(self.ctx == 0, got, part))


def local(
    inputs,
    cotangent,
    positions,
    attn_gain,
    query_weight,
    query_bias,
    key_weight,
    key_bias,
    value_weight,
    value_bias,
    output_weight,
    mlp_gain,
    gate_weight,
    up_weight,
    down_weight,
):
    links = Links()
    seq_count, block_len, width = inputs.shape
    tp, tps, ctx, ctxs = links.tp, links.tps, links.ctx, links.ctxs
    fsdp, fsdps = links.fsdp, links.fsdps
    own = block_len // tps
    local_heads, kv_heads = query_bias.shape[0], key_bias.shape[0]
    head_dim = key_weight.shape[1] // kv_heads
    q_cols = local_heads * head_dim
    kv_cols = 2 * kv_heads * head_dim
    depth = q_cols * tps
    shard = width // fsdps
    tokens = seq_count * block_len
    key_block = block_len // 2 if block_len % (2 * own) == 0 else block_len
    seqs = range(seq_count)

    def place(seq, device):
        return device if seq % 2 == 0 else tps - 1 - device

    def block_rows(value, hop):
        return jnp.concatenate(
            [
                lax.dynamic_slice_in_dim(value[s], place(s, links.at(hop)) * own, own, 0)
                for s in seqs
            ],
            axis=0,
        )

    meta = jnp.stack(
        [fsdp, tp, ctx, ctx * (block_len // key_block)] + [place(s, tp) for s in seqs]
    ).astype(jnp.int32)

    lanes = q_cols + kv_cols
    smalls = jnp.concatenate([b.reshape(-1) for b in (query_bias, key_bias, value_bias)])
    extra = jnp.stack(
        [jnp.pad(row, (0, lanes - row.shape[0])) for row in (attn_gain, mlp_gain, smalls)]
    )
    extra = jnp.pad(extra, ((0, 13), (0, 0)))
    pack = jnp.concatenate(
        [jnp.concatenate([query_weight, key_weight, value_weight], axis=1), extra], axis=0
    )
    pack_core, pack_across = links.to_core(pack), links.to_x(pack)
    qkv = pack, pack_core, pack_across, links.to_core(pack_across)
    oq_blocks = lax.all_gather(jnp.concatenate([output_weight, query_weight], axis=0), "tp", axis=0)
    if ctxs == 2:
        up_mine = up_weight.T
        half = up_mine.shape[0] // 2
        up_near = links.to_x(
            after(lax.dynamic_slice_in_dim(up_mine, ctx * half, half, 0), pack_across)
        )
    else:
        up_near = pack_across
    rows = jnp.stack([item[shard : shard + 3] for item in qkv])
    rows = [
        lax.dynamic_index_in_dim(rows, jnp.bitwise_xor(fsdp, j), 0, keepdims=False) for j in range(4)
    ]
    attn_gamma = jnp.concatenate([r[0, :shard] for r in rows])[None].astype(jnp.float32)
    mlp_gamma = jnp.concatenate([r[1, :shard] for r in rows])[None].astype(jnp.float32)
    bias = jnp.concatenate(
        [r[2, : smalls.shape[0]].reshape(-1, head_dim // fsdps) for r in rows], axis=1
    ).reshape(1, lanes).astype(jnp.float32)
    bias = after(bias, up_near)

    cosine, sine = rope_tables(positions.reshape(tokens), head_dim)
    normed_one, query_blocks, kv_own = project(
        meta, inputs, attn_gamma, bias, qkv, cosine, sine, (local_heads, kv_heads, head_dim, tps)
    )
    if ctxs == 2:
        kv_before = lax.ppermute(kv_own, "ctx", [(0, 1)])
    else:
        kv_before = lax.all_gather(
            kv_own.reshape(seq_count, block_len, kv_cols), "ctx", axis=1, tiled=True
        ).reshape(seq_count * block_len * ctxs, kv_cols)

    def swap(block_of):
        return [block_of(tp)] + [
            links.hop_tp(block_of((tp + hop) % tps), hop) for hop in range(1, tps)
        ]

    queries = jnp.stack(swap(lambda d: lax.dynamic_index_in_dim(query_blocks, d, 0, keepdims=False)))

    def gather_whole(item):
        return lax.all_gather(after(item, up_near), "fsdp", axis=1, tiled=True)

    gate_full, down_full = gather_whole(gate_weight.T), gather_whole(down_weight)
    o_wide = after(oq_blocks, kv_own)[:, :q_cols].reshape(depth, shard)
    o_across = links.to_x(o_wide)
    o_core = links.to_core(after(o_wide, queries))

    late_cot = after(cotangent, kv_own)
    cot_all = jnp.concatenate([block_rows(late_cot, hop) for hop in range(tps)], axis=0)
    one_all = jnp.concatenate(
        [block_rows(normed_one.reshape(seq_count, block_len, width), hop) for hop in range(tps)], axis=0
    )

    order = jnp.tile(jnp.arange(own, dtype=jnp.int32), depth // head_dim // kv_heads)[None]
    order = after(order, (cot_all, one_all))
    sizes = (seq_count, kv_heads, head_dim, tps)
    mixed, lse = attend(meta, queries, kv_before, kv_own, order, key_block, sizes)
    o_core_across = links.to_core(after(o_across, mixed))
    o_parts = (o_wide, o_core, o_across, o_core_across)
    hidden, normed_two = merge(meta, mixed, inputs, o_parts, mlp_gamma, tps)
    two_blocks = [normed_two, links.hop_tp(normed_two)]
    q_wide = jnp.concatenate([oq_blocks[j, q_cols:] for j in range(tps)], axis=1)
    if ctxs == 2:
        up_far = links.to_y(after(up_near, normed_two))
        up_core, up_near_core = (links.to_core(after(item, mixed)) for item in (up_mine, up_near))
        up_far_core = links.to_core(up_far)
        up_full = assemble(meta, up_mine, up_near, up_far, up_core, up_near_core, up_far_core)
    else:
        up_full = gather_whole(up_weight.T)
    two_blocks.append(links.hop_tp(after(two_blocks[-1], (gate_full, up_full, down_full))))
    two_blocks.append(links.hop_tp(two_blocks[-1]))
    q_full = lax.all_gather(after(q_wide, down_full), "fsdp", axis=0, tiled=True)

    kept, two_parts, mixed_parts, two_total = None, [], [], None
    for hop in range(tps):
        block = two_blocks[hop]
        if hop + 1 < tps:
            block = after(block, two_blocks[hop + 1])
        if two_total is not None:
            block = after(block, two_total)
        kept, two_part, mixed_part = feed(
            meta, block, cot_all, gate_full, up_full, down_full, hop, tps, kept
        )
        two_parts.append(two_part)
        mixed_parts.append(mixed_part)
        if hop >= 1:
            two_total = two_part if hop == 1 else add_low(two_part, two_got)
            two_got = links.hop_tp(two_total)
        two_total = two_total if hop >= 2 else None
    two_own = two_parts[0]
    act_all, gate_all, up_all = kept
    two_all = jnp.concatenate(two_blocks, axis=0)
    down_term = inner_rows(cot_all, after(act_all, two_total)).astype(LOW)
    down_weight_grad = links.reduce_weight(down_term)
    two_got = after(two_got, down_term)

    hidden_grad, branch_grad, attended_grad, mlp_term = turn(
        meta, two_own, two_got, hidden, cotangent, o_parts, mlp_gamma, depth, tps
    )
    mixed_got = links.hop_tp(after(mixed_parts[1], two_got))
    q_grads, kv_parts, token = [], [], two_got
    for s in seqs:
        q_grad, grad_before, grad_own = attend_back(
            meta, s, queries, kv_before, kv_own, order, mixed, attended_grad, after(lse, token),
            cosine, sine, key_block, sizes,
        )
        q_grads.append(q_grad)
        if ctxs == 2:
            kv_parts.append((grad_own, lax.ppermute(grad_before, "ctx", [(1, 0)])))
        else:
            wide_grad = lax.dynamic_update_slice_in_dim(grad_before, grad_own, ctx * block_len, 2)
            kv_parts.append((lax.psum_scatter(wide_grad, "ctx", scatter_dimension=2, tiled=True), None))
        token = (mixed_got, q_grad)
    mixed_got = links.hop_tp(add_low(mixed_parts[2], after(mixed_got, q_grads[0])))
    q_grad = jnp.concatenate(q_grads, axis=0)
    kv_parts = [
        mine if got is None else add_low(after(mine, mixed_got), got) for mine, got in kv_parts
    ]
    gate_term = inner_rows(two_all, after(gate_all, kv_parts)).astype(LOW)
    mixed_got = links.hop_tp(add_low(mixed_parts[3], mixed_got))

    def kv_rows(hop):
        return jnp.stack(
            [
                lax.dynamic_slice_in_dim(kv_parts[s], place(s, links.at(hop)) * own, own, 2)
                for s in seqs
            ],
            axis=2,
        )

    kv_mine = kv_rows(0)
    kv_got = links.hop_tp(kv_rows(1))
    kv_got = links.hop_tp(add_low(kv_rows(2), after(kv_got, (gate_term, mixed_got))))
    up_term = inner_rows(two_all, after(up_all, (gate_term, kv_parts))).astype(LOW)
    gate_weight_grad = links.reduce_weight(after(gate_term, kv_got)).T
    kv_got = links.hop_tp(add_low(kv_rows(3), after(kv_got, up_term)))
    up_weight_grad = links.reduce_weight(after(up_term, kv_got)).T
    out_low = hidden + mixed_parts[0].astype(jnp.float32) + mixed_got.astype(jnp.float32)
    out_low = lax.optimization_barrier(out_low.astype(LOW))
    out_blocks = [out_low, links.hop_tp(out_low)]
    output_part = links.scatter_fsdp(inner_rows(mixed, after(branch_grad, up_term)).astype(LOW), 1)
    input_low, kv_grad, attn_term = finish(
        meta, after(q_grad, down_weight_grad), kv_mine, kv_got, cosine, sine, q_full, qkv, inputs, hidden_grad, attn_gamma, tps
    )
    input_low = lax.optimization_barrier(input_low)
    in_blocks = [input_low, links.hop_tp(input_low)]

    kv_each = kv_cols // tps
    attn_sum = jnp.sum(attn_term, axis=0)
    mlp_sum = jnp.sum(mlp_term, axis=0)

    def share(device):
        grads = jnp.concatenate(
            [
                lax.dynamic_slice_in_dim(q_grad, device * q_cols, q_cols, 1),
                lax.dynamic_slice_in_dim(kv_grad, device * kv_each, kv_each, 1),
            ],
            axis=1,
        )
        gains = jnp.concatenate(
            [lax.dynamic_slice_in_dim(item, device * shard, shard, 1) for item in (attn_sum, mlp_sum)], axis=0
        )
        gains = jnp.pad(gains, ((0, 14), (0, q_cols + kv_each - shard))).astype(LOW)
        return jnp.concatenate([grads, gains], axis=0)

    shares = swap(share)
    own_tokens = seq_count * own
    grads_all = jnp.concatenate([item[:own_tokens] for item in shares], axis=0)
    gain_rows = sum(item[own_tokens : own_tokens + 2].astype(jnp.float32) for item in shares)
    bias_row = jnp.sum(grads_all.astype(jnp.float32), axis=0, keepdims=True)
    below = jnp.pad(jnp.concatenate([gain_rows, bias_row], axis=0), ((0, 13), (0, 0))).astype(LOW)
    term = inner_rows(one_all, grads_all).astype(LOW)
    in_blocks.append(links.hop_tp(after(in_blocks[-1], (term, out_blocks[1], gate_weight_grad))))
    out_blocks.append(links.hop_tp(after(out_blocks[-1], in_blocks[1])))

    def output_rows(hop):
        return lax.dynamic_slice_in_dim(output_part, links.at(hop) * q_cols, q_cols, 0)

    output_got = links.hop_tp(after(output_rows(1), in_blocks[1]))
    in_blocks.append(
        links.hop_tp(after(in_blocks[-1], (out_blocks[2], output_got, up_weight_grad)))
    )
    out_blocks.append(links.hop_tp(after(out_blocks[-1], in_blocks[2])))
    output_got = links.hop_tp(add_low(output_rows(2), after(output_got, in_blocks[2])))
    term = jnp.concatenate(
        [item for j in range(fsdps) for item in (term[j * shard : (j + 1) * shard], below)], axis=0
    )
    total = links.sum_ctx(links.scatter_fsdp(term, 0))
    query_weight_grad = total[:shard, :q_cols]
    below = total[shard:]
    part = head_dim // fsdps
    query_bias_grad = lax.dynamic_slice_in_dim(
        below[2, :q_cols].reshape(local_heads, head_dim), fsdp * part, part, 1
    )
    kv_low = jnp.concatenate(
        [total[:shard, q_cols:], below[:, :q_cols].reshape(-1, kv_each), below[:, q_cols:]], axis=0
    ).astype(LOW)
    kv_low = lax.optimization_barrier(after(kv_low, in_blocks[2]))
    kv_blocks = links.gather_tp(kv_low)
    output_got = links.hop_tp(add_low(output_rows(3), output_got))
    output_weight_grad = links.sum_ctx(add_low(output_rows(0), output_got))
    out_blocks[0] = after(out_blocks[0], (kv_blocks[-1], output_weight_grad, up_weight_grad))
    outputs = spread_out(meta, out_blocks, seq_count, LOW)
    in_blocks[0] = after(in_blocks[0], outputs)
    input_grad = spread_out(meta, in_blocks, seq_count, jnp.float32)
    all_low = jnp.stack(kv_blocks)
    by_device = [
        lax.dynamic_index_in_dim(all_low, links.at(j), 0, keepdims=False) for j in range(tps)
    ]
    kv_weight = jnp.concatenate([item[:shard] for item in by_device], axis=1).astype(jnp.float32)
    mine = lax.dynamic_index_in_dim(all_low, (tp - fsdp + tps) % tps, 0, keepdims=False)
    gains = mine[shard : shard + 16 * (q_cols // kv_each)].reshape(16, q_cols).astype(jnp.float32)
    kv_bias = jnp.stack([item[-14] for item in by_device]).reshape(2, kv_heads, head_dim)
    kv_bias = lax.dynamic_slice_in_dim(kv_bias, fsdp * part, part, 2).astype(jnp.float32)
    half = kv_cols // 2

    return (
        outputs,
        input_grad,
        gains[0],
        query_weight_grad,
        query_bias_grad,
        kv_weight[:, :half],
        kv_bias[0],
        kv_weight[:, half:],
        kv_bias[1],
        output_weight_grad,
        gains[1],
        gate_weight_grad,
        up_weight_grad,
        down_weight_grad,
    )


def solution(mesh):
    in_specs = (
        P("fsdp", "ctx", None),
        P("fsdp", "ctx", None),
        P("fsdp", "ctx"),
        P("fsdp"),
        P("fsdp", "tp"),
        P("tp", "fsdp"),
        P("fsdp", None),
        P(None, "fsdp"),
        P("fsdp", None),
        P(None, "fsdp"),
        P("tp", "fsdp"),
        P("fsdp"),
        P("fsdp", "tp"),
        P("fsdp", "tp"),
        P("tp", "fsdp"),
    )
    out_specs = (
        P("fsdp", "ctx", None),
        P("fsdp", "ctx", None),
        P("fsdp"),
        P("fsdp", "tp"),
        P("tp", "fsdp"),
        P("fsdp", None),
        P(None, "fsdp"),
        P("fsdp", None),
        P(None, "fsdp"),
        P("tp", "fsdp"),
        P("fsdp"),
        P("fsdp", "tp"),
        P("fsdp", "tp"),
        P("tp", "fsdp"),
    )
    return jax.shard_map(local, mesh=mesh, in_specs=in_specs, out_specs=out_specs, check_vma=False)
```

```python
import functools
import math

import jax
import jax.numpy as jnp
from jax import lax
from jax.experimental import pallas as pl
from jax.experimental.pallas import tpu as pltpu
from jax.sharding import PartitionSpec as P

EPS = 1e-06
THETA = 1000000.0
LOG2E = 1.0 / math.log(2.0)
LOW = jnp.bfloat16
MASKED = -1e30
MIB = 1024 * 1024


def rope_tables(position, width):
    half = width // 2
    freqs = jnp.exp(jnp.arange(half, dtype=jnp.float32) * (-2.0 * math.log(THETA) / width))
    angle = position.astype(jnp.float32)[..., None] * freqs
    cosine, sine = jnp.cos(angle), jnp.sin(angle)
    return (
        jnp.concatenate([cosine, cosine], axis=-1),
        jnp.concatenate([-sine, sine], axis=-1),
    )


def dot(left, right):
    return jnp.dot(left, right, preferred_element_type=jnp.float32)


def inner_rows(left, right):
    return lax.dot_general(
        left, right, (((0,), (0,)), ((), ())), preferred_element_type=jnp.float32
    )


def inner_cols(left, right):
    return lax.dot_general(
        left, right, (((1,), (1,)), ((), ())), preferred_element_type=jnp.float32
    )


def add_low(left, right):
    return (left.astype(jnp.float32) + right.astype(jnp.float32)).astype(LOW)


def after(value, token):
    return lax.optimization_barrier((value, token))[0]


def root_of(values):
    return lax.rsqrt(jnp.mean(values * values, axis=-1, keepdims=True) + EPS)


FSDP, TP, CTX, BEFORE, PLACE = 0, 1, 2, 3, 4


def shard_at(meta, flip, size):
    return pl.multiple_of(jnp.bitwise_xor(meta[FSDP], flip) * size, size)


def tp_at(meta, hop, tps, size):
    return pl.multiple_of(lax.rem(meta[TP] + tps - hop, tps) * size, size)


def call(kernel, grid, in_specs, out_specs, out_shape, scratch=(), cost=None, name=None, vmem=48):
    return pl.pallas_call(
        kernel,
        grid_spec=pltpu.PrefetchScalarGridSpec(
            num_scalar_prefetch=1,
            grid=grid,
            in_specs=in_specs,
            out_specs=out_specs,
            scratch_shapes=list(scratch),
        ),
        out_shape=out_shape,
        compiler_params=pltpu.CompilerParams(vmem_limit_bytes=vmem * MIB),
        cost_estimate=cost,
        name=name,
    )


def whole(array):
    return pl.BlockSpec(array.shape, lambda *_: (0,) * array.ndim)


def shape(dims, kind):
    return jax.ShapeDtypeStruct(dims, kind)


def project_kernel(
    local_heads, kv_heads, head_dim, meta, x_ref, gain_ref, bias_ref, *refs
):
    weights, (cos_ref, sin_ref, n_ref, q_ref, kv_ref) = refs[:4], refs[4:]
    rows = x_ref.shape[1]
    size = n_ref.shape[1] // 4
    values = x_ref[...].reshape(rows, -1).astype(jnp.float32)
    n_ref[...] = (values * root_of(values) * gain_ref[...]).astype(LOW)
    lin = bias_ref[...]
    for flip, weight in enumerate(weights):
        lin = lin + dot(n_ref[:, pl.ds(shard_at(meta, flip, size), size)], weight[:size, :])
    cosine, sine = cos_ref[...], sin_ref[...]
    for head in range(local_heads + 2 * kv_heads):
        part = lin[:, head * head_dim : (head + 1) * head_dim]
        if head < local_heads + kv_heads:
            part = part * cosine + pltpu.roll(part, head_dim // 2, 1) * sine
        if head < local_heads:
            q_ref[0, :, head * head_dim : (head + 1) * head_dim] = part.astype(LOW)
        else:
            at = (head - local_heads) * head_dim
            kv_ref[:, at : at + head_dim] = part.astype(LOW)


def project(meta, inputs, gain, bias, weights, cosine, sine, sizes):
    seq_count, block_len, width = inputs.shape
    local_heads, kv_heads, head_dim, tps = sizes
    own = block_len // tps
    q_cols, kv_cols = local_heads * head_dim, 2 * kv_heads * head_dim

    def row(i, m):
        return (i, 0)

    def device(i, m):
        seq, place = i // tps, i % tps
        return jnp.where(seq % 2 == 0, place, tps - 1 - place), seq, 0

    tokens = seq_count * block_len
    return call(
        functools.partial(project_kernel, local_heads, kv_heads, head_dim),
        (seq_count * tps,),
        [
            pl.BlockSpec((1, own, width), lambda i, m: (i // tps, i % tps, 0)),
            whole(gain), whole(bias), *(whole(w) for w in weights),
            pl.BlockSpec((own, head_dim), row), pl.BlockSpec((own, head_dim), row),
        ],
        [
            pl.BlockSpec((own, width), row),
            pl.BlockSpec((1, own, q_cols), device),
            pl.BlockSpec((own, kv_cols), row),
        ],
        [
            shape((tokens, width), LOW),
            shape((tps, seq_count * own, q_cols), LOW),
            shape((tokens, kv_cols), LOW),
        ],
        cost=pl.CostEstimate(
            flops=2 * tokens * width * (q_cols + kv_cols), bytes_accessed=8 * tokens * width, transcendentals=0
        ),
        name="project",
    )(meta, inputs, gain, bias, *weights, cosine, sine)


def fwd_kernel(
    heads, block, parts, meta, *refs
):
    q_refs, (kb_ref, vb_ref, k_ref, v_ref, order_ref, o_ref, lse_ref, qg_ref, acc_ref, m_ref, l_ref) = (
        refs[:parts], refs[parts:]
    )
    own, cols = q_refs[0].shape[1:]
    head_dim = acc_ref.shape[0]
    scale = LOG2E / math.sqrt(head_dim)
    each = cols // head_dim
    for head in range(heads):
        qg_ref[head * own : (head + 1) * own, :] = q_refs[head // each][
            0, :, (head % each) * head_dim : (head % each + 1) * head_dim
        ]
    acc_ref[...] = jnp.zeros_like(acc_ref)
    m_ref[...] = jnp.full_like(m_ref, MASKED)
    l_ref[...] = jnp.zeros_like(l_ref)
    first = meta[PLACE + pl.program_id(0)] * own
    last = first // block

    def step(key_ref, value_ref, index, masked):
        start = pl.multiple_of(index * block, block)
        keys = key_ref[pl.ds(start, block), :]
        values = value_ref[pl.ds(start, block), :]
        logits = inner_cols(keys, qg_ref[...]) * scale
        if masked:
            key_order = (start - first) + lax.broadcasted_iota(jnp.int32, logits.shape, 0)
            logits = jnp.where(key_order <= order_ref[...], logits, MASKED)
        before = m_ref[...]
        peak = jnp.maximum(before, jnp.max(logits, axis=0, keepdims=True))
        weights = jnp.exp2(logits - peak)
        fade = jnp.exp2(before - peak)
        m_ref[...] = peak
        l_ref[...] = l_ref[...] * fade + jnp.sum(weights, axis=0, keepdims=True)
        acc_ref[...] = acc_ref[...] * fade + inner_rows(values, weights.astype(LOW))

    def early(index, carry):
        step(kb_ref, vb_ref, index, False)
        return carry

    def late(index, carry):
        step(k_ref, v_ref, index, False)
        return carry

    lax.fori_loop(0, meta[BEFORE], early, 0)
    lax.fori_loop(0, last, late, 0)
    step(k_ref, v_ref, last, True)
    total = l_ref[...]
    lse_ref[...] = (m_ref[...] + jnp.log2(total)).reshape(lse_ref.shape)
    mixed = jnp.transpose(acc_ref[...] / total)
    for head in range(heads):
        o_ref[:, head * head_dim : (head + 1) * head_dim] = mixed[
            head * own : (head + 1) * own, :
        ].astype(LOW)


def bwd_kernel(heads, block, parts, seq, meta, *refs):
    q_refs, (
        kb_ref, vb_ref, k_ref, v_ref, order_ref, o_ref, g_ref, lse_ref, cos_ref, sin_ref,
        dq_ref, db_ref, dd_ref, qg_ref, gg_ref, acc_ref,
    ) = refs[:parts], refs[parts:]
    own, cols = q_refs[0].shape[1:]
    head_dim = acc_ref.shape[1]
    scale = 1.0 / math.sqrt(head_dim)
    each = cols // head_dim
    for head in range(heads):
        rows = slice(head * own, (head + 1) * own)
        at = slice(head * head_dim, (head + 1) * head_dim)
        qg_ref[rows, :] = q_refs[head // each][
            0, :, (head % each) * head_dim : (head % each + 1) * head_dim
        ]
        gg_ref[rows, :] = g_ref[:, at]
        acc_ref[rows, :] = g_ref[:, at].astype(jnp.float32) * o_ref[:, at].astype(jnp.float32)
    center = jnp.sum(jnp.transpose(acc_ref[...]), axis=0, keepdims=True)
    acc_ref[...] = jnp.zeros_like(acc_ref)
    lse = lse_ref[...].reshape(order_ref.shape)
    first = meta[PLACE + seq] * own
    last = first // block

    def step(key_ref, value_ref, out_ref, index, masked):
        start = pl.multiple_of(index * block, block)
        keys = key_ref[pl.ds(start, block), :]
        values = value_ref[pl.ds(start, block), :]
        logits = inner_cols(keys, qg_ref[...]) * (scale * LOG2E)
        if masked:
            key_order = (start - first) + lax.broadcasted_iota(jnp.int32, logits.shape, 0)
            logits = jnp.where(key_order <= order_ref[...], logits, MASKED)
        probs = jnp.exp2(logits - lse)
        out_ref[1, 0, pl.ds(start, block), :] = dot(probs.astype(LOW), gg_ref[...]).astype(LOW)
        prob_grad = inner_cols(values, gg_ref[...])
        logit_grad = (probs * (prob_grad - center)).astype(LOW)
        out_ref[0, 0, pl.ds(start, block), :] = (dot(logit_grad, qg_ref[...]) * scale).astype(LOW)
        acc_ref[...] += inner_rows(logit_grad, keys)

    def early(index, carry):
        step(kb_ref, vb_ref, db_ref, index, False)
        return carry

    def late(index, carry):
        step(k_ref, v_ref, dd_ref, index, False)
        return carry

    def clear(ref):
        def body(index, carry):
            start = pl.multiple_of(index * block, block)
            ref[:, :, pl.ds(start, block), :] = jnp.zeros((2, 1, block, head_dim), LOW)
            return carry

        return body

    lax.fori_loop(0, meta[BEFORE], early, 0)
    lax.fori_loop(meta[BEFORE], kb_ref.shape[0] // block, clear(db_ref), 0)
    lax.fori_loop(0, last, late, 0)
    step(k_ref, v_ref, dd_ref, last, True)
    lax.fori_loop(last + 1, k_ref.shape[0] // block, clear(dd_ref), 0)
    for head in range(heads):
        grad = acc_ref[head * own : (head + 1) * own, :] * scale
        grad = grad * cos_ref[...] - pltpu.roll(grad, head_dim // 2, 1) * sin_ref[...]
        dq_ref[:, head * head_dim : (head + 1) * head_dim] = grad.astype(LOW)


def attention_specs(queries, kv_before, kv_own, sizes, seq=None):
    seq_count, kv_heads, head_dim, tps = sizes
    rows = queries.shape[1] // seq_count
    parts = tps // kv_heads
    heads = queries.shape[2] * parts // head_dim
    before, block_len = kv_before.shape[0] // seq_count, kv_own.shape[0] // seq_count

    def spec(dims, index):
        if seq is None:
            return pl.BlockSpec(dims, index)
        return pl.BlockSpec(dims, lambda g, m: index(seq, g, m))

    def piece(part):
        return spec(
            (1, rows, queries.shape[2]),
            lambda s, g, m: (lax.rem(m[TP] + tps - (g * parts + part), tps), s, 0),
        )

    specs = [piece(part) for part in range(parts)] + [
        spec((before, head_dim), lambda s, g, m: (s, g)),
        spec((before, head_dim), lambda s, g, m: (s, kv_heads + g)),
        spec((block_len, head_dim), lambda s, g, m: (s, g)),
        spec((block_len, head_dim), lambda s, g, m: (s, kv_heads + g)),
        spec((1, heads * rows), lambda s, g, m: (0, 0)),
    ]
    return specs, rows, parts, heads, before, block_len


def attend(meta, queries, kv_before, kv_own, order, block, sizes):
    seq_count, kv_heads, head_dim, tps = sizes
    specs, rows, parts, heads, before, block_len = attention_specs(queries, kv_before, kv_own, sizes)
    width, wide = kv_heads * heads * head_dim, heads * rows
    work = seq_count * rows * width * (before + block_len)
    return call(
        functools.partial(fwd_kernel, heads, block, parts),
        (seq_count, kv_heads),
        specs,
        [
            pl.BlockSpec((rows, heads * head_dim), lambda s, g, m: (s, g)),
            pl.BlockSpec((1, 1, 1, wide), lambda s, g, m: (s, g, 0, 0)),
        ],
        [shape((seq_count * rows, width), LOW), shape((seq_count, kv_heads, 1, wide), jnp.float32)],
        [
            pltpu.VMEM((wide, head_dim), LOW),
            pltpu.VMEM((head_dim, wide), jnp.float32),
            pltpu.VMEM((1, wide), jnp.float32),
            pltpu.VMEM((1, wide), jnp.float32),
        ],
        cost=pl.CostEstimate(flops=8 * work, bytes_accessed=1 << 22, transcendentals=0),
        name="attend",
    )(meta, *([queries] * parts), kv_before, kv_before, kv_own, kv_own, order)


def attend_back(
    meta, seq, queries, kv_before, kv_own, order, mixed, grads, lse, cosine, sine, block, sizes
):
    seq_count, kv_heads, head_dim, tps = sizes
    specs, rows, parts, heads, before, block_len = attention_specs(
        queries, kv_before, kv_own, sizes, seq
    )
    width, wide = kv_heads * heads * head_dim, heads * rows
    work = rows * width * (before + block_len)
    wide_spec = pl.BlockSpec((rows, heads * head_dim), lambda g, m: (seq, g))
    table_spec = pl.BlockSpec((rows, head_dim), lambda g, m: (seq * tps + m[PLACE + seq], 0))
    return call(
        functools.partial(bwd_kernel, heads, block, parts, seq),
        (kv_heads,),
        specs
        + [
            wide_spec,
            wide_spec,
            pl.BlockSpec((1, 1, 1, wide), lambda g, m: (seq, g, 0, 0)),
            table_spec,
            table_spec,
        ],
        [
            pl.BlockSpec((rows, heads * head_dim), lambda g, m: (0, g)),
            pl.BlockSpec((2, 1, before, head_dim), lambda g, m: (0, g, 0, 0)),
            pl.BlockSpec((2, 1, block_len, head_dim), lambda g, m: (0, g, 0, 0)),
        ],
        [
            shape((rows, width), LOW),
            shape((2, kv_heads, before, head_dim), LOW),
            shape((2, kv_heads, block_len, head_dim), LOW),
        ],
        [
            pltpu.VMEM((wide, head_dim), LOW),
            pltpu.VMEM((wide, head_dim), LOW),
            pltpu.VMEM((wide, head_dim), jnp.float32),
        ],
        cost=pl.CostEstimate(flops=16 * work, bytes_accessed=1 << 22, transcendentals=0),
        name="attend_back",
    )(
        meta, *([queries] * parts), kv_before, kv_before, kv_own, kv_own, order,
        mixed, grads, lse, cosine, sine,
    )


def merge_kernel(tps, meta, o_ref, x_ref, *refs):
    weights, (gain_ref, h_ref, n_ref, turned_ref) = refs[:4], refs[4:]
    rows, width = h_ref.shape
    size, depth = width // 4, o_ref.shape[1]
    part = depth // tps
    for hop in range(tps):
        turned_ref[:, hop * part : (hop + 1) * part] = o_ref[:, pl.ds(tp_at(meta, hop, tps, part), part)]
    turned = turned_ref[...]
    for flip, weight in enumerate(weights):
        at = pl.ds(shard_at(meta, flip, size), size)
        h_ref[:, at] = x_ref[0, :, at].astype(jnp.float32) + dot(turned, weight[...])
    hidden = h_ref[...]
    n_ref[...] = (hidden * root_of(hidden) * gain_ref[...]).astype(LOW)


def merge(meta, mixed, inputs, weights, gain, tps):
    seq_count, block_len, width = inputs.shape
    own = block_len // tps
    depth = mixed.shape[1]
    row = pl.BlockSpec((own, width), lambda s, m: (s, 0))
    return call(
        functools.partial(merge_kernel, tps),
        (seq_count,),
        [
            pl.BlockSpec((own, depth), lambda s, m: (s, 0)),
            pl.BlockSpec((1, own, width), lambda s, m: (s, m[PLACE + s], 0)),
            *(whole(w) for w in weights),
            whole(gain),
        ],
        [row, row],
        [shape((seq_count * own, width), jnp.float32), shape((seq_count * own, width), LOW)],
        [pltpu.VMEM((own, depth), LOW)],
        cost=pl.CostEstimate(
            flops=2 * seq_count * own * depth * width, bytes_accessed=1 << 23, transcendentals=0
        ),
        name="merge",
    )(meta, mixed, inputs, *weights, gain)


def turn_kernel(
    tps, meta, a_ref, b_ref, h_ref, c_ref, *refs,
):
    weights, (gain_ref, hg_ref, bg_ref, ag_ref, term_ref, turned_ref) = refs[:4], refs[4:]
    rows, width = h_ref.shape
    size, depth = width // 4, ag_ref.shape[1]
    two_grad = a_ref[...].astype(jnp.float32) + b_ref[...].astype(jnp.float32)
    hidden = h_ref[...]
    root = root_of(hidden)
    term_ref[...] = jnp.sum(two_grad * hidden * root, axis=0, keepdims=True).reshape(term_ref.shape)
    scaled = gain_ref[...] * two_grad
    grad = (
        c_ref[...].reshape(rows, width).astype(jnp.float32)
        + root * scaled
        - hidden * root**3 * jnp.mean(scaled * hidden, axis=-1, keepdims=True)
    )
    hg_ref[...] = grad
    bg_ref[...] = grad.astype(LOW)
    turned_ref[...] = jnp.zeros_like(turned_ref)
    for flip, weight in enumerate(weights):
        turned_ref[...] += inner_cols(bg_ref[:, pl.ds(shard_at(meta, flip, size), size)], weight[...])
    part = depth // tps
    for hop in range(tps):
        ag_ref[:, pl.ds(tp_at(meta, hop, tps, part), part)] = turned_ref[
            :, hop * part : (hop + 1) * part
        ].astype(LOW)


def turn(meta, two_own, two_got, hidden, cotangent, weights, gain, depth, tps):
    seq_count, block_len, width = cotangent.shape
    own = block_len // tps
    row = pl.BlockSpec((own, width), lambda s, m: (s, 0))
    tokens = seq_count * own
    return call(
        functools.partial(turn_kernel, tps),
        (seq_count,),
        [
            row, row, row,
            pl.BlockSpec((1, own, width), lambda s, m: (s, m[PLACE + s], 0)),
            *(whole(w) for w in weights),
            whole(gain),
        ],
        [
            row, row,
            pl.BlockSpec((own, depth), lambda s, m: (s, 0)),
            pl.BlockSpec((1, 1, width), lambda s, m: (s, 0, 0)),
        ],
        [
            shape((tokens, width), jnp.float32),
            shape((tokens, width), LOW),
            shape((tokens, depth), LOW),
            shape((seq_count, 1, width), jnp.float32),
        ],
        [pltpu.VMEM((own, depth), jnp.float32)],
        cost=pl.CostEstimate(flops=2 * tokens * depth * width, bytes_accessed=1 << 23, transcendentals=0),
        name="turn",
    )(meta, two_own, two_got, hidden, cotangent, *weights, gain)


def back_through_norm(grad, values, gain):
    root = root_of(values)
    scaled = gain * grad
    term = jnp.sum(grad * values * root, axis=0, keepdims=True)
    return root * scaled - values * root**3 * jnp.mean(scaled * values, axis=-1, keepdims=True), term


def finish_kernel(meta, g_ref, q_ref, x_ref, hg_ref, gain_ref, out_ref, term_ref):
    values = x_ref[...].reshape(hg_ref.shape).astype(jnp.float32)
    part, term = back_through_norm(inner_cols(g_ref[...], q_ref[...]), values, gain_ref[...])
    term_ref[...] = term.reshape(term_ref.shape)
    out_ref[...] = (hg_ref[...] + part).astype(LOW)


def finish(meta, q_grad, q_full, inputs, hidden_grad, gain, tps):
    seq_count, block_len, width = inputs.shape
    own = block_len // tps
    tokens = seq_count * own
    row = pl.BlockSpec((own, width), lambda s, m: (s, 0))
    return call(
        finish_kernel,
        (seq_count,),
        [
            pl.BlockSpec((own, q_grad.shape[1]), lambda s, m: (s, 0)),
            whole(q_full),
            pl.BlockSpec((1, own, width), lambda s, m: (s, m[PLACE + s], 0)),
            row,
            whole(gain),
        ],
        [row, pl.BlockSpec((1, 1, width), lambda s, m: (s, 0, 0))],
        [shape((tokens, width), LOW), shape((seq_count, 1, width), jnp.float32)],
        cost=pl.CostEstimate(
            flops=2 * tokens * q_grad.shape[1] * width, bytes_accessed=1 << 23, transcendentals=0
        ),
        name="finish",
    )(meta, q_grad, q_full, inputs, hidden_grad, gain)


def one_from_kv(meta, kv_grad, weights, one_ref):
    size = one_ref.shape[1] // 4
    skip = weights[0].shape[1] - kv_grad.shape[1]
    for flip, weight in enumerate(weights):
        one_ref[:, pl.ds(shard_at(meta, flip, size), size)] = inner_cols(
            kv_grad, weight[:size, skip:]
        )
    return one_ref[...]


def kv_kernel(kv_heads, head_dim, meta, a_ref, b_ref, cos_ref, sin_ref, *refs):
    weights, (x_ref, kv_ref, term_ref, one_ref) = refs[:4], refs[4:]
    cosine, sine = cos_ref[...], sin_ref[...]
    for kind in range(2):
        for head in range(kv_heads):
            grad = (
                a_ref[kind, head, 0].astype(jnp.float32) + b_ref[kind, head, 0].astype(jnp.float32)
            )
            if kind == 0:
                grad = grad * cosine - pltpu.roll(grad, head_dim // 2, 1) * sine
            at = (kind * kv_heads + head) * head_dim
            kv_ref[:, at : at + head_dim] = grad.astype(LOW)
    one = one_from_kv(meta, kv_ref[...], weights, one_ref)
    values = x_ref[...].reshape(one.shape).astype(jnp.float32)
    term = jnp.sum(one * values * root_of(values), axis=0, keepdims=True)
    term_ref[...] = term.reshape(term_ref.shape)


def kv_back(meta, kv_mine, kv_got, cosine, sine, weights, inputs, tps):
    seq_count, block_len, width = inputs.shape
    own = block_len // tps
    kv_heads, head_dim = kv_mine.shape[1], kv_mine.shape[4]
    kv_cols = 2 * kv_heads * head_dim
    kv_spec = pl.BlockSpec((2, kv_heads, 1, own, head_dim), lambda s, m: (0, 0, s, 0, 0))
    table_spec = pl.BlockSpec((own, head_dim), lambda s, m: (s * tps + m[PLACE + s], 0))
    return call(
        functools.partial(kv_kernel, kv_heads, head_dim),
        (seq_count,),
        [
            kv_spec, kv_spec, table_spec, table_spec,
            *(whole(w) for w in weights),
            pl.BlockSpec((1, own, width), lambda s, m: (s, m[PLACE + s], 0)),
        ],
        [
            pl.BlockSpec((own, kv_cols), lambda s, m: (s, 0)),
            pl.BlockSpec((1, 1, width), lambda s, m: (s, 0, 0)),
        ],
        [shape((seq_count * own, kv_cols), LOW), shape((seq_count, 1, width), jnp.float32)],
        [pltpu.VMEM((own, width), jnp.float32)],
        cost=pl.CostEstimate(
            flops=2 * seq_count * own * kv_cols * width, bytes_accessed=1 << 22, transcendentals=0
        ),
        name="kv_back",
    )(meta, kv_mine, kv_got, cosine, sine, *weights, inputs)


def last_kernel(tps, meta, *refs):
    blocks, kvs, weights = refs[:tps], refs[tps : 2 * tps], refs[2 * tps : 2 * tps + 4]
    x_ref, gain_ref, out_ref, one_ref = refs[2 * tps + 4 :]
    seq = pl.program_id(0)
    own = blocks[0].shape[0]
    for hop in range(tps):
        device = lax.rem(meta[TP] + tps - hop, tps)
        place = jnp.where(seq % 2 == 0, device, tps - 1 - device)
        at = pl.ds(pl.multiple_of(place * own, own), own)
        one = one_from_kv(meta, kvs[hop][...], weights, one_ref)
        values = x_ref[0, at, :].astype(jnp.float32)
        part, _ = back_through_norm(one, values, gain_ref[...])
        out_ref[0, at, :] = blocks[hop][...].astype(jnp.float32) + part


def last(meta, blocks, kvs, weights, inputs, gain):
    seq_count, block_len, width = inputs.shape
    tps = len(blocks)
    own = block_len // tps
    every = pl.BlockSpec((1, block_len, width), lambda s, m: (s, 0, 0))
    return call(
        functools.partial(last_kernel, tps),
        (seq_count,),
        [pl.BlockSpec((own, width), lambda s, m: (s, 0))] * tps
        + [pl.BlockSpec((own, kvs[0].shape[1]), lambda s, m: (s, 0))] * tps
        + [whole(w) for w in weights]
        + [every, whole(gain)],
        every,
        shape(inputs.shape, jnp.float32),
        [pltpu.VMEM((own, width), jnp.float32)],
        cost=pl.CostEstimate(
            flops=2 * seq_count * block_len * kvs[0].shape[1] * width, bytes_accessed=1 << 24, transcendentals=0
        ),
        name="last",
    )(meta, *blocks, *kvs, *weights, inputs, gain)


def feed_kernel(first, hidden, *refs):
    n_ref, c_ref, wg_ref, wu_ref, wd_ref = refs[1:6]
    act_ref, gg_ref, ug_ref, two_ref, mix_ref, two_acc, mix_acc = refs[6 if first else 9 :]
    step, tile = pl.program_id(0), wg_ref.shape[0]
    steps = -(-hidden // tile)

    def body(count):
        gate = inner_cols(n_ref[...], wg_ref[:count, :])
        up_part = inner_cols(n_ref[...], wu_ref[:count, :])
        act_grad = inner_cols(c_ref[...], wd_ref[:count, :])
        sigma = jax.nn.sigmoid(gate)
        silu = gate * sigma
        act = (silu * up_part).astype(LOW)
        gate_grad = (act_grad * up_part * (sigma * (1.0 + gate * (1.0 - sigma)))).astype(LOW)
        up_grad = (act_grad * silu).astype(LOW)
        act_ref[:, :count], gg_ref[:, :count], ug_ref[:, :count] = act, gate_grad, up_grad
        return (
            dot(gate_grad, wg_ref[:count, :]) + dot(up_grad, wu_ref[:count, :]),
            dot(act, wd_ref[:count, :]),
        )

    @pl.when(step == 0)
    def _():
        two_acc[...], mix_acc[...] = body(tile)

    @pl.when(jnp.logical_and(step > 0, step < steps - 1))
    def _():
        two, mix = body(tile)
        two_acc[...] += two
        mix_acc[...] += mix

    @pl.when(step == steps - 1)
    def _():
        two, mix = body(hidden - (steps - 1) * tile)
        two_ref[...] = (two_acc[...] + two).astype(LOW)
        mix_ref[...] = (mix_acc[...] + mix).astype(LOW)


def feed(meta, normed, cots, gate, up, down, hop, tps, kept):
    rows, width = normed.shape
    hidden = down.shape[0]
    tile = 768
    assert hidden > tile
    weight = pl.BlockSpec((tile, width), lambda j, m: (j, 0))
    column = pl.BlockSpec((rows, tile), lambda j, m: (hop, j))
    fixed = pl.BlockSpec((rows, width), lambda j, m: (0, 0))
    first = hop == 0
    wide = shape((tps * rows, hidden), LOW)
    *hiddens, two_part, mixed_part = pl.pallas_call(
        functools.partial(feed_kernel, first, hidden),
        grid_spec=pltpu.PrefetchScalarGridSpec(
            num_scalar_prefetch=1,
            grid=(-(-hidden // tile),),
            in_specs=[fixed, pl.BlockSpec((rows, width), lambda j, m: (hop, 0)), weight, weight, weight]
            + ([] if first else [pl.BlockSpec(memory_space=pl.ANY)] * 3),
            out_specs=[column, column, column, fixed, fixed],
            scratch_shapes=[pltpu.VMEM((rows, width), jnp.float32)] * 2,
        ),
        out_shape=[wide, wide, wide, shape((rows, width), LOW), shape((rows, width), LOW)],
        input_output_aliases={} if first else {6: 0, 7: 1, 8: 2},
        compiler_params=pltpu.CompilerParams(vmem_limit_bytes=56 * MIB),
        cost_estimate=pl.CostEstimate(
            flops=12 * rows * width * hidden, bytes_accessed=6 * width * hidden, transcendentals=rows * hidden
        ),
        name="feed",
    )(meta, normed, cots, gate, up, down, *(() if first else kept))
    return hiddens, two_part, mixed_part


def assemble_kernel(tiles, meta, own_ref, near_ref, far_ref, o_own_ref, o_near_ref, o_far_ref, out_ref):
    size = own_ref.shape[1]
    is_near = (pl.program_id(0) // tiles) == meta[CTX]
    out_ref[:, pl.ds(shard_at(meta, 0, size), size)] = own_ref[...]
    out_ref[:, pl.ds(shard_at(meta, 1, size), size)] = o_own_ref[...]

    @pl.when(is_near)
    def _():
        out_ref[:, pl.ds(shard_at(meta, 2, size), size)] = near_ref[...]
        out_ref[:, pl.ds(shard_at(meta, 3, size), size)] = o_near_ref[...]

    @pl.when(jnp.logical_not(is_near))
    def _():
        out_ref[:, pl.ds(shard_at(meta, 2, size), size)] = far_ref[...]
        out_ref[:, pl.ds(shard_at(meta, 3, size), size)] = o_far_ref[...]


def assemble(meta, own, near, far, other, other_near, other_far):
    rows, size = own.shape
    tiles = 2 if rows % 64 == 0 else 1
    tile = rows // (2 * tiles)
    every = pl.BlockSpec((tile, size), lambda i, m: (i, 0))
    half = pl.BlockSpec((tile, size), lambda i, m: (i % tiles, 0))
    return call(
        functools.partial(assemble_kernel, tiles),
        (2 * tiles,),
        [every, half, half, every, half, half],
        pl.BlockSpec((tile, 4 * size), lambda i, m: (i, 0)),
        shape((rows, 4 * size), LOW),
        cost=pl.CostEstimate(flops=0, bytes_accessed=16 * rows * size, transcendentals=0),
        name="assemble",
    )(meta, own, near, far, other, other_near, other_far)


def lay_kernel(low_ref, high_ref, out_ref):
    both = jnp.concatenate([low_ref[...], high_ref[...]], axis=0)
    out_ref[...] = jnp.transpose(both.astype(jnp.float32))


def lay(low, high):
    rows, cols = low.shape
    return pl.pallas_call(
        lay_kernel,
        in_specs=[pl.BlockSpec(memory_space=pltpu.VMEM)] * 2,
        out_specs=pl.BlockSpec(memory_space=pltpu.VMEM),
        out_shape=shape((cols, 2 * rows), jnp.float32),
        compiler_params=pltpu.CompilerParams(vmem_limit_bytes=48 * MIB),
        cost_estimate=pl.CostEstimate(flops=0, bytes_accessed=12 * rows * cols, transcendentals=0),
        name="lay",
    )(low, high)


def spread_kernel(tps, meta, *refs):
    out_ref = refs[tps]
    seq_count = out_ref.shape[0]
    own = refs[0].shape[0] // seq_count
    for hop in range(tps):
        device = lax.rem(meta[TP] + tps - hop, tps)
        for s in range(seq_count):
            place = device if s % 2 == 0 else tps - 1 - device
            at = pl.ds(pl.multiple_of(place * own, own), own)
            out_ref[s, at, :] = refs[hop][s * own : (s + 1) * own, :].astype(out_ref.dtype)


def spread_out(meta, blocks, seq_count, kind):
    tps = len(blocks)
    rows, width = blocks[0].shape
    dims = (seq_count, rows // seq_count * tps, width)
    return call(
        functools.partial(spread_kernel, tps),
        (1,),
        [whole(item) for item in blocks],
        pl.BlockSpec(dims, lambda *_: (0, 0, 0)),
        shape(dims, kind),
        cost=pl.CostEstimate(flops=0, bytes_accessed=8 * rows * tps * width, transcendentals=0),
        name="spread",
    )(meta, *blocks)


class Links:
    def __init__(self):
        self.tp, self.ctx, self.fsdp = (lax.axis_index(a) for a in ("tp", "ctx", "fsdp"))
        self.tps, self.ctxs, self.fsdps = (lax.axis_size(a) for a in ("tp", "ctx", "fsdp"))
        self.core, self.x = self.fsdp % 2, self.fsdp // 2
        assert self.fsdps == 4

    def to_core(self, value):
        return lax.ppermute(value, "fsdp", [(0, 1), (1, 0), (2, 3), (3, 2)])

    def to_x(self, value):
        return lax.ppermute(value, "fsdp", [(0, 2), (2, 0), (1, 3), (3, 1)])

    def to_y(self, value):
        return lax.ppermute(value, "ctx", [(0, 1), (1, 0)])

    def hop_tp(self, value, hop=1):
        return lax.ppermute(value, "tp", [(i, (i + hop) % self.tps) for i in range(self.tps)])

    def gather_fsdp(self, shard):
        across = self.to_x(shard)
        return shard, across, self.to_core(jnp.concatenate([shard, across], axis=0))

    def gather_tp(self, block):
        blocks = [block]
        for _ in range(1, self.tps):
            blocks.append(self.hop_tp(blocks[-1]))
        return blocks

    def scatter_tp(self, blocks):
        total = blocks[1]
        for hop in range(1, self.tps):
            got = self.hop_tp(total)
            if hop < self.tps - 1:
                total = add_low(blocks[hop + 1], got)
        return blocks[0], got

    def at(self, hop):
        return (self.tp - hop + self.tps) % self.tps

    def pairs(self, value, axis):
        size = value.shape[axis] // 4

        def pair(core):
            return jnp.concatenate(
                [
                    lax.dynamic_slice_in_dim(value, (2 * x + core) * size, size, axis)
                    for x in range(2)
                ],
                axis,
            )

        return pair(self.core), pair(1 - self.core)

    def scatter_core(self, pairs):
        return add_low(pairs[0], self.to_core(pairs[1]))

    def scatter_x(self, both, axis):
        size = both.shape[axis] // 2
        away = lax.dynamic_slice_in_dim(both, (1 - self.x) * size, size, axis)
        keep = lax.dynamic_slice_in_dim(both, self.x * size, size, axis)
        return add_low(keep, self.to_x(away))

    def sum_ctx(self, value):
        value = lax.optimization_barrier(value.astype(LOW))
        if self.ctxs == 2:
            return value.astype(jnp.float32) + self.to_y(value).astype(jnp.float32)
        return lax.psum(value.astype(jnp.float32), "ctx")

    def reduce_weight(self, term):
        part = lax.psum_scatter(term, ("fsdp", "ctx"), scatter_dimension=0, tiled=True)
        if self.ctxs != 2:
            return lax.all_gather(part, "ctx", axis=0, tiled=True).astype(jnp.float32).T
        part = lax.optimization_barrier(part)
        got = self.to_y(part)
        return lay(jnp.where(self.ctx == 0, part, got), jnp.where(self.ctx == 0, got, part))


def local(
    inputs,
    cotangent,
    positions,
    attn_gain,
    query_weight,
    query_bias,
    key_weight,
    key_bias,
    value_weight,
    value_bias,
    output_weight,
    mlp_gain,
    gate_weight,
    up_weight,
    down_weight,
):
    links = Links()
    seq_count, block_len, width = inputs.shape
    tp, tps, ctx, ctxs = links.tp, links.tps, links.ctx, links.ctxs
    fsdp, fsdps = links.fsdp, links.fsdps
    own = block_len // tps
    local_heads, kv_heads = query_bias.shape[0], key_bias.shape[0]
    head_dim = key_weight.shape[1] // kv_heads
    q_cols = local_heads * head_dim
    kv_cols = 2 * kv_heads * head_dim
    depth = q_cols * tps
    shard = width // fsdps
    tokens = seq_count * block_len
    key_block = block_len // 2 if block_len % (2 * own) == 0 else block_len
    seqs = range(seq_count)

    def place(seq, device):
        return device if seq % 2 == 0 else tps - 1 - device

    def block_rows(value, hop):
        return jnp.concatenate(
            [
                lax.dynamic_slice_in_dim(value[s], place(s, links.at(hop)) * own, own, 0)
                for s in seqs
            ],
            axis=0,
        )

    meta = jnp.stack(
        [fsdp, tp, ctx, ctx * (block_len // key_block)] + [place(s, tp) for s in seqs]
    ).astype(jnp.int32)

    lanes = q_cols + kv_cols
    smalls = jnp.concatenate([b.reshape(-1) for b in (query_bias, key_bias, value_bias)])
    extra = jnp.stack(
        [jnp.pad(row, (0, lanes - row.shape[0])) for row in (attn_gain, mlp_gain, smalls)]
    )
    extra = jnp.pad(extra, ((0, 13), (0, 0)))
    pack = jnp.concatenate(
        [jnp.concatenate([query_weight, key_weight, value_weight], axis=1), extra], axis=0
    )
    pack_core, pack_across = links.to_core(pack), links.to_x(pack)
    qkv = pack, pack_core, pack_across, links.to_core(pack_across)
    o_blocks = links.gather_tp(output_weight)
    up_mine = up_weight.T

    rows = jnp.stack([item[shard : shard + 3] for item in qkv])
    rows = [
        lax.dynamic_index_in_dim(rows, jnp.bitwise_xor(fsdp, j), 0, keepdims=False) for j in range(4)
    ]
    attn_gamma = jnp.concatenate([r[0, :shard] for r in rows])[None].astype(jnp.float32)
    mlp_gamma = jnp.concatenate([r[1, :shard] for r in rows])[None].astype(jnp.float32)
    bias = jnp.concatenate(
        [r[2, : smalls.shape[0]].reshape(-1, head_dim // fsdps) for r in rows], axis=1
    ).reshape(1, lanes).astype(jnp.float32)
    bias = after(bias, o_blocks[1])

    cosine, sine = rope_tables(positions.reshape(tokens), head_dim)
    normed_one, query_blocks, kv_own = project(
        meta, inputs, attn_gamma, bias, qkv, cosine, sine, (local_heads, kv_heads, head_dim, tps)
    )
    if ctxs == 2:
        kv_before = lax.ppermute(kv_own, "ctx", [(0, 1)])
        half = up_mine.shape[0] // 2
        up_near = links.to_x(
            after(lax.dynamic_slice_in_dim(up_mine, ctx * half, half, 0), pack_across)
        )
        up_far = links.to_y(after(up_near, kv_before))
    else:
        kv_before = lax.all_gather(
            kv_own.reshape(seq_count, block_len, kv_cols), "ctx", axis=1, tiled=True
        ).reshape(seq_count * block_len * ctxs, kv_cols)

    def swap(block_of):
        return [block_of(tp)] + [
            links.hop_tp(block_of((tp + hop) % tps), hop) for hop in range(1, tps)
        ]

    queries = jnp.stack(swap(lambda d: lax.dynamic_index_in_dim(query_blocks, d, 0, keepdims=False)))

    def gather_whole(item):
        return lax.all_gather(after(item, pack_across), "fsdp", axis=1, tiled=True)

    gate_full, down_full = gather_whole(gate_weight.T), gather_whole(down_weight)
    o_blocks = o_blocks[:2] + [after(item, kv_own) for item in o_blocks[2:]]
    o_wide = jnp.concatenate(o_blocks, axis=0)
    q_blocks = links.gather_tp(after(query_weight, kv_own))
    o_across = links.to_x(o_wide)
    o_core = links.to_core(after(o_wide, queries))

    late_cot = after(cotangent, kv_own)
    cot_all = jnp.concatenate([block_rows(late_cot, hop) for hop in range(tps)], axis=0)
    one_all = jnp.concatenate(
        [block_rows(normed_one.reshape(seq_count, block_len, width), hop) for hop in range(tps)], axis=0
    )

    order = jnp.tile(jnp.arange(own, dtype=jnp.int32), depth // head_dim // kv_heads)[None]
    order = after(order, (cot_all, one_all, q_blocks[2], *([up_near] if ctxs == 2 else [])))
    sizes = (seq_count, kv_heads, head_dim, tps)
    mixed, lse = attend(meta, queries, kv_before, kv_own, order, key_block, sizes)
    o_core_across = links.to_core(after(o_across, mixed))
    o_parts = (o_wide, o_core, o_across, o_core_across)
    hidden, normed_two = merge(meta, mixed, inputs, o_parts, mlp_gamma, tps)
    two_blocks = [normed_two, links.hop_tp(normed_two)]
    q_wide = jnp.zeros((query_weight.shape[0], depth), LOW)
    for hop, item in enumerate(q_blocks):
        q_wide = lax.dynamic_update_slice_in_dim(q_wide, item, links.at(hop) * q_cols, 1)
    if ctxs == 2:
        up_cores = [links.to_core(after(item, mixed)) for item in (up_mine, up_near)]
        up_cores.append(links.to_core(after(up_far, normed_two)))
        up_full = assemble(meta, up_mine, up_near, up_far, *up_cores)
    else:
        up_full = gather_whole(up_mine)
    q_full = lax.all_gather(after(q_wide, down_full), "fsdp", axis=0, tiled=True)

    two_blocks.append(links.hop_tp(after(two_blocks[-1], (gate_full, up_full, down_full))))
    two_blocks.append(links.hop_tp(two_blocks[-1]))
    kept, two_parts, mixed_parts, two_total = None, [], [], None
    for hop in range(tps):
        block = two_blocks[hop]
        if hop + 1 < tps:
            block = after(block, two_blocks[hop + 1])
        if two_total is not None:
            block = after(block, two_total)
        kept, two_part, mixed_part = feed(
            meta, block, cot_all, gate_full, up_full, down_full, hop, tps, kept
        )
        two_parts.append(two_part)
        mixed_parts.append(mixed_part)
        if hop >= 1:
            two_total = two_part if hop == 1 else add_low(two_part, two_got)
            two_got = links.hop_tp(two_total)
        two_total = two_total if hop >= 2 else None
    two_own = two_parts[0]
    act_all, gate_all, up_all = kept
    two_all = jnp.concatenate(two_blocks, axis=0)
    down_term = inner_rows(cot_all, after(act_all, two_total)).astype(LOW)
    two_got = after(two_got, down_term)

    hidden_grad, branch_grad, attended_grad, mlp_term = turn(
        meta, two_own, two_got, hidden, cotangent, o_parts, mlp_gamma, depth, tps
    )
    mixed_got = links.hop_tp(after(mixed_parts[1], two_got))
    q_grads, kv_parts, token = [], [], two_got
    for s in seqs:
        q_grad, grad_before, grad_own = attend_back(
            meta, s, queries, kv_before, kv_own, order, mixed, attended_grad, after(lse, token),
            cosine, sine, key_block, sizes,
        )
        q_grads.append(q_grad)
        if ctxs == 2:
            kv_parts.append((grad_own, lax.ppermute(grad_before, "ctx", [(1, 0)])))
        else:
            wide_grad = lax.dynamic_update_slice_in_dim(grad_before, grad_own, ctx * block_len, 2)
            kv_parts.append((lax.psum_scatter(wide_grad, "ctx", scatter_dimension=2, tiled=True), None))
        token = (mixed_got, q_grad)
    mixed_got = links.hop_tp(add_low(mixed_parts[2], after(mixed_got, q_grads[0])))
    q_grad = jnp.concatenate(q_grads, axis=0)
    shares = swap(lambda d: lax.dynamic_slice_in_dim(q_grad, d * q_cols, q_cols, 1))
    input_low, attn_term = finish(meta, q_grad, q_full, inputs, hidden_grad, attn_gamma, tps)
    output_pairs = links.pairs(inner_rows(mixed, after(branch_grad, q_grads[-1])).astype(LOW), 1)
    token = (mixed_got, input_low, kv_parts, shares, output_pairs)
    kv_parts = [
        mine if got is None else add_low(after(mine, token), got) for mine, got in kv_parts
    ]

    def kv_rows(hop):
        return jnp.stack(
            [
                lax.dynamic_slice_in_dim(kv_parts[s], place(s, links.at(hop)) * own, own, 2)
                for s in seqs
            ],
            axis=2,
        )

    def fsdp_rows(value, below):
        return jnp.concatenate(
            [item for j in range(fsdps) for item in (value[j * shard : (j + 1) * shard], below(j))], axis=0
        )

    def output_rows(hop):
        return lax.dynamic_slice_in_dim(output_part, links.at(hop) * q_cols, q_cols, 0)

    kv_mine, kv_next = kv_rows(0), kv_rows(1)
    mixed_next = add_low(mixed_parts[3], mixed_got)
    mixed_got = links.hop_tp(after(mixed_next, (shares, kv_next, input_low, output_pairs)))
    kv_got = links.hop_tp(kv_next)
    gate_term = inner_rows(two_all, after(gate_all, kv_next)).astype(LOW)
    down_weight_grad = links.reduce_weight(after(down_term, kv_next))
    kv_next = add_low(kv_rows(2), kv_got)

    in_blocks = [input_low, links.hop_tp(after(input_low, (mixed_got, kv_next, gate_term)))]
    kv_got = links.hop_tp(kv_next)
    gate_weight_grad = links.reduce_weight(after(gate_term, mixed_got)).T
    up_term = inner_rows(two_all, after(up_all, (mixed_got, gate_term))).astype(LOW)
    output_both = links.scatter_core(after(output_pairs, mixed_got))
    kv_next = add_low(kv_rows(3), kv_got)
    out_low = hidden + mixed_parts[0].astype(jnp.float32) + mixed_got.astype(jnp.float32)
    out_low = lax.optimization_barrier(out_low.astype(LOW))

    out_blocks = [out_low, links.hop_tp(after(out_low, (in_blocks[1], kv_next, up_term, output_both)))]
    kv_got = links.hop_tp(kv_next)
    up_weight_grad = links.reduce_weight(after(up_term, in_blocks[1])).T
    output_part = links.scatter_x(after(output_both, in_blocks[1]), 1)
    grads_all = after(jnp.concatenate(shares, axis=0), in_blocks[1])
    q_bias_row = jnp.sum(grads_all.astype(jnp.float32), axis=0, keepdims=True)
    q_below = jnp.pad(q_bias_row, ((0, 15), (0, 0))).astype(LOW)
    q_pairs = links.pairs(fsdp_rows(inner_rows(one_all, grads_all).astype(LOW), lambda j: q_below), 0)
    kv_grad, kv_term = kv_back(meta, kv_mine, kv_got, cosine, sine, qkv, inputs, tps)
    gain_terms = jnp.concatenate(
        [jnp.sum(attn_term, axis=0) + jnp.sum(kv_term, axis=0), jnp.sum(mlp_term, axis=0)], axis=1
    ).reshape(-1, kv_cols)
    gain_terms = jnp.pad(gain_terms, ((0, 16 - gain_terms.shape[0]), (0, 0))).astype(LOW)
    kv_blocks = [jnp.concatenate([kv_grad, gain_terms], axis=0)]

    in_blocks.append(links.hop_tp(after(in_blocks[1], (out_blocks[1], kv_blocks[0], q_pairs))))
    kv_blocks.append(links.hop_tp(kv_blocks[0]))
    q_both = links.scatter_core(after(q_pairs, out_blocks[1]))
    output_got = links.hop_tp(after(output_rows(1), out_blocks[1]))
    output_next = add_low(output_rows(2), output_got)

    out_blocks.append(
        links.hop_tp(
            after(out_blocks[1], (in_blocks[2], kv_blocks[1], q_both, output_next, down_weight_grad))
        )
    )
    kv_blocks.append(links.hop_tp(kv_blocks[1]))
    q_part = links.scatter_x(after(q_both, in_blocks[2]), 0)
    output_got = links.hop_tp(after(output_next, in_blocks[2]))
    output_next = add_low(output_rows(3), output_got)

    in_blocks.append(
        links.hop_tp(after(in_blocks[2], (out_blocks[2], kv_blocks[2], q_part, output_next)))
    )
    kv_blocks.append(links.hop_tp(kv_blocks[2]))
    q_total = links.sum_ctx(after(q_part, out_blocks[2]))
    output_got = links.hop_tp(after(output_next, out_blocks[2]))
    output_sum = add_low(output_rows(0), output_got)
    own_tokens = seq_count * own
    kv_all = jnp.concatenate([item[:own_tokens] for item in kv_blocks], axis=0)
    gain_rows = sum(
        item[own_tokens : own_tokens + 2 * width // kv_cols].astype(jnp.float32) for item in kv_blocks
    ).reshape(2, width)
    kv_bias_row = jnp.sum(kv_all.astype(jnp.float32), axis=0, keepdims=True)

    def kv_below(j):
        gains = jnp.pad(gain_rows[:, j * shard : (j + 1) * shard], ((0, 0), (0, kv_cols - shard)))
        return jnp.pad(jnp.concatenate([gains, kv_bias_row], axis=0), ((0, 13), (0, 0))).astype(LOW)

    kv_pairs = links.pairs(fsdp_rows(inner_rows(one_all, kv_all).astype(LOW), kv_below), 0)

    out_blocks.append(
        links.hop_tp(
            after(out_blocks[2], (in_blocks[3], kv_pairs, q_total, output_sum, gate_weight_grad))
        )
    )
    kv_both = links.scatter_core(after(kv_pairs, in_blocks[3]))
    output_weight_grad = links.sum_ctx(after(output_sum, in_blocks[3]))
    kv_part = links.scatter_x(kv_both, 0)
    in_blocks[0] = after(in_blocks[0], kv_both)
    input_grad = last(meta, in_blocks, kv_blocks, qkv, inputs, attn_gamma)
    out_blocks[0] = after(out_blocks[0], (kv_part, input_grad, up_weight_grad))
    kv_total = links.sum_ctx(kv_part)
    outputs = spread_out(meta, out_blocks, seq_count, LOW)
    query_weight_grad = q_total[:shard]
    part = head_dim // fsdps
    query_bias_grad = lax.dynamic_slice_in_dim(
        q_total[shard].reshape(local_heads, head_dim), fsdp * part, part, 1
    )
    kv_weight = kv_total[:shard]
    gains = kv_total[shard : shard + 2, :shard]
    kv_bias = kv_total[shard + 2].reshape(2, kv_heads, head_dim)
    kv_bias = lax.dynamic_slice_in_dim(kv_bias, fsdp * part, part, 2)
    half = kv_cols // 2

    return (
        outputs,
        input_grad,
        gains[0],
        query_weight_grad,
        query_bias_grad,
        kv_weight[:, :half],
        kv_bias[0],
        kv_weight[:, half:],
        kv_bias[1],
        output_weight_grad,
        gains[1],
        gate_weight_grad,
        up_weight_grad,
        down_weight_grad,
    )


def solution(mesh):
    in_specs = (
        P("fsdp", "ctx", None),
        P("fsdp", "ctx", None),
        P("fsdp", "ctx"),
        P("fsdp"),
        P("fsdp", "tp"),
        P("tp", "fsdp"),
        P("fsdp", None),
        P(None, "fsdp"),
        P("fsdp", None),
        P(None, "fsdp"),
        P("tp", "fsdp"),
        P("fsdp"),
        P("fsdp", "tp"),
        P("fsdp", "tp"),
        P("tp", "fsdp"),
    )
    out_specs = (
        P("fsdp", "ctx", None),
        P("fsdp", "ctx", None),
        P("fsdp"),
        P("fsdp", "tp"),
        P("tp", "fsdp"),
        P("fsdp", None),
        P(None, "fsdp"),
        P("fsdp", None),
        P(None, "fsdp"),
        P("tp", "fsdp"),
        P("fsdp"),
        P("fsdp", "tp"),
        P("fsdp", "tp"),
        P("tp", "fsdp"),
    )
    return jax.shard_map(local, mesh=mesh, in_specs=in_specs, out_specs=out_specs, check_vma=False)
```

```python
import functools
import math

import jax
import jax.numpy as jnp
from jax import lax
from jax.experimental import pallas as pl
from jax.experimental.pallas import tpu as pltpu
from jax.sharding import PartitionSpec as P

EPS = 1e-06
THETA = 1000000.0
LOG2E = 1.0 / math.log(2.0)
LOW = jnp.bfloat16
MASKED = -1e30
MIB = 1024 * 1024


def rope_tables(position, width):
    half = width // 2
    freqs = jnp.exp(jnp.arange(half, dtype=jnp.float32) * (-2.0 * math.log(THETA) / width))
    angle = position.astype(jnp.float32)[..., None] * freqs
    cosine, sine = jnp.cos(angle), jnp.sin(angle)
    return (
        jnp.concatenate([cosine, cosine], axis=-1),
        jnp.concatenate([-sine, sine], axis=-1),
    )


def dot(left, right):
    return jnp.dot(left, right, preferred_element_type=jnp.float32)


def inner_rows(left, right):
    return lax.dot_general(
        left, right, (((0,), (0,)), ((), ())), preferred_element_type=jnp.float32
    )


def inner_cols(left, right):
    return lax.dot_general(
        left, right, (((1,), (1,)), ((), ())), preferred_element_type=jnp.float32
    )


def add_low(left, right):
    return (left.astype(jnp.float32) + right.astype(jnp.float32)).astype(LOW)


def after(value, token):
    return lax.optimization_barrier((value, token))[0]


def root_of(values):
    return lax.rsqrt(jnp.mean(values * values, axis=-1, keepdims=True) + EPS)


FSDP, TP, CTX, BEFORE, PLACE = 0, 1, 2, 3, 4


def shard_at(meta, flip, size):
    return pl.multiple_of(jnp.bitwise_xor(meta[FSDP], flip) * size, size)


def tp_at(meta, hop, tps, size):
    return pl.multiple_of(lax.rem(meta[TP] + tps - hop, tps) * size, size)


def call(kernel, grid, in_specs, out_specs, out_shape, scratch=(), cost=None, name=None, vmem=48):
    return pl.pallas_call(
        kernel,
        grid_spec=pltpu.PrefetchScalarGridSpec(
            num_scalar_prefetch=1,
            grid=grid,
            in_specs=in_specs,
            out_specs=out_specs,
            scratch_shapes=list(scratch),
        ),
        out_shape=out_shape,
        compiler_params=pltpu.CompilerParams(vmem_limit_bytes=vmem * MIB),
        cost_estimate=cost,
        name=name,
    )


def whole(array):
    return pl.BlockSpec(array.shape, lambda *_: (0,) * array.ndim)


def shape(dims, kind):
    return jax.ShapeDtypeStruct(dims, kind)


def project_kernel(
    local_heads, kv_heads, head_dim, meta, x_ref, gain_ref, bias_ref, *refs
):
    weights, (cos_ref, sin_ref, n_ref, q_ref, kv_ref) = refs[:4], refs[4:]
    rows = x_ref.shape[1]
    size = n_ref.shape[1] // 4
    values = x_ref[...].reshape(rows, -1).astype(jnp.float32)
    n_ref[...] = (values * root_of(values) * gain_ref[...]).astype(LOW)
    lin = bias_ref[...]
    for flip, weight in enumerate(weights):
        lin = lin + dot(n_ref[:, pl.ds(shard_at(meta, flip, size), size)], weight[:size, :])
    cosine, sine = cos_ref[...], sin_ref[...]
    for head in range(local_heads + 2 * kv_heads):
        part = lin[:, head * head_dim : (head + 1) * head_dim]
        if head < local_heads + kv_heads:
            part = part * cosine + pltpu.roll(part, head_dim // 2, 1) * sine
        if head < local_heads:
            q_ref[0, :, head * head_dim : (head + 1) * head_dim] = part.astype(LOW)
        else:
            at = (head - local_heads) * head_dim
            kv_ref[:, at : at + head_dim] = part.astype(LOW)


def project(meta, inputs, gain, bias, weights, cosine, sine, sizes):
    seq_count, block_len, width = inputs.shape
    local_heads, kv_heads, head_dim, tps = sizes
    own = block_len // tps
    q_cols, kv_cols = local_heads * head_dim, 2 * kv_heads * head_dim

    def row(i, m):
        return (i, 0)

    def device(i, m):
        seq, place = i // tps, i % tps
        return jnp.where(seq % 2 == 0, place, tps - 1 - place), seq, 0

    tokens = seq_count * block_len
    return call(
        functools.partial(project_kernel, local_heads, kv_heads, head_dim),
        (seq_count * tps,),
        [
            pl.BlockSpec((1, own, width), lambda i, m: (i // tps, i % tps, 0)),
            whole(gain), whole(bias), *(whole(w) for w in weights),
            pl.BlockSpec((own, head_dim), row), pl.BlockSpec((own, head_dim), row),
        ],
        [
            pl.BlockSpec((own, width), row),
            pl.BlockSpec((1, own, q_cols), device),
            pl.BlockSpec((own, kv_cols), row),
        ],
        [
            shape((tokens, width), LOW),
            shape((tps, seq_count * own, q_cols), LOW),
            shape((tokens, kv_cols), LOW),
        ],
        cost=pl.CostEstimate(
            flops=2 * tokens * width * (q_cols + kv_cols), bytes_accessed=8 * tokens * width, transcendentals=0
        ),
        name="project",
    )(meta, inputs, gain, bias, *weights, cosine, sine)


def fwd_kernel(
    heads, block, parts, meta, *refs
):
    q_refs, (kb_ref, vb_ref, k_ref, v_ref, order_ref, o_ref, lse_ref, qg_ref, acc_ref, m_ref, l_ref) = (
        refs[:parts], refs[parts:]
    )
    own, cols = q_refs[0].shape[1:]
    head_dim = acc_ref.shape[0]
    scale = LOG2E / math.sqrt(head_dim)
    each = cols // head_dim
    for head in range(heads):
        qg_ref[head * own : (head + 1) * own, :] = q_refs[head // each][
            0, :, (head % each) * head_dim : (head % each + 1) * head_dim
        ]
    acc_ref[...] = jnp.zeros_like(acc_ref)
    m_ref[...] = jnp.full_like(m_ref, MASKED)
    l_ref[...] = jnp.zeros_like(l_ref)
    first = meta[PLACE + pl.program_id(0)] * own
    last = first // block

    def step(key_ref, value_ref, index, masked):
        start = pl.multiple_of(index * block, block)
        keys = key_ref[pl.ds(start, block), :]
        values = value_ref[pl.ds(start, block), :]
        logits = inner_cols(keys, qg_ref[...]) * scale
        if masked:
            key_order = (start - first) + lax.broadcasted_iota(jnp.int32, logits.shape, 0)
            logits = jnp.where(key_order <= order_ref[...], logits, MASKED)
        before = m_ref[...]
        peak = jnp.maximum(before, jnp.max(logits, axis=0, keepdims=True))
        weights = jnp.exp2(logits - peak)
        fade = jnp.exp2(before - peak)
        m_ref[...] = peak
        l_ref[...] = l_ref[...] * fade + jnp.sum(weights, axis=0, keepdims=True)
        acc_ref[...] = acc_ref[...] * fade + inner_rows(values, weights.astype(LOW))

    def early(index, carry):
        step(kb_ref, vb_ref, index, False)
        return carry

    def late(index, carry):
        step(k_ref, v_ref, index, False)
        return carry

    lax.fori_loop(0, meta[BEFORE], early, 0)
    lax.fori_loop(0, last, late, 0)
    step(k_ref, v_ref, last, True)
    total = l_ref[...]
    lse_ref[...] = (m_ref[...] + jnp.log2(total)).reshape(lse_ref.shape)
    mixed = jnp.transpose(acc_ref[...] / total)
    for head in range(heads):
        o_ref[:, head * head_dim : (head + 1) * head_dim] = mixed[
            head * own : (head + 1) * own, :
        ].astype(LOW)


def bwd_kernel(heads, block, parts, seq, meta, *refs):
    q_refs, (
        kb_ref, vb_ref, k_ref, v_ref, order_ref, o_ref, g_ref, lse_ref, cos_ref, sin_ref,
        dq_ref, db_ref, dd_ref, qg_ref, gg_ref, acc_ref,
    ) = refs[:parts], refs[parts:]
    own, cols = q_refs[0].shape[1:]
    head_dim = acc_ref.shape[1]
    scale = 1.0 / math.sqrt(head_dim)
    each = cols // head_dim
    for head in range(heads):
        rows = slice(head * own, (head + 1) * own)
        at = slice(head * head_dim, (head + 1) * head_dim)
        qg_ref[rows, :] = q_refs[head // each][
            0, :, (head % each) * head_dim : (head % each + 1) * head_dim
        ]
        gg_ref[rows, :] = g_ref[:, at]
        acc_ref[rows, :] = g_ref[:, at].astype(jnp.float32) * o_ref[:, at].astype(jnp.float32)
    center = jnp.sum(jnp.transpose(acc_ref[...]), axis=0, keepdims=True)
    acc_ref[...] = jnp.zeros_like(acc_ref)
    lse = lse_ref[...].reshape(order_ref.shape)
    first = meta[PLACE + seq] * own
    last = first // block

    def step(key_ref, value_ref, out_ref, index, masked):
        start = pl.multiple_of(index * block, block)
        keys = key_ref[pl.ds(start, block), :]
        values = value_ref[pl.ds(start, block), :]
        logits = inner_cols(keys, qg_ref[...]) * (scale * LOG2E)
        if masked:
            key_order = (start - first) + lax.broadcasted_iota(jnp.int32, logits.shape, 0)
            logits = jnp.where(key_order <= order_ref[...], logits, MASKED)
        probs = jnp.exp2(logits - lse)
        out_ref[1, 0, pl.ds(start, block), :] = dot(probs.astype(LOW), gg_ref[...]).astype(LOW)
        prob_grad = inner_cols(values, gg_ref[...])
        logit_grad = (probs * (prob_grad - center)).astype(LOW)
        out_ref[0, 0, pl.ds(start, block), :] = (dot(logit_grad, qg_ref[...]) * scale).astype(LOW)
        acc_ref[...] += inner_rows(logit_grad, keys)

    def early(index, carry):
        step(kb_ref, vb_ref, db_ref, index, False)
        return carry

    def late(index, carry):
        step(k_ref, v_ref, dd_ref, index, False)
        return carry

    def clear(ref):
        def body(index, carry):
            start = pl.multiple_of(index * block, block)
            ref[:, :, pl.ds(start, block), :] = jnp.zeros((2, 1, block, head_dim), LOW)
            return carry

        return body

    lax.fori_loop(0, meta[BEFORE], early, 0)
    lax.fori_loop(meta[BEFORE], kb_ref.shape[0] // block, clear(db_ref), 0)
    lax.fori_loop(0, last, late, 0)
    step(k_ref, v_ref, dd_ref, last, True)
    lax.fori_loop(last + 1, k_ref.shape[0] // block, clear(dd_ref), 0)
    for head in range(heads):
        grad = acc_ref[head * own : (head + 1) * own, :] * scale
        grad = grad * cos_ref[...] - pltpu.roll(grad, head_dim // 2, 1) * sin_ref[...]
        dq_ref[:, head * head_dim : (head + 1) * head_dim] = grad.astype(LOW)


def attention_specs(queries, kv_before, kv_own, sizes, seq=None):
    seq_count, kv_heads, head_dim, tps = sizes
    rows = queries.shape[1] // seq_count
    parts = tps // kv_heads
    heads = queries.shape[2] * parts // head_dim
    before, block_len = kv_before.shape[0] // seq_count, kv_own.shape[0] // seq_count

    def spec(dims, index):
        if seq is None:
            return pl.BlockSpec(dims, index)
        return pl.BlockSpec(dims, lambda g, m: index(seq, g, m))

    def piece(part):
        return spec(
            (1, rows, queries.shape[2]),
            lambda s, g, m: (lax.rem(m[TP] + tps - (g * parts + part), tps), s, 0),
        )

    specs = [piece(part) for part in range(parts)] + [
        spec((before, head_dim), lambda s, g, m: (s, g)),
        spec((before, head_dim), lambda s, g, m: (s, kv_heads + g)),
        spec((block_len, head_dim), lambda s, g, m: (s, g)),
        spec((block_len, head_dim), lambda s, g, m: (s, kv_heads + g)),
        spec((1, heads * rows), lambda s, g, m: (0, 0)),
    ]
    return specs, rows, parts, heads, before, block_len


def attend(meta, queries, kv_before, kv_own, order, block, sizes):
    seq_count, kv_heads, head_dim, tps = sizes
    specs, rows, parts, heads, before, block_len = attention_specs(queries, kv_before, kv_own, sizes)
    width, wide = kv_heads * heads * head_dim, heads * rows
    work = seq_count * rows * width * (before + block_len)
    return call(
        functools.partial(fwd_kernel, heads, block, parts),
        (seq_count, kv_heads),
        specs,
        [
            pl.BlockSpec((rows, heads * head_dim), lambda s, g, m: (s, g)),
            pl.BlockSpec((1, 1, 1, wide), lambda s, g, m: (s, g, 0, 0)),
        ],
        [shape((seq_count * rows, width), LOW), shape((seq_count, kv_heads, 1, wide), jnp.float32)],
        [
            pltpu.VMEM((wide, head_dim), LOW),
            pltpu.VMEM((head_dim, wide), jnp.float32),
            pltpu.VMEM((1, wide), jnp.float32),
            pltpu.VMEM((1, wide), jnp.float32),
        ],
        cost=pl.CostEstimate(flops=8 * work, bytes_accessed=1 << 22, transcendentals=0),
        name="attend",
    )(meta, *([queries] * parts), kv_before, kv_before, kv_own, kv_own, order)


def attend_back(
    meta, seq, queries, kv_before, kv_own, order, mixed, grads, lse, cosine, sine, block, sizes
):
    seq_count, kv_heads, head_dim, tps = sizes
    specs, rows, parts, heads, before, block_len = attention_specs(
        queries, kv_before, kv_own, sizes, seq
    )
    width, wide = kv_heads * heads * head_dim, heads * rows
    work = rows * width * (before + block_len)
    wide_spec = pl.BlockSpec((rows, heads * head_dim), lambda g, m: (seq, g))
    table_spec = pl.BlockSpec((rows, head_dim), lambda g, m: (seq * tps + m[PLACE + seq], 0))
    return call(
        functools.partial(bwd_kernel, heads, block, parts, seq),
        (kv_heads,),
        specs
        + [
            wide_spec,
            wide_spec,
            pl.BlockSpec((1, 1, 1, wide), lambda g, m: (seq, g, 0, 0)),
            table_spec,
            table_spec,
        ],
        [
            pl.BlockSpec((rows, heads * head_dim), lambda g, m: (0, g)),
            pl.BlockSpec((2, 1, before, head_dim), lambda g, m: (0, g, 0, 0)),
            pl.BlockSpec((2, 1, block_len, head_dim), lambda g, m: (0, g, 0, 0)),
        ],
        [
            shape((rows, width), LOW),
            shape((2, kv_heads, before, head_dim), LOW),
            shape((2, kv_heads, block_len, head_dim), LOW),
        ],
        [
            pltpu.VMEM((wide, head_dim), LOW),
            pltpu.VMEM((wide, head_dim), LOW),
            pltpu.VMEM((wide, head_dim), jnp.float32),
        ],
        cost=pl.CostEstimate(flops=16 * work, bytes_accessed=1 << 22, transcendentals=0),
        name="attend_back",
    )(
        meta, *([queries] * parts), kv_before, kv_before, kv_own, kv_own, order,
        mixed, grads, lse, cosine, sine,
    )


def output_pieces(meta, weights, tps):
    own, other, near, far, other_near, other_far = weights
    depth, half = own.shape[0], near.shape[0]
    low = pl.multiple_of(meta[CTX] * (depth - half), 128)
    high = pl.multiple_of((1 - meta[CTX]) * (depth - half), 128)
    pieces = [(0, None, own), (1, None, other)]
    if half == depth:
        return pieces + [(2, None, near), (3, None, other_near)]
    return pieces + [(2, low, near), (2, high, far), (3, low, other_near), (3, high, other_far)]


def merge_kernel(tps, meta, o_ref, x_ref, *refs):
    weights, (gain_ref, h_ref, n_ref, turned_ref) = refs[:6], refs[6:]
    rows, width = h_ref.shape
    size, depth = width // 4, o_ref.shape[1]
    part = depth // tps
    for hop in range(tps):
        turned_ref[:, hop * part : (hop + 1) * part] = o_ref[:, pl.ds(tp_at(meta, hop, tps, part), part)]
    h_ref[...] = x_ref[...].reshape(rows, width).astype(jnp.float32)
    for flip, first, weight in output_pieces(meta, weights, tps):
        left = turned_ref[...] if first is None else turned_ref[:, pl.ds(first, weight.shape[0])]
        h_ref[:, pl.ds(shard_at(meta, flip, size), size)] += dot(left, weight[...])
    hidden = h_ref[...]
    n_ref[...] = (hidden * root_of(hidden) * gain_ref[...]).astype(LOW)


def merge(meta, mixed, inputs, weights, gain, tps):
    seq_count, block_len, width = inputs.shape
    own = block_len // tps
    depth = mixed.shape[1]
    row = pl.BlockSpec((own, width), lambda s, m: (s, 0))
    return call(
        functools.partial(merge_kernel, tps),
        (seq_count,),
        [
            pl.BlockSpec((own, depth), lambda s, m: (s, 0)),
            pl.BlockSpec((1, own, width), lambda s, m: (s, m[PLACE + s], 0)),
            *(whole(w) for w in weights),
            whole(gain),
        ],
        [row, row],
        [shape((seq_count * own, width), jnp.float32), shape((seq_count * own, width), LOW)],
        [pltpu.VMEM((own, depth), LOW)],
        cost=pl.CostEstimate(
            flops=2 * seq_count * own * depth * width, bytes_accessed=1 << 23, transcendentals=0
        ),
        name="merge",
    )(meta, mixed, inputs, *weights, gain)


def turn_kernel(
    tps, meta, a_ref, b_ref, h_ref, c_ref, *refs,
):
    weights, (gain_ref, hg_ref, bg_ref, ag_ref, term_ref, turned_ref) = refs[:6], refs[6:]
    rows, width = h_ref.shape
    size, depth = width // 4, ag_ref.shape[1]
    two_grad = a_ref[...].astype(jnp.float32) + b_ref[...].astype(jnp.float32)
    hidden = h_ref[...]
    root = root_of(hidden)
    term_ref[...] = jnp.sum(two_grad * hidden * root, axis=0, keepdims=True).reshape(term_ref.shape)
    scaled = gain_ref[...] * two_grad
    grad = (
        c_ref[...].reshape(rows, width).astype(jnp.float32)
        + root * scaled
        - hidden * root**3 * jnp.mean(scaled * hidden, axis=-1, keepdims=True)
    )
    hg_ref[...] = grad
    bg_ref[...] = grad.astype(LOW)
    turned_ref[...] = jnp.zeros_like(turned_ref)
    for flip, first, weight in output_pieces(meta, weights, tps):
        at = slice(None) if first is None else pl.ds(first, weight.shape[0])
        turned_ref[:, at] += inner_cols(bg_ref[:, pl.ds(shard_at(meta, flip, size), size)], weight[...])
    part = depth // tps
    for hop in range(tps):
        ag_ref[:, pl.ds(tp_at(meta, hop, tps, part), part)] = turned_ref[
            :, hop * part : (hop + 1) * part
        ].astype(LOW)


def turn(meta, two_own, two_got, hidden, cotangent, weights, gain, depth, tps):
    seq_count, block_len, width = cotangent.shape
    own = block_len // tps
    row = pl.BlockSpec((own, width), lambda s, m: (s, 0))
    tokens = seq_count * own
    return call(
        functools.partial(turn_kernel, tps),
        (seq_count,),
        [
            row, row, row,
            pl.BlockSpec((1, own, width), lambda s, m: (s, m[PLACE + s], 0)),
            *(whole(w) for w in weights),
            whole(gain),
        ],
        [
            row, row,
            pl.BlockSpec((own, depth), lambda s, m: (s, 0)),
            pl.BlockSpec((1, 1, width), lambda s, m: (s, 0, 0)),
        ],
        [
            shape((tokens, width), jnp.float32),
            shape((tokens, width), LOW),
            shape((tokens, depth), LOW),
            shape((seq_count, 1, width), jnp.float32),
        ],
        [pltpu.VMEM((own, depth), jnp.float32)],
        cost=pl.CostEstimate(flops=2 * tokens * depth * width, bytes_accessed=1 << 23, transcendentals=0),
        name="turn",
    )(meta, two_own, two_got, hidden, cotangent, *weights, gain)


def back_through_norm(grad, values, gain):
    root = root_of(values)
    scaled = gain * grad
    term = jnp.sum(grad * values * root, axis=0, keepdims=True)
    return root * scaled - values * root**3 * jnp.mean(scaled * values, axis=-1, keepdims=True), term


def finish_kernel(meta, g_ref, q_ref, x_ref, hg_ref, gain_ref, out_ref, term_ref):
    values = x_ref[...].reshape(hg_ref.shape).astype(jnp.float32)
    part, term = back_through_norm(inner_cols(g_ref[...], q_ref[...]), values, gain_ref[...])
    term_ref[...] = term.reshape(term_ref.shape)
    out_ref[...] = (hg_ref[...] + part).astype(LOW)


def finish(meta, q_grad, q_full, inputs, hidden_grad, gain, tps):
    seq_count, block_len, width = inputs.shape
    own = block_len // tps
    tokens = seq_count * own
    row = pl.BlockSpec((own, width), lambda s, m: (s, 0))
    return call(
        finish_kernel,
        (seq_count,),
        [
            pl.BlockSpec((own, q_grad.shape[1]), lambda s, m: (s, 0)),
            whole(q_full),
            pl.BlockSpec((1, own, width), lambda s, m: (s, m[PLACE + s], 0)),
            row,
            whole(gain),
        ],
        [row, pl.BlockSpec((1, 1, width), lambda s, m: (s, 0, 0))],
        [shape((tokens, width), LOW), shape((seq_count, 1, width), jnp.float32)],
        cost=pl.CostEstimate(
            flops=2 * tokens * q_grad.shape[1] * width, bytes_accessed=1 << 23, transcendentals=0
        ),
        name="finish",
    )(meta, q_grad, q_full, inputs, hidden_grad, gain)


def one_from_kv(meta, kv_grad, weights, one_ref):
    size = one_ref.shape[1] // 4
    skip = weights[0].shape[1] - kv_grad.shape[1]
    for flip, weight in enumerate(weights):
        one_ref[:, pl.ds(shard_at(meta, flip, size), size)] = inner_cols(
            kv_grad, weight[:size, skip:]
        )
    return one_ref[...]


def kv_kernel(kv_heads, head_dim, meta, a_ref, b_ref, cos_ref, sin_ref, *refs):
    weights, (x_ref, kv_ref, term_ref, one_ref) = refs[:4], refs[4:]
    cosine, sine = cos_ref[...], sin_ref[...]
    for kind in range(2):
        for head in range(kv_heads):
            grad = (
                a_ref[kind, head, 0].astype(jnp.float32) + b_ref[kind, head, 0].astype(jnp.float32)
            )
            if kind == 0:
                grad = grad * cosine - pltpu.roll(grad, head_dim // 2, 1) * sine
            at = (kind * kv_heads + head) * head_dim
            kv_ref[:, at : at + head_dim] = grad.astype(LOW)
    one = one_from_kv(meta, kv_ref[...], weights, one_ref)
    values = x_ref[...].reshape(one.shape).astype(jnp.float32)
    term = jnp.sum(one * values * root_of(values), axis=0, keepdims=True)
    term_ref[...] = term.reshape(term_ref.shape)


def kv_back(meta, kv_mine, kv_got, cosine, sine, weights, inputs, tps):
    seq_count, block_len, width = inputs.shape
    own = block_len // tps
    kv_heads, head_dim = kv_mine.shape[1], kv_mine.shape[4]
    kv_cols = 2 * kv_heads * head_dim
    kv_spec = pl.BlockSpec((2, kv_heads, 1, own, head_dim), lambda s, m: (0, 0, s, 0, 0))
    table_spec = pl.BlockSpec((own, head_dim), lambda s, m: (s * tps + m[PLACE + s], 0))
    return call(
        functools.partial(kv_kernel, kv_heads, head_dim),
        (seq_count,),
        [
            kv_spec, kv_spec, table_spec, table_spec,
            *(whole(w) for w in weights),
            pl.BlockSpec((1, own, width), lambda s, m: (s, m[PLACE + s], 0)),
        ],
        [
            pl.BlockSpec((own, kv_cols), lambda s, m: (s, 0)),
            pl.BlockSpec((1, 1, width), lambda s, m: (s, 0, 0)),
        ],
        [shape((seq_count * own, kv_cols), LOW), shape((seq_count, 1, width), jnp.float32)],
        [pltpu.VMEM((own, width), jnp.float32)],
        cost=pl.CostEstimate(
            flops=2 * seq_count * own * kv_cols * width, bytes_accessed=1 << 22, transcendentals=0
        ),
        name="kv_back",
    )(meta, kv_mine, kv_got, cosine, sine, *weights, inputs)


def last_kernel(tps, meta, *refs):
    blocks, kvs, weights = refs[:tps], refs[tps : 2 * tps], refs[2 * tps : 2 * tps + 4]
    x_ref, gain_ref, out_ref, one_ref = refs[2 * tps + 4 :]
    seq = pl.program_id(0)
    own = blocks[0].shape[0]
    for hop in range(tps):
        device = lax.rem(meta[TP] + tps - hop, tps)
        place = jnp.where(seq % 2 == 0, device, tps - 1 - device)
        at = pl.ds(pl.multiple_of(place * own, own), own)
        one = one_from_kv(meta, kvs[hop][...], weights, one_ref)
        values = x_ref[0, at, :].astype(jnp.float32)
        part, _ = back_through_norm(one, values, gain_ref[...])
        out_ref[0, at, :] = blocks[hop][...].astype(jnp.float32) + part


def last(meta, blocks, kvs, weights, inputs, gain):
    seq_count, block_len, width = inputs.shape
    tps = len(blocks)
    own = block_len // tps
    every = pl.BlockSpec((1, block_len, width), lambda s, m: (s, 0, 0))
    return call(
        functools.partial(last_kernel, tps),
        (seq_count,),
        [pl.BlockSpec((own, width), lambda s, m: (s, 0))] * tps
        + [pl.BlockSpec((own, kvs[0].shape[1]), lambda s, m: (s, 0))] * tps
        + [whole(w) for w in weights]
        + [every, whole(gain)],
        every,
        shape(inputs.shape, jnp.float32),
        [pltpu.VMEM((own, width), jnp.float32)],
        cost=pl.CostEstimate(
            flops=2 * seq_count * block_len * kvs[0].shape[1] * width, bytes_accessed=1 << 24, transcendentals=0
        ),
        name="last",
    )(meta, *blocks, *kvs, *weights, inputs, gain)


def feed_kernel(first, hidden, *refs):
    n_ref, c_ref, wg_ref, wu_ref, wd_ref = refs[1:6]
    act_ref, gg_ref, ug_ref, two_ref, mix_ref, two_acc, mix_acc = refs[6 if first else 9 :]
    step, tile = pl.program_id(0), wg_ref.shape[0]
    steps = -(-hidden // tile)

    def body(count):
        gate = inner_cols(n_ref[...], wg_ref[:count, :])
        up_part = inner_cols(n_ref[...], wu_ref[:count, :])
        act_grad = inner_cols(c_ref[...], wd_ref[:count, :])
        sigma = jax.nn.sigmoid(gate)
        silu = gate * sigma
        act = (silu * up_part).astype(LOW)
        gate_grad = (act_grad * up_part * (sigma * (1.0 + gate * (1.0 - sigma)))).astype(LOW)
        up_grad = (act_grad * silu).astype(LOW)
        act_ref[:, :count], gg_ref[:, :count], ug_ref[:, :count] = act, gate_grad, up_grad
        return (
            dot(gate_grad, wg_ref[:count, :]) + dot(up_grad, wu_ref[:count, :]),
            dot(act, wd_ref[:count, :]),
        )

    @pl.when(step == 0)
    def _():
        two_acc[...], mix_acc[...] = body(tile)

    @pl.when(jnp.logical_and(step > 0, step < steps - 1))
    def _():
        two, mix = body(tile)
        two_acc[...] += two
        mix_acc[...] += mix

    @pl.when(step == steps - 1)
    def _():
        two, mix = body(hidden - (steps - 1) * tile)
        two_ref[...] = (two_acc[...] + two).astype(LOW)
        mix_ref[...] = (mix_acc[...] + mix).astype(LOW)


def feed(meta, normed, cots, gate_down, up, hop, tps, kept):
    rows, width = normed.shape
    hidden = up.shape[1]
    tile = 768
    assert hidden > tile
    gate_spec = pl.BlockSpec((None, tile, width), lambda j, m: (0, j, 0))
    down_spec = pl.BlockSpec((None, tile, width), lambda j, m: (1, j, 0))
    column = pl.BlockSpec((rows, tile), lambda j, m: (hop, j))
    fixed = pl.BlockSpec((rows, width), lambda j, m: (0, 0))
    first = hop == 0
    wide = shape((tps * rows, hidden), LOW)
    *hiddens, two_part, mixed_part = pl.pallas_call(
        functools.partial(feed_kernel, first, hidden),
        grid_spec=pltpu.PrefetchScalarGridSpec(
            num_scalar_prefetch=1,
            grid=(-(-hidden // tile),),
            in_specs=[fixed, pl.BlockSpec((rows, width), lambda j, m: (hop, 0)), gate_spec, gate_spec, down_spec]
            + ([] if first else [pl.BlockSpec(memory_space=pl.ANY)] * 3),
            out_specs=[column, column, column, fixed, fixed],
            scratch_shapes=[pltpu.VMEM((rows, width), jnp.float32)] * 2,
        ),
        out_shape=[wide, wide, wide, shape((rows, width), LOW), shape((rows, width), LOW)],
        input_output_aliases={} if first else {6: 0, 7: 1, 8: 2},
        compiler_params=pltpu.CompilerParams(vmem_limit_bytes=56 * MIB),
        cost_estimate=pl.CostEstimate(
            flops=12 * rows * width * hidden, bytes_accessed=6 * width * hidden, transcendentals=rows * hidden
        ),
        name="feed",
    )(meta, normed, cots, gate_down, up, gate_down, *(() if first else kept))
    return hiddens, two_part, mixed_part


def assemble_kernel(tiles, meta, own_ref, near_ref, far_ref, o_own_ref, o_near_ref, o_far_ref, out_ref):
    size = own_ref.shape[1]
    is_near = (pl.program_id(0) // tiles) == meta[CTX]
    out_ref[:, pl.ds(shard_at(meta, 0, size), size)] = own_ref[...]
    out_ref[:, pl.ds(shard_at(meta, 1, size), size)] = o_own_ref[...]

    @pl.when(is_near)
    def _():
        out_ref[:, pl.ds(shard_at(meta, 2, size), size)] = near_ref[...]
        out_ref[:, pl.ds(shard_at(meta, 3, size), size)] = o_near_ref[...]

    @pl.when(jnp.logical_not(is_near))
    def _():
        out_ref[:, pl.ds(shard_at(meta, 2, size), size)] = far_ref[...]
        out_ref[:, pl.ds(shard_at(meta, 3, size), size)] = o_far_ref[...]


def assemble(meta, own, near, far, other, other_near, other_far):
    rows, size = own.shape
    tiles = 2 if rows % 64 == 0 else 1
    tile = rows // (2 * tiles)
    every = pl.BlockSpec((tile, size), lambda i, m: (i, 0))
    half = pl.BlockSpec((tile, size), lambda i, m: (i % tiles, 0))
    return call(
        functools.partial(assemble_kernel, tiles),
        (2 * tiles,),
        [every, half, half, every, half, half],
        pl.BlockSpec((tile, 4 * size), lambda i, m: (i, 0)),
        shape((rows, 4 * size), LOW),
        cost=pl.CostEstimate(flops=0, bytes_accessed=16 * rows * size, transcendentals=0),
        name="assemble",
    )(meta, own, near, far, other, other_near, other_far)


def lay_kernel(low_ref, high_ref, out_ref):
    both = jnp.concatenate([low_ref[...], high_ref[...]], axis=0)
    out_ref[...] = jnp.transpose(both.astype(jnp.float32))


def lay(low, high):
    rows, cols = low.shape
    return pl.pallas_call(
        lay_kernel,
        in_specs=[pl.BlockSpec(memory_space=pltpu.VMEM)] * 2,
        out_specs=pl.BlockSpec(memory_space=pltpu.VMEM),
        out_shape=shape((cols, 2 * rows), jnp.float32),
        compiler_params=pltpu.CompilerParams(vmem_limit_bytes=48 * MIB),
        cost_estimate=pl.CostEstimate(flops=0, bytes_accessed=12 * rows * cols, transcendentals=0),
        name="lay",
    )(low, high)


def spread_kernel(tps, meta, *refs):
    out_ref = refs[tps]
    seq_count = out_ref.shape[0]
    own = refs[0].shape[0] // seq_count
    for hop in range(tps):
        device = lax.rem(meta[TP] + tps - hop, tps)
        for s in range(seq_count):
            place = device if s % 2 == 0 else tps - 1 - device
            at = pl.ds(pl.multiple_of(place * own, own), own)
            out_ref[s, at, :] = refs[hop][s * own : (s + 1) * own, :].astype(out_ref.dtype)


def spread_out(meta, blocks, seq_count, kind):
    tps = len(blocks)
    rows, width = blocks[0].shape
    dims = (seq_count, rows // seq_count * tps, width)
    return call(
        functools.partial(spread_kernel, tps),
        (1,),
        [whole(item) for item in blocks],
        pl.BlockSpec(dims, lambda *_: (0, 0, 0)),
        shape(dims, kind),
        cost=pl.CostEstimate(flops=0, bytes_accessed=8 * rows * tps * width, transcendentals=0),
        name="spread",
    )(meta, *blocks)


class Links:
    def __init__(self):
        self.tp, self.ctx, self.fsdp = (lax.axis_index(a) for a in ("tp", "ctx", "fsdp"))
        self.tps, self.ctxs, self.fsdps = (lax.axis_size(a) for a in ("tp", "ctx", "fsdp"))
        self.core, self.x = self.fsdp % 2, self.fsdp // 2
        assert self.fsdps == 4

    def to_core(self, value):
        return lax.ppermute(value, "fsdp", [(0, 1), (1, 0), (2, 3), (3, 2)])

    def to_x(self, value):
        return lax.ppermute(value, "fsdp", [(0, 2), (2, 0), (1, 3), (3, 1)])

    def to_y(self, value):
        return lax.ppermute(value, "ctx", [(0, 1), (1, 0)])

    def hop_tp(self, value, hop=1):
        return lax.ppermute(value, "tp", [(i, (i + hop) % self.tps) for i in range(self.tps)])

    def gather_fsdp(self, shard):
        across = self.to_x(shard)
        return shard, across, self.to_core(jnp.concatenate([shard, across], axis=0))

    def gather_tp(self, block):
        blocks = [block]
        for _ in range(1, self.tps):
            blocks.append(self.hop_tp(blocks[-1]))
        return blocks

    def scatter_tp(self, blocks):
        total = blocks[1]
        for hop in range(1, self.tps):
            got = self.hop_tp(total)
            if hop < self.tps - 1:
                total = add_low(blocks[hop + 1], got)
        return blocks[0], got

    def at(self, hop):
        return (self.tp - hop + self.tps) % self.tps

    def pairs(self, value, axis):
        size = value.shape[axis] // 4

        def pair(core):
            return jnp.concatenate(
                [
                    lax.dynamic_slice_in_dim(value, (2 * x + core) * size, size, axis)
                    for x in range(2)
                ],
                axis,
            )

        return pair(self.core), pair(1 - self.core)

    def scatter_core(self, pairs):
        return add_low(pairs[0], self.to_core(pairs[1]))

    def scatter_x(self, both, axis):
        size = both.shape[axis] // 2
        away = lax.dynamic_slice_in_dim(both, (1 - self.x) * size, size, axis)
        keep = lax.dynamic_slice_in_dim(both, self.x * size, size, axis)
        return add_low(keep, self.to_x(away))

    def sum_ctx(self, value):
        value = lax.optimization_barrier(value.astype(LOW))
        if self.ctxs == 2:
            return value.astype(jnp.float32) + self.to_y(value).astype(jnp.float32)
        return lax.psum(value.astype(jnp.float32), "ctx")

    def reduce_weight(self, term):
        part = lax.psum_scatter(term, ("fsdp", "ctx"), scatter_dimension=0, tiled=True)
        if self.ctxs != 2:
            return lax.all_gather(part, "ctx", axis=0, tiled=True), None
        part = lax.optimization_barrier(part)
        return part, self.to_y(part)

    def lay_weight(self, part, got):
        if got is None:
            return part.astype(jnp.float32).T
        return lay(jnp.where(self.ctx == 0, part, got), jnp.where(self.ctx == 0, got, part))


def local(
    inputs,
    cotangent,
    positions,
    attn_gain,
    query_weight,
    query_bias,
    key_weight,
    key_bias,
    value_weight,
    value_bias,
    output_weight,
    mlp_gain,
    gate_weight,
    up_weight,
    down_weight,
):
    links = Links()
    seq_count, block_len, width = inputs.shape
    tp, tps, ctx, ctxs = links.tp, links.tps, links.ctx, links.ctxs
    fsdp, fsdps = links.fsdp, links.fsdps
    own = block_len // tps
    local_heads, kv_heads = query_bias.shape[0], key_bias.shape[0]
    head_dim = key_weight.shape[1] // kv_heads
    q_cols = local_heads * head_dim
    kv_cols = 2 * kv_heads * head_dim
    depth = q_cols * tps
    shard = width // fsdps
    tokens = seq_count * block_len
    key_block = block_len // 2 if block_len % (2 * own) == 0 else block_len
    seqs = range(seq_count)

    def place(seq, device):
        return device if seq % 2 == 0 else tps - 1 - device

    def block_rows(value, hop):
        return jnp.concatenate(
            [
                lax.dynamic_slice_in_dim(value[s], place(s, links.at(hop)) * own, own, 0)
                for s in seqs
            ],
            axis=0,
        )

    meta = jnp.stack(
        [fsdp, tp, ctx, ctx * (block_len // key_block)] + [place(s, tp) for s in seqs]
    ).astype(jnp.int32)

    lanes = q_cols + kv_cols
    smalls = jnp.concatenate([b.reshape(-1) for b in (query_bias, key_bias, value_bias)])
    extra = jnp.stack(
        [jnp.pad(row, (0, lanes - row.shape[0])) for row in (attn_gain, mlp_gain, smalls)]
    )
    extra = jnp.pad(extra, ((0, 13), (0, 0)))
    pack = jnp.concatenate(
        [jnp.concatenate([query_weight, key_weight, value_weight], axis=1), extra], axis=0
    )
    pack_core, pack_across = links.to_core(pack), links.to_x(pack)
    qkv = pack, pack_core, pack_across, links.to_core(pack_across)
    o_blocks = links.gather_tp(output_weight)
    up_mine = up_weight.T

    rows = jnp.stack([item[shard : shard + 3] for item in qkv])
    rows = [
        lax.dynamic_index_in_dim(rows, jnp.bitwise_xor(fsdp, j), 0, keepdims=False) for j in range(4)
    ]
    attn_gamma = jnp.concatenate([r[0, :shard] for r in rows])[None].astype(jnp.float32)
    mlp_gamma = jnp.concatenate([r[1, :shard] for r in rows])[None].astype(jnp.float32)
    bias = jnp.concatenate(
        [r[2, : smalls.shape[0]].reshape(-1, head_dim // fsdps) for r in rows], axis=1
    ).reshape(1, lanes).astype(jnp.float32)
    bias = after(bias, o_blocks[1])

    cosine, sine = rope_tables(positions.reshape(tokens), head_dim)
    normed_one, query_blocks, kv_own = project(
        meta, inputs, attn_gamma, bias, qkv, cosine, sine, (local_heads, kv_heads, head_dim, tps)
    )
    if ctxs == 2:
        kv_before = lax.ppermute(kv_own, "ctx", [(0, 1)])
        half = up_mine.shape[0] // 2
        up_near = links.to_x(
            after(lax.dynamic_slice_in_dim(up_mine, ctx * half, half, 0), pack_across)
        )
        up_far = links.to_y(after(up_near, kv_before))
    else:
        kv_before = lax.all_gather(
            kv_own.reshape(seq_count, block_len, kv_cols), "ctx", axis=1, tiled=True
        ).reshape(seq_count * block_len * ctxs, kv_cols)

    def swap(block_of):
        return [block_of(tp)] + [
            links.hop_tp(block_of((tp + hop) % tps), hop) for hop in range(1, tps)
        ]

    queries = jnp.stack(swap(lambda d: lax.dynamic_index_in_dim(query_blocks, d, 0, keepdims=False)))

    def gather_whole(*items):
        return lax.all_gather(after(jnp.stack(items), pack_across), "fsdp", axis=2, tiled=True)

    gate_down = gather_whole(gate_weight.T, down_weight)
    o_blocks = o_blocks[:2] + [after(item, kv_own) for item in o_blocks[2:]]
    o_wide = jnp.concatenate(o_blocks, axis=0)
    q_blocks = links.gather_tp(after(query_weight, kv_own))
    if ctxs == 2:
        o_near = links.to_x(lax.dynamic_slice_in_dim(o_wide, ctx * (depth // 2), depth // 2, 0))
        o_far = links.to_y(after(o_near, kv_before))
    else:
        o_near = o_far = links.to_x(o_wide)
    o_core = links.to_core(after(o_wide, queries))

    late_cot = after(cotangent, kv_own)
    cot_all = jnp.concatenate([block_rows(late_cot, hop) for hop in range(tps)], axis=0)
    one_all = jnp.concatenate(
        [block_rows(normed_one.reshape(seq_count, block_len, width), hop) for hop in range(tps)], axis=0
    )

    order = jnp.tile(jnp.arange(own, dtype=jnp.int32), depth // head_dim // kv_heads)[None]
    order = after(order, (cot_all, one_all, q_blocks[2], *([up_near] if ctxs == 2 else [])))
    sizes = (seq_count, kv_heads, head_dim, tps)
    mixed, lse = attend(meta, queries, kv_before, kv_own, order, key_block, sizes)
    o_core_near, o_core_far = (
        links.to_core(after(item, (mixed, q_blocks[-1]))) for item in (o_near, o_far)
    )
    o_parts = (o_wide, o_core, o_near, o_far, o_core_near, o_core_far)
    hidden, normed_two = merge(meta, mixed, inputs, o_parts, mlp_gamma, tps)
    two_blocks = [normed_two, links.hop_tp(normed_two)]
    if ctxs == 2:
        up_cores = [links.to_core(after(item, mixed)) for item in (up_mine, up_near)]
        up_cores.append(links.to_core(after(up_far, normed_two)))
        up_full = assemble(meta, up_mine, up_near, up_far, *up_cores)[None]
    else:
        up_full = gather_whole(up_mine)

    two_blocks.append(links.hop_tp(after(two_blocks[-1], (gate_down, up_full))))
    two_blocks.append(links.hop_tp(two_blocks[-1]))
    kept, two_parts, mixed_parts, two_total = None, [], [], None
    for hop in range(tps):
        block = two_blocks[hop]
        if hop + 1 < tps:
            block = after(block, two_blocks[hop + 1])
        if two_total is not None:
            block = after(block, two_total)
        kept, two_part, mixed_part = feed(
            meta, block, cot_all, gate_down, up_full, hop, tps, kept
        )
        two_parts.append(two_part)
        mixed_parts.append(mixed_part)
        if hop == 0:
            q_wide = jnp.zeros((query_weight.shape[0], depth), LOW)
            for back, item in enumerate(q_blocks):
                q_wide = lax.dynamic_update_slice_in_dim(q_wide, item, links.at(back) * q_cols, 1)
            q_full = lax.all_gather(q_wide, "fsdp", axis=0, tiled=True)
        if hop >= 1:
            two_total = two_part if hop == 1 else add_low(two_part, two_got)
            two_got = links.hop_tp(two_total)
        two_total = two_total if hop >= 2 else None
    two_own = two_parts[0]
    act_all, gate_all, up_all = kept
    two_all = jnp.concatenate(two_blocks, axis=0)
    down_term = inner_rows(cot_all, after(act_all, two_total)).astype(LOW)
    two_got = after(two_got, (down_term, two_all))

    hidden_grad, branch_grad, attended_grad, mlp_term = turn(
        meta, two_own, two_got, hidden, cotangent, o_parts, mlp_gamma, depth, tps
    )
    mixed_got = links.hop_tp(after(mixed_parts[1], two_got))
    q_grads, kv_parts, token = [], [], two_got
    for s in seqs:
        q_grad, grad_before, grad_own = attend_back(
            meta, s, queries, kv_before, kv_own, order, mixed, attended_grad, after(lse, token),
            cosine, sine, key_block, sizes,
        )
        q_grads.append(q_grad)
        if ctxs == 2:
            kv_parts.append((grad_own, lax.ppermute(grad_before, "ctx", [(1, 0)])))
        else:
            wide_grad = lax.dynamic_update_slice_in_dim(grad_before, grad_own, ctx * block_len, 2)
            kv_parts.append((lax.psum_scatter(wide_grad, "ctx", scatter_dimension=2, tiled=True), None))
        token = (mixed_got, q_grad)
    mixed_got = links.hop_tp(add_low(mixed_parts[2], after(mixed_got, q_grads[0])))
    q_grad = jnp.concatenate(q_grads, axis=0)
    shares = swap(lambda d: lax.dynamic_slice_in_dim(q_grad, d * q_cols, q_cols, 1))
    input_low, attn_term = finish(meta, q_grad, q_full, inputs, hidden_grad, attn_gamma, tps)
    output_pairs = links.pairs(inner_rows(mixed, after(branch_grad, q_grads[-1])).astype(LOW), 1)
    token = (mixed_got, input_low, kv_parts, shares, output_pairs)
    kv_parts = [
        mine if got is None else add_low(after(mine, token), got) for mine, got in kv_parts
    ]

    def kv_rows(hop):
        return jnp.stack(
            [
                lax.dynamic_slice_in_dim(kv_parts[s], place(s, links.at(hop)) * own, own, 2)
                for s in seqs
            ],
            axis=2,
        )

    def fsdp_rows(value, below):
        return jnp.concatenate(
            [item for j in range(fsdps) for item in (value[j * shard : (j + 1) * shard], below(j))], axis=0
        )

    def output_rows(hop):
        return lax.dynamic_slice_in_dim(output_part, links.at(hop) * q_cols, q_cols, 0)

    kv_mine, kv_next = kv_rows(0), kv_rows(1)
    mixed_next = add_low(mixed_parts[3], mixed_got)
    mixed_got = links.hop_tp(after(mixed_next, shares))
    kv_got = links.hop_tp(after(kv_next, (input_low, output_pairs)))
    down_weight_grad = links.lay_weight(*links.reduce_weight(after(down_term, kv_next)))
    kv_next = add_low(kv_rows(2), kv_got)
    gate_term = inner_rows(two_all, after(gate_all, kv_next)).astype(LOW)

    in_blocks = [input_low, links.hop_tp(after(input_low, (mixed_got, kv_next, gate_term)))]
    kv_got = links.hop_tp(after(kv_next, mixed_got))
    gate_weight_grad = links.lay_weight(*links.reduce_weight(after(gate_term, mixed_got))).T
    output_both = links.scatter_core(after(output_pairs, mixed_got))
    up_term = inner_rows(two_all, after(up_all, mixed_got)).astype(LOW)
    kv_next = add_low(kv_rows(3), after(kv_got, up_term))
    out_low = hidden + mixed_parts[0].astype(jnp.float32) + mixed_got.astype(jnp.float32)
    out_low = lax.optimization_barrier(out_low.astype(LOW))

    out_blocks = [out_low, links.hop_tp(after(out_low, (in_blocks[1], kv_next)))]
    kv_got = links.hop_tp(after(kv_next, in_blocks[1]))
    up_part, up_got = links.reduce_weight(after(up_term, in_blocks[1]))
    output_part = links.scatter_x(after(output_both, in_blocks[1]), 1)
    grads_all = after(jnp.concatenate(shares, axis=0), kv_got)
    q_bias_row = jnp.sum(grads_all.astype(jnp.float32), axis=0, keepdims=True)
    q_below = jnp.pad(q_bias_row, ((0, 15), (0, 0))).astype(LOW)
    q_pairs = links.pairs(fsdp_rows(inner_rows(one_all, grads_all).astype(LOW), lambda j: q_below), 0)
    kv_grad, kv_term = kv_back(meta, kv_mine, kv_got, cosine, sine, qkv, inputs, tps)
    gain_terms = jnp.concatenate(
        [jnp.sum(attn_term, axis=0) + jnp.sum(kv_term, axis=0), jnp.sum(mlp_term, axis=0)], axis=1
    ).reshape(-1, kv_cols)
    gain_terms = jnp.pad(gain_terms, ((0, 16 - gain_terms.shape[0]), (0, 0))).astype(LOW)
    kv_blocks = [jnp.concatenate([kv_grad, gain_terms], axis=0)]

    in_blocks.append(links.hop_tp(after(in_blocks[1], (out_blocks[1], kv_blocks[0], q_pairs))))
    kv_blocks.append(links.hop_tp(after(kv_blocks[0], out_blocks[1])))
    q_both = links.scatter_core(after(q_pairs, out_blocks[1]))

    out_blocks.append(
        links.hop_tp(
            after(out_blocks[1], (in_blocks[2], kv_blocks[1], q_both))
        )
    )
    kv_blocks.append(links.hop_tp(after(kv_blocks[1], in_blocks[2])))
    q_part = links.scatter_x(after(q_both, in_blocks[2]), 0)
    output_got = links.hop_tp(after(output_rows(1), in_blocks[2]))
    output_next = add_low(output_rows(2), output_got)

    in_blocks.append(
        links.hop_tp(after(in_blocks[2], (out_blocks[2], kv_blocks[2], q_part, output_next)))
    )
    kv_blocks.append(links.hop_tp(after(kv_blocks[2], (out_blocks[2], down_weight_grad))))
    q_total = links.sum_ctx(after(q_part, out_blocks[2]))
    output_got = links.hop_tp(after(output_next, out_blocks[2]))
    output_next = add_low(output_rows(3), output_got)
    output_got = links.hop_tp(after(output_next, in_blocks[3]))
    output_sum = add_low(output_rows(0), output_got)
    own_tokens = seq_count * own
    kv_all = jnp.concatenate([item[:own_tokens] for item in kv_blocks], axis=0)
    gain_rows = sum(
        item[own_tokens : own_tokens + 2 * width // kv_cols].astype(jnp.float32) for item in kv_blocks
    ).reshape(2, width)
    kv_bias_row = jnp.sum(kv_all.astype(jnp.float32), axis=0, keepdims=True)

    def kv_below(j):
        gains = jnp.pad(gain_rows[:, j * shard : (j + 1) * shard], ((0, 0), (0, kv_cols - shard)))
        return jnp.pad(jnp.concatenate([gains, kv_bias_row], axis=0), ((0, 13), (0, 0))).astype(LOW)

    kv_pairs = links.pairs(fsdp_rows(inner_rows(one_all, kv_all).astype(LOW), kv_below), 0)

    out_blocks.append(
        links.hop_tp(
            after(out_blocks[2], (in_blocks[3], kv_pairs))
        )
    )
    kv_both = links.scatter_core(kv_pairs)
    output_weight_grad = links.sum_ctx(output_sum)
    input_grad = last(meta, in_blocks, kv_blocks, qkv, inputs, attn_gamma)
    kv_part = links.scatter_x(after(kv_both, (in_blocks[3], gate_weight_grad)), 0)
    up_part = after(up_part, (input_grad, out_blocks[3]))
    up_weight_grad = links.lay_weight(up_part, up_got).T
    out_blocks[0] = after(out_blocks[0], (output_sum, q_total))
    kv_total = links.sum_ctx(after(kv_part, input_grad))
    outputs = spread_out(meta, out_blocks, seq_count, LOW)
    query_weight_grad = q_total[:shard]
    part = head_dim // fsdps
    query_bias_grad = lax.dynamic_slice_in_dim(
        q_total[shard].reshape(local_heads, head_dim), fsdp * part, part, 1
    )
    kv_weight = kv_total[:shard]
    gains = kv_total[shard : shard + 2, :shard]
    kv_bias = kv_total[shard + 2].reshape(2, kv_heads, head_dim)
    kv_bias = lax.dynamic_slice_in_dim(kv_bias, fsdp * part, part, 2)
    half = kv_cols // 2

    return (
        outputs,
        input_grad,
        gains[0],
        query_weight_grad,
        query_bias_grad,
        kv_weight[:, :half],
        kv_bias[0],
        kv_weight[:, half:],
        kv_bias[1],
        output_weight_grad,
        gains[1],
        gate_weight_grad,
        up_weight_grad,
        down_weight_grad,
    )


def solution(mesh):
    in_specs = (
        P("fsdp", "ctx", None),
        P("fsdp", "ctx", None),
        P("fsdp", "ctx"),
        P("fsdp"),
        P("fsdp", "tp"),
        P("tp", "fsdp"),
        P("fsdp", None),
        P(None, "fsdp"),
        P("fsdp", None),
        P(None, "fsdp"),
        P("tp", "fsdp"),
        P("fsdp"),
        P("fsdp", "tp"),
        P("fsdp", "tp"),
        P("tp", "fsdp"),
    )
    out_specs = (
        P("fsdp", "ctx", None),
        P("fsdp", "ctx", None),
        P("fsdp"),
        P("fsdp", "tp"),
        P("tp", "fsdp"),
        P("fsdp", None),
        P(None, "fsdp"),
        P("fsdp", None),
        P(None, "fsdp"),
        P("tp", "fsdp"),
        P("fsdp"),
        P("fsdp", "tp"),
        P("fsdp", "tp"),
        P("tp", "fsdp"),
    )
    return jax.shard_map(local, mesh=mesh, in_specs=in_specs, out_specs=out_specs, check_vma=False)
```

```python
import functools
import math

import jax
import jax.numpy as jnp
from jax import lax
from jax.experimental import pallas as pl
from jax.experimental.pallas import tpu as pltpu
from jax.sharding import PartitionSpec as P

EPS = 1e-06
THETA = 1000000.0
LOG2E = 1.0 / math.log(2.0)
LOW = jnp.bfloat16
MASKED = -1e30
MIB = 1024 * 1024


def rope_tables(position, width):
    half = width // 2
    freqs = jnp.exp(jnp.arange(half, dtype=jnp.float32) * (-2.0 * math.log(THETA) / width))
    angle = position.astype(jnp.float32)[..., None] * freqs
    cosine, sine = jnp.cos(angle), jnp.sin(angle)
    return (
        jnp.concatenate([cosine, cosine], axis=-1),
        jnp.concatenate([-sine, sine], axis=-1),
    )


def dot(left, right):
    return jnp.dot(left, right, preferred_element_type=jnp.float32)


def inner_rows(left, right):
    return lax.dot_general(
        left, right, (((0,), (0,)), ((), ())), preferred_element_type=jnp.float32
    )


def inner_cols(left, right):
    return lax.dot_general(
        left, right, (((1,), (1,)), ((), ())), preferred_element_type=jnp.float32
    )


def add_low(left, right):
    return (left.astype(jnp.float32) + right.astype(jnp.float32)).astype(LOW)


def after(value, token):
    return lax.optimization_barrier((value, token))[0]


def root_of(values):
    return lax.rsqrt(jnp.mean(values * values, axis=-1, keepdims=True) + EPS)


FSDP, TP, CTX, BEFORE, PLACE = 0, 1, 2, 3, 4


def shard_at(meta, flip, size):
    return pl.multiple_of(jnp.bitwise_xor(meta[FSDP], flip) * size, size)


def tp_at(meta, hop, tps, size):
    return pl.multiple_of(lax.rem(meta[TP] + tps - hop, tps) * size, size)


def call(kernel, grid, in_specs, out_specs, out_shape, scratch=(), cost=None, name=None, vmem=48):
    return pl.pallas_call(
        kernel,
        grid_spec=pltpu.PrefetchScalarGridSpec(
            num_scalar_prefetch=1,
            grid=grid,
            in_specs=in_specs,
            out_specs=out_specs,
            scratch_shapes=list(scratch),
        ),
        out_shape=out_shape,
        compiler_params=pltpu.CompilerParams(vmem_limit_bytes=vmem * MIB),
        cost_estimate=cost,
        name=name,
    )


def whole(array):
    return pl.BlockSpec(array.shape, lambda *_: (0,) * array.ndim)


def shape(dims, kind):
    return jax.ShapeDtypeStruct(dims, kind)


def project_kernel(
    local_heads, kv_heads, head_dim, meta, x_ref, gain_ref, bias_ref, *refs
):
    weights, (cos_ref, sin_ref, n_ref, q_ref, kv_ref) = refs[:4], refs[4:]
    rows = x_ref.shape[1]
    size = n_ref.shape[1] // 4
    values = x_ref[...].reshape(rows, -1).astype(jnp.float32)
    n_ref[...] = (values * root_of(values) * gain_ref[...]).astype(LOW)
    lin = bias_ref[...]
    for flip, weight in enumerate(weights):
        lin = lin + dot(n_ref[:, pl.ds(shard_at(meta, flip, size), size)], weight[:size, :])
    cosine, sine = cos_ref[...], sin_ref[...]
    for head in range(local_heads + 2 * kv_heads):
        part = lin[:, head * head_dim : (head + 1) * head_dim]
        if head < local_heads + kv_heads:
            part = part * cosine + pltpu.roll(part, head_dim // 2, 1) * sine
        if head < local_heads:
            q_ref[0, :, head * head_dim : (head + 1) * head_dim] = part.astype(LOW)
        else:
            at = (head - local_heads) * head_dim
            kv_ref[:, at : at + head_dim] = part.astype(LOW)


def project(meta, inputs, gain, bias, weights, cosine, sine, sizes):
    seq_count, block_len, width = inputs.shape
    local_heads, kv_heads, head_dim, tps = sizes
    own = block_len // tps
    q_cols, kv_cols = local_heads * head_dim, 2 * kv_heads * head_dim

    def row(i, m):
        return (i, 0)

    def device(i, m):
        seq, place = i // tps, i % tps
        return jnp.where(seq % 2 == 0, place, tps - 1 - place), seq, 0

    tokens = seq_count * block_len
    return call(
        functools.partial(project_kernel, local_heads, kv_heads, head_dim),
        (seq_count * tps,),
        [
            pl.BlockSpec((1, own, width), lambda i, m: (i // tps, i % tps, 0)),
            whole(gain), whole(bias), *(whole(w) for w in weights),
            pl.BlockSpec((own, head_dim), row), pl.BlockSpec((own, head_dim), row),
        ],
        [
            pl.BlockSpec((own, width), row),
            pl.BlockSpec((1, own, q_cols), device),
            pl.BlockSpec((own, kv_cols), row),
        ],
        [
            shape((tokens, width), LOW),
            shape((tps, seq_count * own, q_cols), LOW),
            shape((tokens, kv_cols), LOW),
        ],
        cost=pl.CostEstimate(
            flops=2 * tokens * width * (q_cols + kv_cols), bytes_accessed=8 * tokens * width, transcendentals=0
        ),
        name="project",
    )(meta, inputs, gain, bias, *weights, cosine, sine)


def fwd_kernel(
    heads, block, parts, meta, *refs
):
    q_refs, (kb_ref, vb_ref, k_ref, v_ref, order_ref, o_ref, lse_ref, qg_ref, acc_ref, m_ref, l_ref) = (
        refs[:parts], refs[parts:]
    )
    own, cols = q_refs[0].shape[1:]
    head_dim = acc_ref.shape[0]
    scale = LOG2E / math.sqrt(head_dim)
    each = cols // head_dim
    for head in range(heads):
        qg_ref[head * own : (head + 1) * own, :] = q_refs[head // each][
            0, :, (head % each) * head_dim : (head % each + 1) * head_dim
        ]
    acc_ref[...] = jnp.zeros_like(acc_ref)
    m_ref[...] = jnp.full_like(m_ref, MASKED)
    l_ref[...] = jnp.zeros_like(l_ref)
    first = meta[PLACE + pl.program_id(0)] * own
    last = first // block

    def step(key_ref, value_ref, index, masked):
        start = pl.multiple_of(index * block, block)
        keys = key_ref[pl.ds(start, block), :]
        values = value_ref[pl.ds(start, block), :]
        logits = inner_cols(keys, qg_ref[...]) * scale
        if masked:
            key_order = (start - first) + lax.broadcasted_iota(jnp.int32, logits.shape, 0)
            logits = jnp.where(key_order <= order_ref[...], logits, MASKED)
        before = m_ref[...]
        peak = jnp.maximum(before, jnp.max(logits, axis=0, keepdims=True))
        weights = jnp.exp2(logits - peak)
        fade = jnp.exp2(before - peak)
        m_ref[...] = peak
        l_ref[...] = l_ref[...] * fade + jnp.sum(weights, axis=0, keepdims=True)
        acc_ref[...] = acc_ref[...] * fade + inner_rows(values, weights.astype(LOW))

    def early(index, carry):
        step(kb_ref, vb_ref, index, False)
        return carry

    def late(index, carry):
        step(k_ref, v_ref, index, False)
        return carry

    lax.fori_loop(0, meta[BEFORE], early, 0)
    lax.fori_loop(0, last, late, 0)
    step(k_ref, v_ref, last, True)
    total = l_ref[...]
    lse_ref[...] = (m_ref[...] + jnp.log2(total)).reshape(lse_ref.shape)
    mixed = jnp.transpose(acc_ref[...] / total)
    for head in range(heads):
        o_ref[:, head * head_dim : (head + 1) * head_dim] = mixed[
            head * own : (head + 1) * own, :
        ].astype(LOW)


def bwd_kernel(heads, block, parts, seq, meta, *refs):
    q_refs, (
        kb_ref, vb_ref, k_ref, v_ref, order_ref, o_ref, g_ref, lse_ref, cos_ref, sin_ref,
        dq_ref, db_ref, dd_ref, qg_ref, gg_ref, both_ref, acc_ref,
    ) = refs[:parts], refs[parts:]
    own, cols = q_refs[0].shape[1:]
    head_dim = acc_ref.shape[0]
    scale = 1.0 / math.sqrt(head_dim)
    each = cols // head_dim
    for head in range(heads):
        rows = slice(head * own, (head + 1) * own)
        at = slice(head * head_dim, (head + 1) * head_dim)
        qg_ref[rows, :] = q_refs[head // each][
            0, :, (head % each) * head_dim : (head % each + 1) * head_dim
        ]
        gg_ref[rows, :] = g_ref[:, at]
        both_ref[rows, :] = g_ref[:, at].astype(jnp.float32) * o_ref[:, at].astype(jnp.float32)
    center = jnp.sum(jnp.transpose(both_ref[...]), axis=0, keepdims=True)
    acc_ref[...] = jnp.zeros_like(acc_ref)
    lse = lse_ref[...].reshape(order_ref.shape)
    first = meta[PLACE + seq] * own
    last = first // block

    def step(key_ref, value_ref, out_ref, index, masked):
        start = pl.multiple_of(index * block, block)
        keys = key_ref[pl.ds(start, block), :]
        values = value_ref[pl.ds(start, block), :]
        logits = inner_cols(keys, qg_ref[...]) * (scale * LOG2E)
        if masked:
            key_order = (start - first) + lax.broadcasted_iota(jnp.int32, logits.shape, 0)
            logits = jnp.where(key_order <= order_ref[...], logits, MASKED)
        probs = jnp.exp2(logits - lse)
        out_ref[1, 0, pl.ds(start, block), :] = dot(probs.astype(LOW), gg_ref[...]).astype(LOW)
        prob_grad = inner_cols(values, gg_ref[...])
        logit_grad = (probs * (prob_grad - center)).astype(LOW)
        out_ref[0, 0, pl.ds(start, block), :] = (dot(logit_grad, qg_ref[...]) * scale).astype(LOW)
        acc_ref[...] += inner_rows(keys, logit_grad)

    def early(index, carry):
        step(kb_ref, vb_ref, db_ref, index, False)
        return carry

    def late(index, carry):
        step(k_ref, v_ref, dd_ref, index, False)
        return carry

    def clear(ref):
        def body(index, carry):
            start = pl.multiple_of(index * block, block)
            ref[:, :, pl.ds(start, block), :] = jnp.zeros((2, 1, block, head_dim), LOW)
            return carry

        return body

    lax.fori_loop(0, meta[BEFORE], early, 0)
    lax.fori_loop(meta[BEFORE], kb_ref.shape[0] // block, clear(db_ref), 0)
    lax.fori_loop(0, last, late, 0)
    step(k_ref, v_ref, dd_ref, last, True)
    lax.fori_loop(last + 1, k_ref.shape[0] // block, clear(dd_ref), 0)
    both_ref[...] = jnp.transpose(acc_ref[...])
    for head in range(heads):
        grad = both_ref[head * own : (head + 1) * own, :] * scale
        grad = grad * cos_ref[...] - pltpu.roll(grad, head_dim // 2, 1) * sin_ref[...]
        dq_ref[:, head * head_dim : (head + 1) * head_dim] = grad.astype(LOW)


def attention_specs(queries, kv_before, kv_own, sizes, seq=None):
    seq_count, kv_heads, head_dim, tps = sizes
    rows = queries.shape[1] // seq_count
    parts = tps // kv_heads
    heads = queries.shape[2] * parts // head_dim
    before, block_len = kv_before.shape[0] // seq_count, kv_own.shape[0] // seq_count

    def spec(dims, index):
        if seq is None:
            return pl.BlockSpec(dims, index)
        return pl.BlockSpec(dims, lambda g, m: index(seq, g, m))

    def piece(part):
        return spec(
            (1, rows, queries.shape[2]),
            lambda s, g, m: (lax.rem(m[TP] + tps - (g * parts + part), tps), s, 0),
        )

    specs = [piece(part) for part in range(parts)] + [
        spec((before, head_dim), lambda s, g, m: (s, g)),
        spec((before, head_dim), lambda s, g, m: (s, kv_heads + g)),
        spec((block_len, head_dim), lambda s, g, m: (s, g)),
        spec((block_len, head_dim), lambda s, g, m: (s, kv_heads + g)),
        spec((1, heads * rows), lambda s, g, m: (0, 0)),
    ]
    return specs, rows, parts, heads, before, block_len


def attend(meta, queries, kv_before, kv_own, order, block, sizes):
    seq_count, kv_heads, head_dim, tps = sizes
    specs, rows, parts, heads, before, block_len = attention_specs(queries, kv_before, kv_own, sizes)
    width, wide = kv_heads * heads * head_dim, heads * rows
    work = seq_count * rows * width * (before + block_len)
    return call(
        functools.partial(fwd_kernel, heads, block, parts),
        (seq_count, kv_heads),
        specs,
        [
            pl.BlockSpec((rows, heads * head_dim), lambda s, g, m: (s, g)),
            pl.BlockSpec((1, 1, 1, wide), lambda s, g, m: (s, g, 0, 0)),
        ],
        [shape((seq_count * rows, width), LOW), shape((seq_count, kv_heads, 1, wide), jnp.float32)],
        [
            pltpu.VMEM((wide, head_dim), LOW),
            pltpu.VMEM((head_dim, wide), jnp.float32),
            pltpu.VMEM((1, wide), jnp.float32),
            pltpu.VMEM((1, wide), jnp.float32),
        ],
        cost=pl.CostEstimate(flops=8 * work, bytes_accessed=1 << 22, transcendentals=0),
        name="attend",
    )(meta, *([queries] * parts), kv_before, kv_before, kv_own, kv_own, order)


def attend_back(
    meta, seq, queries, kv_before, kv_own, order, mixed, grads, lse, cosine, sine, block, sizes
):
    seq_count, kv_heads, head_dim, tps = sizes
    specs, rows, parts, heads, before, block_len = attention_specs(
        queries, kv_before, kv_own, sizes, seq
    )
    width, wide = kv_heads * heads * head_dim, heads * rows
    work = rows * width * (before + block_len)
    wide_spec = pl.BlockSpec((rows, heads * head_dim), lambda g, m: (seq, g))
    table_spec = pl.BlockSpec((rows, head_dim), lambda g, m: (seq * tps + m[PLACE + seq], 0))
    return call(
        functools.partial(bwd_kernel, heads, block, parts, seq),
        (kv_heads,),
        specs
        + [
            wide_spec,
            wide_spec,
            pl.BlockSpec((1, 1, 1, wide), lambda g, m: (seq, g, 0, 0)),
            table_spec,
            table_spec,
        ],
        [
            pl.BlockSpec((rows, heads * head_dim), lambda g, m: (0, g)),
            pl.BlockSpec((2, 1, before, head_dim), lambda g, m: (0, g, 0, 0)),
            pl.BlockSpec((2, 1, block_len, head_dim), lambda g, m: (0, g, 0, 0)),
        ],
        [
            shape((rows, width), LOW),
            shape((2, kv_heads, before, head_dim), LOW),
            shape((2, kv_heads, block_len, head_dim), LOW),
        ],
        [
            pltpu.VMEM((wide, head_dim), LOW),
            pltpu.VMEM((wide, head_dim), LOW),
            pltpu.VMEM((wide, head_dim), jnp.float32),
            pltpu.VMEM((head_dim, wide), jnp.float32),
        ],
        cost=pl.CostEstimate(flops=16 * work, bytes_accessed=1 << 22, transcendentals=0),
        name="attend_back",
    )(
        meta, *([queries] * parts), kv_before, kv_before, kv_own, kv_own, order,
        mixed, grads, lse, cosine, sine,
    )


def output_pieces(meta, weights, tps):
    own, other, near, far, other_near, other_far = weights
    depth, half = own.shape[0], near.shape[0]
    low = pl.multiple_of(meta[CTX] * (depth - half), 128)
    high = pl.multiple_of((1 - meta[CTX]) * (depth - half), 128)
    pieces = [(0, None, own), (1, None, other)]
    if half == depth:
        return pieces + [(2, None, near), (3, None, other_near)]
    return pieces + [(2, low, near), (2, high, far), (3, low, other_near), (3, high, other_far)]


def merge_kernel(tps, meta, o_ref, x_ref, *refs):
    weights, (gain_ref, h_ref, n_ref, turned_ref) = refs[:6], refs[6:]
    rows, width = h_ref.shape
    size, depth = width // 4, o_ref.shape[1]
    part = depth // tps
    for hop in range(tps):
        turned_ref[:, hop * part : (hop + 1) * part] = o_ref[:, pl.ds(tp_at(meta, hop, tps, part), part)]
    h_ref[...] = x_ref[...].reshape(rows, width).astype(jnp.float32)
    for flip, first, weight in output_pieces(meta, weights, tps):
        left = turned_ref[...] if first is None else turned_ref[:, pl.ds(first, weight.shape[0])]
        h_ref[:, pl.ds(shard_at(meta, flip, size), size)] += dot(left, weight[...])
    hidden = h_ref[...]
    n_ref[...] = (hidden * root_of(hidden) * gain_ref[...]).astype(LOW)


def merge(meta, mixed, inputs, weights, gain, tps):
    seq_count, block_len, width = inputs.shape
    own = block_len // tps
    depth = mixed.shape[1]
    row = pl.BlockSpec((own, width), lambda s, m: (s, 0))
    return call(
        functools.partial(merge_kernel, tps),
        (seq_count,),
        [
            pl.BlockSpec((own, depth), lambda s, m: (s, 0)),
            pl.BlockSpec((1, own, width), lambda s, m: (s, m[PLACE + s], 0)),
            *(whole(w) for w in weights),
            whole(gain),
        ],
        [row, row],
        [shape((seq_count * own, width), jnp.float32), shape((seq_count * own, width), LOW)],
        [pltpu.VMEM((own, depth), LOW)],
        cost=pl.CostEstimate(
            flops=2 * seq_count * own * depth * width, bytes_accessed=1 << 23, transcendentals=0
        ),
        name="merge",
    )(meta, mixed, inputs, *weights, gain)


def turn_kernel(
    tps, meta, a_ref, b_ref, h_ref, c_ref, *refs,
):
    weights, (gain_ref, hg_ref, bg_ref, ag_ref, term_ref, turned_ref) = refs[:6], refs[6:]
    rows, width = h_ref.shape
    size, depth = width // 4, ag_ref.shape[1]
    two_grad = a_ref[...].astype(jnp.float32) + b_ref[...].astype(jnp.float32)
    hidden = h_ref[...]
    root = root_of(hidden)
    term_ref[...] = jnp.sum(two_grad * hidden * root, axis=0, keepdims=True).reshape(term_ref.shape)
    scaled = gain_ref[...] * two_grad
    grad = (
        c_ref[...].reshape(rows, width).astype(jnp.float32)
        + root * scaled
        - hidden * root**3 * jnp.mean(scaled * hidden, axis=-1, keepdims=True)
    )
    hg_ref[...] = grad
    bg_ref[...] = grad.astype(LOW)
    turned_ref[...] = jnp.zeros_like(turned_ref)
    for flip, first, weight in output_pieces(meta, weights, tps):
        at = slice(None) if first is None else pl.ds(first, weight.shape[0])
        turned_ref[:, at] += inner_cols(bg_ref[:, pl.ds(shard_at(meta, flip, size), size)], weight[...])
    part = depth // tps
    for hop in range(tps):
        ag_ref[:, pl.ds(tp_at(meta, hop, tps, part), part)] = turned_ref[
            :, hop * part : (hop + 1) * part
        ].astype(LOW)


def turn(meta, two_own, two_got, hidden, cotangent, weights, gain, depth, tps):
    seq_count, block_len, width = cotangent.shape
    own = block_len // tps
    row = pl.BlockSpec((own, width), lambda s, m: (s, 0))
    tokens = seq_count * own
    return call(
        functools.partial(turn_kernel, tps),
        (seq_count,),
        [
            row, row, row,
            pl.BlockSpec((1, own, width), lambda s, m: (s, m[PLACE + s], 0)),
            *(whole(w) for w in weights),
            whole(gain),
        ],
        [
            row, row,
            pl.BlockSpec((own, depth), lambda s, m: (s, 0)),
            pl.BlockSpec((1, 1, width), lambda s, m: (s, 0, 0)),
        ],
        [
            shape((tokens, width), jnp.float32),
            shape((tokens, width), LOW),
            shape((tokens, depth), LOW),
            shape((seq_count, 1, width), jnp.float32),
        ],
        [pltpu.VMEM((own, depth), jnp.float32)],
        cost=pl.CostEstimate(flops=2 * tokens * depth * width, bytes_accessed=1 << 23, transcendentals=0),
        name="turn",
    )(meta, two_own, two_got, hidden, cotangent, *weights, gain)


def back_through_norm(grad, values, gain):
    root = root_of(values)
    scaled = gain * grad
    term = jnp.sum(grad * values * root, axis=0, keepdims=True)
    return root * scaled - values * root**3 * jnp.mean(scaled * values, axis=-1, keepdims=True), term


def finish_kernel(tps, meta, g_ref, q_ref, x_ref, hg_ref, gain_ref, out_ref, term_ref, turned_ref):
    part = g_ref.shape[1] // tps
    for hop in range(tps):
        turned_ref[:, hop * part : (hop + 1) * part] = g_ref[:, pl.ds(tp_at(meta, hop, tps, part), part)]
    values = x_ref[...].reshape(hg_ref.shape).astype(jnp.float32)
    part, term = back_through_norm(inner_cols(turned_ref[...], q_ref[...]), values, gain_ref[...])
    term_ref[...] = term.reshape(term_ref.shape)
    out_ref[...] = (hg_ref[...] + part).astype(LOW)


def finish(meta, q_grad, q_full, inputs, hidden_grad, gain, tps):
    seq_count, block_len, width = inputs.shape
    own = block_len // tps
    tokens = seq_count * own
    row = pl.BlockSpec((own, width), lambda s, m: (s, 0))
    return call(
        functools.partial(finish_kernel, tps),
        (seq_count,),
        [
            pl.BlockSpec((own, q_grad.shape[1]), lambda s, m: (s, 0)),
            whole(q_full),
            pl.BlockSpec((1, own, width), lambda s, m: (s, m[PLACE + s], 0)),
            row,
            whole(gain),
        ],
        [row, pl.BlockSpec((1, 1, width), lambda s, m: (s, 0, 0))],
        [shape((tokens, width), LOW), shape((seq_count, 1, width), jnp.float32)],
        [pltpu.VMEM((own, q_grad.shape[1]), LOW)],
        cost=pl.CostEstimate(
            flops=2 * tokens * q_grad.shape[1] * width, bytes_accessed=1 << 23, transcendentals=0
        ),
        name="finish",
    )(meta, q_grad, q_full, inputs, hidden_grad, gain)


def one_from_kv(meta, kv_grad, weights, one_ref):
    size = one_ref.shape[1] // 4
    skip = weights[0].shape[1] - kv_grad.shape[1]
    for flip, weight in enumerate(weights):
        one_ref[:, pl.ds(shard_at(meta, flip, size), size)] = inner_cols(
            kv_grad, weight[:size, skip:]
        )
    return one_ref[...]


def kv_kernel(kv_heads, head_dim, meta, a_ref, b_ref, cos_ref, sin_ref, *refs):
    weights, (x_ref, kv_ref, term_ref, one_ref) = refs[:4], refs[4:]
    cosine, sine = cos_ref[...], sin_ref[...]
    for kind in range(2):
        for head in range(kv_heads):
            grad = (
                a_ref[kind, head, 0].astype(jnp.float32) + b_ref[kind, head, 0].astype(jnp.float32)
            )
            if kind == 0:
                grad = grad * cosine - pltpu.roll(grad, head_dim // 2, 1) * sine
            at = (kind * kv_heads + head) * head_dim
            kv_ref[:, at : at + head_dim] = grad.astype(LOW)
    one = one_from_kv(meta, kv_ref[...], weights, one_ref)
    values = x_ref[...].reshape(one.shape).astype(jnp.float32)
    term = jnp.sum(one * values * root_of(values), axis=0, keepdims=True)
    term_ref[...] = term.reshape(term_ref.shape)


def kv_back(meta, kv_mine, kv_got, cosine, sine, weights, inputs, tps):
    seq_count, block_len, width = inputs.shape
    own = block_len // tps
    kv_heads, head_dim = kv_mine.shape[1], kv_mine.shape[4]
    kv_cols = 2 * kv_heads * head_dim
    kv_spec = pl.BlockSpec((2, kv_heads, 1, own, head_dim), lambda s, m: (0, 0, s, 0, 0))
    table_spec = pl.BlockSpec((own, head_dim), lambda s, m: (s * tps + m[PLACE + s], 0))
    return call(
        functools.partial(kv_kernel, kv_heads, head_dim),
        (seq_count,),
        [
            kv_spec, kv_spec, table_spec, table_spec,
            *(whole(w) for w in weights),
            pl.BlockSpec((1, own, width), lambda s, m: (s, m[PLACE + s], 0)),
        ],
        [
            pl.BlockSpec((own, kv_cols), lambda s, m: (s, 0)),
            pl.BlockSpec((1, 1, width), lambda s, m: (s, 0, 0)),
        ],
        [shape((seq_count * own, kv_cols), LOW), shape((seq_count, 1, width), jnp.float32)],
        [pltpu.VMEM((own, width), jnp.float32)],
        cost=pl.CostEstimate(
            flops=2 * seq_count * own * kv_cols * width, bytes_accessed=1 << 22, transcendentals=0
        ),
        name="kv_back",
    )(meta, kv_mine, kv_got, cosine, sine, *weights, inputs)


def last_kernel(tps, meta, *refs):
    blocks, kvs, weights = refs[:tps], refs[tps : 2 * tps], refs[2 * tps : 2 * tps + 4]
    x_ref, gain_ref, out_ref, one_ref = refs[2 * tps + 4 :]
    seq = pl.program_id(0)
    own = blocks[0].shape[0]
    for hop in range(tps):
        device = lax.rem(meta[TP] + tps - hop, tps)
        place = jnp.where(seq % 2 == 0, device, tps - 1 - device)
        at = pl.ds(pl.multiple_of(place * own, own), own)
        one = one_from_kv(meta, kvs[hop][...], weights, one_ref)
        values = x_ref[0, at, :].astype(jnp.float32)
        part, _ = back_through_norm(one, values, gain_ref[...])
        out_ref[0, at, :] = blocks[hop][...].astype(jnp.float32) + part


def last(meta, blocks, kvs, weights, inputs, gain):
    seq_count, block_len, width = inputs.shape
    tps = len(blocks)
    own = block_len // tps
    every = pl.BlockSpec((1, block_len, width), lambda s, m: (s, 0, 0))
    return call(
        functools.partial(last_kernel, tps),
        (seq_count,),
        [pl.BlockSpec((own, width), lambda s, m: (s, 0))] * tps
        + [pl.BlockSpec((own, kvs[0].shape[1]), lambda s, m: (s, 0))] * tps
        + [whole(w) for w in weights]
        + [every, whole(gain)],
        every,
        shape(inputs.shape, jnp.float32),
        [pltpu.VMEM((own, width), jnp.float32)],
        cost=pl.CostEstimate(
            flops=2 * seq_count * block_len * kvs[0].shape[1] * width, bytes_accessed=1 << 24, transcendentals=0
        ),
        name="last",
    )(meta, *blocks, *kvs, *weights, inputs, gain)


def feed_kernel(first, hidden, *refs):
    n_ref, c_ref, wg_ref, wu_ref, wd_ref = refs[1:6]
    act_ref, gg_ref, ug_ref, all_ref, two_ref, mix_ref, two_acc, mix_acc = refs[6 if first else 10 :]
    step, tile = pl.program_id(0), wg_ref.shape[0]
    steps = -(-hidden // tile)

    def body(count):
        gate = inner_cols(n_ref[...], wg_ref[:count, :])
        up_part = inner_cols(n_ref[...], wu_ref[:count, :])
        act_grad = inner_cols(c_ref[...], wd_ref[:count, :])
        sigma = jax.nn.sigmoid(gate)
        silu = gate * sigma
        act = (silu * up_part).astype(LOW)
        gate_grad = (act_grad * up_part * (sigma * (1.0 + gate * (1.0 - sigma)))).astype(LOW)
        up_grad = (act_grad * silu).astype(LOW)
        act_ref[:, :count], gg_ref[:, :count], ug_ref[:, :count] = act, gate_grad, up_grad
        return (
            dot(gate_grad, wg_ref[:count, :]) + dot(up_grad, wu_ref[:count, :]),
            dot(act, wd_ref[:count, :]),
        )

    @pl.when(step == 0)
    def _():
        all_ref[...] = n_ref[...]
        two_acc[...], mix_acc[...] = body(tile)

    @pl.when(jnp.logical_and(step > 0, step < steps - 1))
    def _():
        two, mix = body(tile)
        two_acc[...] += two
        mix_acc[...] += mix

    @pl.when(step == steps - 1)
    def _():
        two, mix = body(hidden - (steps - 1) * tile)
        two_ref[...] = (two_acc[...] + two).astype(LOW)
        mix_ref[...] = (mix_acc[...] + mix).astype(LOW)


def feed(meta, normed, cots, gate_down, up, hop, tps, kept):
    rows, width = normed.shape
    hidden = up.shape[1]
    tile = 768
    assert hidden > tile
    gate_spec = pl.BlockSpec((None, tile, width), lambda j, m: (0, j, 0))
    down_spec = pl.BlockSpec((None, tile, width), lambda j, m: (1, j, 0))
    column = pl.BlockSpec((rows, tile), lambda j, m: (hop, j))
    fixed = pl.BlockSpec((rows, width), lambda j, m: (0, 0))
    first = hop == 0
    wide = shape((tps * rows, hidden), LOW)
    *hiddens, two_part, mixed_part = pl.pallas_call(
        functools.partial(feed_kernel, first, hidden),
        grid_spec=pltpu.PrefetchScalarGridSpec(
            num_scalar_prefetch=1,
            grid=(-(-hidden // tile),),
            in_specs=[fixed, pl.BlockSpec((rows, width), lambda j, m: (hop, 0)), gate_spec, gate_spec, down_spec]
            + ([] if first else [pl.BlockSpec(memory_space=pl.ANY)] * 4),
            out_specs=[
                column, column, column, pl.BlockSpec((rows, width), lambda j, m: (hop, 0)), fixed, fixed
            ],
            scratch_shapes=[pltpu.VMEM((rows, width), jnp.float32)] * 2,
        ),
        out_shape=[
            wide, wide, wide, shape((tps * rows, width), LOW),
            shape((rows, width), LOW), shape((rows, width), LOW),
        ],
        input_output_aliases={} if first else {6: 0, 7: 1, 8: 2, 9: 3},
        compiler_params=pltpu.CompilerParams(vmem_limit_bytes=56 * MIB),
        cost_estimate=pl.CostEstimate(
            flops=12 * rows * width * hidden, bytes_accessed=6 * width * hidden, transcendentals=rows * hidden
        ),
        name="feed",
    )(meta, normed, cots, gate_down, up, gate_down, *(() if first else kept))
    return hiddens, two_part, mixed_part


def assemble_kernel(tiles, meta, own_ref, near_ref, far_ref, o_own_ref, o_near_ref, o_far_ref, out_ref):
    size = own_ref.shape[1]
    is_near = (pl.program_id(0) // tiles) == meta[CTX]
    out_ref[:, pl.ds(shard_at(meta, 0, size), size)] = own_ref[...]
    out_ref[:, pl.ds(shard_at(meta, 1, size), size)] = o_own_ref[...]

    @pl.when(is_near)
    def _():
        out_ref[:, pl.ds(shard_at(meta, 2, size), size)] = near_ref[...]
        out_ref[:, pl.ds(shard_at(meta, 3, size), size)] = o_near_ref[...]

    @pl.when(jnp.logical_not(is_near))
    def _():
        out_ref[:, pl.ds(shard_at(meta, 2, size), size)] = far_ref[...]
        out_ref[:, pl.ds(shard_at(meta, 3, size), size)] = o_far_ref[...]


def assemble(meta, own, near, far, other, other_near, other_far):
    rows, size = own.shape
    tiles = 2 if rows % 64 == 0 else 1
    tile = rows // (2 * tiles)
    every = pl.BlockSpec((tile, size), lambda i, m: (i, 0))
    half = pl.BlockSpec((tile, size), lambda i, m: (i % tiles, 0))
    return call(
        functools.partial(assemble_kernel, tiles),
        (2 * tiles,),
        [every, half, half, every, half, half],
        pl.BlockSpec((tile, 4 * size), lambda i, m: (i, 0)),
        shape((rows, 4 * size), LOW),
        cost=pl.CostEstimate(flops=0, bytes_accessed=16 * rows * size, transcendentals=0),
        name="assemble",
    )(meta, own, near, far, other, other_near, other_far)


def lay_kernel(low_ref, high_ref, out_ref):
    both = jnp.concatenate([low_ref[...], high_ref[...]], axis=0)
    out_ref[...] = jnp.transpose(both.astype(jnp.float32))


def lay(low, high):
    rows, cols = low.shape
    return pl.pallas_call(
        lay_kernel,
        in_specs=[pl.BlockSpec(memory_space=pltpu.VMEM)] * 2,
        out_specs=pl.BlockSpec(memory_space=pltpu.VMEM),
        out_shape=shape((cols, 2 * rows), jnp.float32),
        compiler_params=pltpu.CompilerParams(vmem_limit_bytes=48 * MIB),
        cost_estimate=pl.CostEstimate(flops=0, bytes_accessed=12 * rows * cols, transcendentals=0),
        name="lay",
    )(low, high)


def spread_kernel(tps, meta, *refs):
    out_ref = refs[tps]
    seq_count = out_ref.shape[0]
    own = refs[0].shape[0] // seq_count
    for hop in range(tps):
        device = lax.rem(meta[TP] + tps - hop, tps)
        for s in range(seq_count):
            place = device if s % 2 == 0 else tps - 1 - device
            at = pl.ds(pl.multiple_of(place * own, own), own)
            out_ref[s, at, :] = refs[hop][s * own : (s + 1) * own, :].astype(out_ref.dtype)


def spread_out(meta, blocks, seq_count, kind):
    tps = len(blocks)
    rows, width = blocks[0].shape
    dims = (seq_count, rows // seq_count * tps, width)
    return call(
        functools.partial(spread_kernel, tps),
        (1,),
        [whole(item) for item in blocks],
        pl.BlockSpec(dims, lambda *_: (0, 0, 0)),
        shape(dims, kind),
        cost=pl.CostEstimate(flops=0, bytes_accessed=8 * rows * tps * width, transcendentals=0),
        name="spread",
    )(meta, *blocks)


class Links:
    def __init__(self):
        self.tp, self.ctx, self.fsdp = (lax.axis_index(a) for a in ("tp", "ctx", "fsdp"))
        self.tps, self.ctxs, self.fsdps = (lax.axis_size(a) for a in ("tp", "ctx", "fsdp"))
        self.core, self.x = self.fsdp % 2, self.fsdp // 2
        assert self.fsdps == 4

    def to_core(self, value):
        return lax.ppermute(value, "fsdp", [(0, 1), (1, 0), (2, 3), (3, 2)])

    def to_x(self, value):
        return lax.ppermute(value, "fsdp", [(0, 2), (2, 0), (1, 3), (3, 1)])

    def to_y(self, value):
        return lax.ppermute(value, "ctx", [(0, 1), (1, 0)])

    def hop_tp(self, value, hop=1):
        return lax.ppermute(value, "tp", [(i, (i + hop) % self.tps) for i in range(self.tps)])

    def gather_fsdp(self, shard):
        across = self.to_x(shard)
        return shard, across, self.to_core(jnp.concatenate([shard, across], axis=0))

    def gather_tp(self, block):
        blocks = [block]
        for _ in range(1, self.tps):
            blocks.append(self.hop_tp(blocks[-1]))
        return blocks

    def scatter_tp(self, blocks):
        total = blocks[1]
        for hop in range(1, self.tps):
            got = self.hop_tp(total)
            if hop < self.tps - 1:
                total = add_low(blocks[hop + 1], got)
        return blocks[0], got

    def at(self, hop):
        return (self.tp - hop + self.tps) % self.tps

    def pairs(self, value, axis):
        size = value.shape[axis] // 4

        def pair(core):
            return jnp.concatenate(
                [
                    lax.dynamic_slice_in_dim(value, (2 * x + core) * size, size, axis)
                    for x in range(2)
                ],
                axis,
            )

        return pair(self.core), pair(1 - self.core)

    def scatter_core(self, pairs):
        return add_low(pairs[0], self.to_core(pairs[1]))

    def scatter_x(self, both, axis):
        size = both.shape[axis] // 2
        away = lax.dynamic_slice_in_dim(both, (1 - self.x) * size, size, axis)
        keep = lax.dynamic_slice_in_dim(both, self.x * size, size, axis)
        return add_low(keep, self.to_x(away))

    def sum_ctx(self, value):
        value = lax.optimization_barrier(value.astype(LOW))
        if self.ctxs == 2:
            return value.astype(jnp.float32) + self.to_y(value).astype(jnp.float32)
        return lax.psum(value.astype(jnp.float32), "ctx")

    def reduce_weight(self, term):
        part = lax.psum_scatter(term, ("fsdp", "ctx"), scatter_dimension=0, tiled=True)
        if self.ctxs != 2:
            return lax.all_gather(part, "ctx", axis=0, tiled=True), None
        part = lax.optimization_barrier(part)
        return part, self.to_y(part)

    def lay_weight(self, part, got):
        if got is None:
            return part.astype(jnp.float32).T
        return lay(jnp.where(self.ctx == 0, part, got), jnp.where(self.ctx == 0, got, part))


def local(
    inputs,
    cotangent,
    positions,
    attn_gain,
    query_weight,
    query_bias,
    key_weight,
    key_bias,
    value_weight,
    value_bias,
    output_weight,
    mlp_gain,
    gate_weight,
    up_weight,
    down_weight,
):
    links = Links()
    seq_count, block_len, width = inputs.shape
    tp, tps, ctx, ctxs = links.tp, links.tps, links.ctx, links.ctxs
    fsdp, fsdps = links.fsdp, links.fsdps
    own = block_len // tps
    local_heads, kv_heads = query_bias.shape[0], key_bias.shape[0]
    head_dim = key_weight.shape[1] // kv_heads
    q_cols = local_heads * head_dim
    kv_cols = 2 * kv_heads * head_dim
    depth = q_cols * tps
    shard = width // fsdps
    tokens = seq_count * block_len
    key_block = block_len // 2 if block_len % (2 * own) == 0 else block_len
    seqs = range(seq_count)

    def place(seq, device):
        return device if seq % 2 == 0 else tps - 1 - device

    def block_rows(value, hop):
        return jnp.concatenate(
            [
                lax.dynamic_slice_in_dim(value[s], place(s, links.at(hop)) * own, own, 0)
                for s in seqs
            ],
            axis=0,
        )

    meta = jnp.stack(
        [fsdp, tp, ctx, ctx * (block_len // key_block)] + [place(s, tp) for s in seqs]
    ).astype(jnp.int32)

    lanes = q_cols + kv_cols
    smalls = jnp.concatenate([b.reshape(-1) for b in (query_bias, key_bias, value_bias)])
    extra = jnp.stack(
        [jnp.pad(row, (0, lanes - row.shape[0])) for row in (attn_gain, mlp_gain, smalls)]
    )
    extra = jnp.pad(extra, ((0, 13), (0, 0)))
    pack = jnp.concatenate(
        [jnp.concatenate([query_weight, key_weight, value_weight], axis=1), extra], axis=0
    )
    pack_core, pack_across = links.to_core(pack), links.to_x(pack)
    qkv = pack, pack_core, pack_across, links.to_core(pack_across)
    o_blocks = links.gather_tp(output_weight)
    up_mine = up_weight.T

    rows = jnp.stack([item[shard : shard + 3] for item in qkv])
    rows = [
        lax.dynamic_index_in_dim(rows, jnp.bitwise_xor(fsdp, j), 0, keepdims=False) for j in range(4)
    ]
    attn_gamma = jnp.concatenate([r[0, :shard] for r in rows])[None].astype(jnp.float32)
    mlp_gamma = jnp.concatenate([r[1, :shard] for r in rows])[None].astype(jnp.float32)
    bias = jnp.concatenate(
        [r[2, : smalls.shape[0]].reshape(-1, head_dim // fsdps) for r in rows], axis=1
    ).reshape(1, lanes).astype(jnp.float32)
    bias = after(bias, o_blocks[1])

    cosine, sine = rope_tables(positions.reshape(tokens), head_dim)
    normed_one, query_blocks, kv_own = project(
        meta, inputs, attn_gamma, bias, qkv, cosine, sine, (local_heads, kv_heads, head_dim, tps)
    )
    if ctxs == 2:
        kv_before = lax.ppermute(kv_own, "ctx", [(0, 1)])
        half = up_mine.shape[0] // 2
        up_near = links.to_x(
            after(lax.dynamic_slice_in_dim(up_mine, ctx * half, half, 0), pack_across)
        )
        up_far = links.to_y(after(up_near, kv_before))
    else:
        kv_before = lax.all_gather(
            kv_own.reshape(seq_count, block_len, kv_cols), "ctx", axis=1, tiled=True
        ).reshape(seq_count * block_len * ctxs, kv_cols)

    def swap(block_of):
        return [block_of(tp)] + [
            links.hop_tp(block_of((tp + hop) % tps), hop) for hop in range(1, tps)
        ]

    queries = jnp.stack(swap(lambda d: lax.dynamic_index_in_dim(query_blocks, d, 0, keepdims=False)))

    def gather_whole(*items):
        return lax.all_gather(after(jnp.stack(items), pack_across), "fsdp", axis=2, tiled=True)

    gate_down = gather_whole(gate_weight.T, down_weight)
    o_blocks = o_blocks[:2] + [after(item, kv_own) for item in o_blocks[2:]]
    o_wide = jnp.concatenate(o_blocks, axis=0)
    q_blocks = links.gather_tp(after(query_weight, queries))
    if ctxs == 2:
        o_near = links.to_x(lax.dynamic_slice_in_dim(o_wide, ctx * (depth // 2), depth // 2, 0))
        o_far = links.to_y(after(o_near, kv_before))
    else:
        o_near = o_far = links.to_x(o_wide)
    o_core = links.to_core(after(o_wide, queries))

    late_cot = after(cotangent, kv_own)
    cot_all = jnp.concatenate([block_rows(late_cot, hop) for hop in range(tps)], axis=0)
    one_all = jnp.concatenate(
        [block_rows(normed_one.reshape(seq_count, block_len, width), hop) for hop in range(tps)], axis=0
    )

    order = jnp.tile(jnp.arange(own, dtype=jnp.int32), depth // head_dim // kv_heads)[None]
    order = after(order, (cot_all, one_all, q_blocks[1], *([up_near] if ctxs == 2 else [])))
    sizes = (seq_count, kv_heads, head_dim, tps)
    mixed, lse = attend(meta, queries, kv_before, kv_own, order, key_block, sizes)
    o_core_near, o_core_far = (
        links.to_core(after(item, (mixed, q_blocks[2]))) for item in (o_near, o_far)
    )
    o_parts = (o_wide, o_core, o_near, o_far, o_core_near, o_core_far)
    hidden, normed_two = merge(meta, mixed, inputs, o_parts, mlp_gamma, tps)
    two_blocks = [normed_two, links.hop_tp(after(normed_two, q_blocks[-1]))]
    if ctxs == 2:
        up_cores = [links.to_core(after(item, mixed)) for item in (up_mine, up_near)]
        up_cores.append(links.to_core(after(up_far, normed_two)))
        up_full = assemble(meta, up_mine, up_near, up_far, *up_cores)[None]
    else:
        up_full = gather_whole(up_mine)

    two_blocks.append(links.hop_tp(after(two_blocks[-1], (gate_down, up_full))))
    two_blocks.append(links.hop_tp(two_blocks[-1]))
    kept, two_parts, mixed_parts, two_total = None, [], [], None
    for hop in range(tps):
        block = two_blocks[hop]
        if hop + 1 < tps:
            block = after(block, two_blocks[hop + 1])
        if two_total is not None:
            block = after(block, two_total)
        kept, two_part, mixed_part = feed(
            meta, block, cot_all, gate_down, up_full, hop, tps, kept
        )
        two_parts.append(two_part)
        mixed_parts.append(mixed_part)
        if hop == 0:
            q_wide = jnp.concatenate(q_blocks, axis=1)
            q_full = lax.all_gather(q_wide, "fsdp", axis=0, tiled=True)
        if hop >= 1:
            two_total = two_part if hop == 1 else add_low(two_part, two_got)
            two_got = links.hop_tp(two_total)
        two_total = two_total if hop >= 2 else None
    two_own = two_parts[0]
    act_all, gate_all, up_all, two_all = kept
    down_term = inner_rows(cot_all, after(act_all, two_total)).astype(LOW)
    two_got = after(two_got, down_term)

    hidden_grad, branch_grad, attended_grad, mlp_term = turn(
        meta, two_own, two_got, hidden, cotangent, o_parts, mlp_gamma, depth, tps
    )
    mixed_got = links.hop_tp(after(mixed_parts[1], two_got))
    q_grads, kv_parts, token = [], [], two_got
    for s in seqs:
        q_grad, grad_before, grad_own = attend_back(
            meta, s, queries, kv_before, kv_own, order, mixed, attended_grad, after(lse, token),
            cosine, sine, key_block, sizes,
        )
        q_grads.append(q_grad)
        if ctxs == 2:
            kv_parts.append((grad_own, lax.ppermute(grad_before, "ctx", [(1, 0)])))
        else:
            wide_grad = lax.dynamic_update_slice_in_dim(grad_before, grad_own, ctx * block_len, 2)
            kv_parts.append((lax.psum_scatter(wide_grad, "ctx", scatter_dimension=2, tiled=True), None))
        token = (mixed_got, q_grad)
    mixed_got = links.hop_tp(add_low(mixed_parts[2], after(mixed_got, q_grads[0])))
    q_grad = jnp.concatenate(q_grads, axis=0)
    shares = swap(lambda d: lax.dynamic_slice_in_dim(q_grad, d * q_cols, q_cols, 1))
    mixed_next = add_low(mixed_parts[3], mixed_got)
    input_low, attn_term = finish(meta, after(q_grad, mixed_next), q_full, inputs, hidden_grad, attn_gamma, tps)
    output_pairs = links.pairs(inner_rows(mixed, after(branch_grad, q_grads[-1])).astype(LOW), 1)
    token = (mixed_got, input_low, kv_parts, shares, output_pairs)
    kv_parts = [
        mine if got is None else add_low(after(mine, token), got) for mine, got in kv_parts
    ]

    def kv_rows(hop):
        return jnp.stack(
            [
                lax.dynamic_slice_in_dim(kv_parts[s], place(s, links.at(hop)) * own, own, 2)
                for s in seqs
            ],
            axis=2,
        )

    def fsdp_rows(value, below):
        return jnp.concatenate(
            [item for j in range(fsdps) for item in (value[j * shard : (j + 1) * shard], below(j))], axis=0
        )

    def output_rows(hop):
        return lax.dynamic_slice_in_dim(output_part, links.at(hop) * q_cols, q_cols, 0)

    kv_mine, kv_next = kv_rows(0), kv_rows(1)
    mixed_got = links.hop_tp(after(mixed_next, shares))
    kv_got = links.hop_tp(after(kv_next, (input_low, output_pairs)))
    down_weight_grad = links.lay_weight(*links.reduce_weight(after(down_term, kv_next)))
    kv_next = add_low(kv_rows(2), kv_got)
    gate_term = inner_rows(two_all, after(gate_all, kv_next)).astype(LOW)

    in_blocks = [input_low, links.hop_tp(after(input_low, (mixed_got, kv_next, gate_term)))]
    kv_got = links.hop_tp(after(kv_next, mixed_got))
    gate_weight_grad = links.lay_weight(*links.reduce_weight(after(gate_term, mixed_got))).T
    output_both = links.scatter_core(after(output_pairs, mixed_got))
    up_term = inner_rows(two_all, after(up_all, mixed_got)).astype(LOW)
    kv_next = add_low(kv_rows(3), after(kv_got, up_term))
    out_low = hidden + mixed_parts[0].astype(jnp.float32) + mixed_got.astype(jnp.float32)
    out_low = lax.optimization_barrier(out_low.astype(LOW))

    out_blocks = [out_low, links.hop_tp(after(out_low, (in_blocks[1], kv_next)))]
    kv_got = links.hop_tp(after(kv_next, in_blocks[1]))
    up_part, up_got = links.reduce_weight(after(up_term, in_blocks[1]))
    output_part = links.scatter_x(after(output_both, in_blocks[1]), 1)
    grads_all = after(jnp.concatenate(shares, axis=0), kv_got)
    q_bias_row = jnp.sum(grads_all.astype(jnp.float32), axis=0, keepdims=True)
    q_below = jnp.pad(q_bias_row, ((0, 15), (0, 0))).astype(LOW)
    q_pairs = links.pairs(fsdp_rows(inner_rows(one_all, grads_all).astype(LOW), lambda j: q_below), 0)
    kv_grad, kv_term = kv_back(meta, kv_mine, kv_got, cosine, sine, qkv, inputs, tps)
    gain_terms = jnp.concatenate(
        [jnp.sum(attn_term, axis=0) + jnp.sum(kv_term, axis=0), jnp.sum(mlp_term, axis=0)], axis=1
    ).reshape(-1, kv_cols)
    gain_terms = jnp.pad(gain_terms, ((0, 16 - gain_terms.shape[0]), (0, 0))).astype(LOW)
    kv_blocks = [jnp.concatenate([kv_grad, gain_terms], axis=0)]

    in_blocks.append(links.hop_tp(after(in_blocks[1], (out_blocks[1], kv_blocks[0], q_pairs))))
    kv_blocks.append(links.hop_tp(after(kv_blocks[0], out_blocks[1])))
    q_both = links.scatter_core(after(q_pairs, out_blocks[1]))

    out_blocks.append(
        links.hop_tp(
            after(out_blocks[1], (in_blocks[2], kv_blocks[1], q_both))
        )
    )
    kv_blocks.append(links.hop_tp(after(kv_blocks[1], in_blocks[2])))
    q_part = links.scatter_x(after(q_both, in_blocks[2]), 0)
    output_got = links.hop_tp(after(output_rows(1), in_blocks[2]))
    output_next = add_low(output_rows(2), output_got)

    in_blocks.append(
        links.hop_tp(after(in_blocks[2], (out_blocks[2], kv_blocks[2], q_part, output_next)))
    )
    kv_blocks.append(links.hop_tp(after(kv_blocks[2], (out_blocks[2], down_weight_grad))))
    q_total = links.sum_ctx(after(q_part, out_blocks[2]))
    output_got = links.hop_tp(after(output_next, out_blocks[2]))
    output_next = add_low(output_rows(3), output_got)
    output_got = links.hop_tp(after(output_next, in_blocks[3]))
    output_sum = add_low(output_rows(0), output_got)
    own_tokens = seq_count * own
    kv_all = jnp.concatenate([item[:own_tokens] for item in kv_blocks], axis=0)
    gain_rows = sum(
        item[own_tokens : own_tokens + 2 * width // kv_cols].astype(jnp.float32) for item in kv_blocks
    ).reshape(2, width)
    kv_bias_row = jnp.sum(kv_all.astype(jnp.float32), axis=0, keepdims=True)

    def kv_below(j):
        gains = jnp.pad(gain_rows[:, j * shard : (j + 1) * shard], ((0, 0), (0, kv_cols - shard)))
        return jnp.pad(jnp.concatenate([gains, kv_bias_row], axis=0), ((0, 13), (0, 0))).astype(LOW)

    kv_pairs = links.pairs(fsdp_rows(inner_rows(one_all, kv_all).astype(LOW), kv_below), 0)

    out_blocks.append(
        links.hop_tp(
            after(out_blocks[2], (in_blocks[3], kv_pairs))
        )
    )
    kv_both = links.scatter_core(kv_pairs)
    output_weight_grad = links.sum_ctx(output_sum)
    input_grad = last(meta, in_blocks, kv_blocks, qkv, inputs, attn_gamma)
    kv_part = links.scatter_x(after(kv_both, (in_blocks[3], gate_weight_grad)), 0)
    up_part = after(up_part, (input_grad, out_blocks[3]))
    up_weight_grad = links.lay_weight(up_part, up_got).T
    out_blocks[0] = after(out_blocks[0], (output_sum, q_total))
    kv_total = links.sum_ctx(after(kv_part, input_grad))
    outputs = spread_out(meta, out_blocks, seq_count, LOW)
    query_weight_grad = q_total[:shard]
    part = head_dim // fsdps
    query_bias_grad = lax.dynamic_slice_in_dim(
        q_total[shard].reshape(local_heads, head_dim), fsdp * part, part, 1
    )
    kv_weight = kv_total[:shard]
    gains = kv_total[shard : shard + 2, :shard]
    kv_bias = kv_total[shard + 2].reshape(2, kv_heads, head_dim)
    kv_bias = lax.dynamic_slice_in_dim(kv_bias, fsdp * part, part, 2)
    half = kv_cols // 2

    return (
        outputs,
        input_grad,
        gains[0],
        query_weight_grad,
        query_bias_grad,
        kv_weight[:, :half],
        kv_bias[0],
        kv_weight[:, half:],
        kv_bias[1],
        output_weight_grad,
        gains[1],
        gate_weight_grad,
        up_weight_grad,
        down_weight_grad,
    )


def solution(mesh):
    in_specs = (
        P("fsdp", "ctx", None),
        P("fsdp", "ctx", None),
        P("fsdp", "ctx"),
        P("fsdp"),
        P("fsdp", "tp"),
        P("tp", "fsdp"),
        P("fsdp", None),
        P(None, "fsdp"),
        P("fsdp", None),
        P(None, "fsdp"),
        P("tp", "fsdp"),
        P("fsdp"),
        P("fsdp", "tp"),
        P("fsdp", "tp"),
        P("tp", "fsdp"),
    )
    out_specs = (
        P("fsdp", "ctx", None),
        P("fsdp", "ctx", None),
        P("fsdp"),
        P("fsdp", "tp"),
        P("tp", "fsdp"),
        P("fsdp", None),
        P(None, "fsdp"),
        P("fsdp", None),
        P(None, "fsdp"),
        P("tp", "fsdp"),
        P("fsdp"),
        P("fsdp", "tp"),
        P("fsdp", "tp"),
        P("tp", "fsdp"),
    )
    return jax.shard_map(local, mesh=mesh, in_specs=in_specs, out_specs=out_specs, check_vma=False)
```

```python
import functools
import math

import jax
import jax.numpy as jnp
from jax import lax
from jax.experimental import pallas as pl
from jax.experimental.pallas import tpu as pltpu
from jax.sharding import PartitionSpec as P

EPS = 1e-06
THETA = 1000000.0
LOG2E = 1.0 / math.log(2.0)
LOW = jnp.bfloat16
MASKED = -1e30
MIB = 1024 * 1024


def rope_tables(position, width):
    half = width // 2
    freqs = jnp.exp(jnp.arange(half, dtype=jnp.float32) * (-2.0 * math.log(THETA) / width))
    angle = position.astype(jnp.float32)[..., None] * freqs
    cosine, sine = jnp.cos(angle), jnp.sin(angle)
    return (
        jnp.concatenate([cosine, cosine], axis=-1),
        jnp.concatenate([-sine, sine], axis=-1),
    )


def dot(left, right):
    return jnp.dot(left, right, preferred_element_type=jnp.float32)


def inner_rows(left, right):
    return lax.dot_general(
        left, right, (((0,), (0,)), ((), ())), preferred_element_type=jnp.float32
    )


def inner_cols(left, right):
    return lax.dot_general(
        left, right, (((1,), (1,)), ((), ())), preferred_element_type=jnp.float32
    )


def add_low(left, right):
    return (left.astype(jnp.float32) + right.astype(jnp.float32)).astype(LOW)


def after(value, token):
    return lax.optimization_barrier((value, token))[0]


def root_of(values):
    return lax.rsqrt(jnp.mean(values * values, axis=-1, keepdims=True) + EPS)


FSDP, TP, CTX, BEFORE, PLACE = 0, 1, 2, 3, 4


def shard_at(meta, flip, size):
    return pl.multiple_of(jnp.bitwise_xor(meta[FSDP], flip) * size, size)


def tp_at(meta, hop, tps, size):
    return pl.multiple_of(lax.rem(meta[TP] + tps - hop, tps) * size, size)


def call(kernel, grid, in_specs, out_specs, out_shape, scratch=(), cost=None, name=None, vmem=48):
    return pl.pallas_call(
        kernel,
        grid_spec=pltpu.PrefetchScalarGridSpec(
            num_scalar_prefetch=1,
            grid=grid,
            in_specs=in_specs,
            out_specs=out_specs,
            scratch_shapes=list(scratch),
        ),
        out_shape=out_shape,
        compiler_params=pltpu.CompilerParams(vmem_limit_bytes=vmem * MIB),
        cost_estimate=cost,
        name=name,
    )


def whole(array):
    return pl.BlockSpec(array.shape, lambda *_: (0,) * array.ndim)


def shape(dims, kind):
    return jax.ShapeDtypeStruct(dims, kind)


def project_kernel(
    local_heads, kv_heads, head_dim, meta, x_ref, gain_ref, bias_ref, *refs
):
    weights, (cos_ref, sin_ref, n_ref, q_ref, kv_ref) = refs[:4], refs[4:]
    rows = x_ref.shape[1]
    size = n_ref.shape[1] // 4
    values = x_ref[...].reshape(rows, -1).astype(jnp.float32)
    n_ref[...] = (values * root_of(values) * gain_ref[...]).astype(LOW)
    lin = bias_ref[...]
    for flip, weight in enumerate(weights):
        lin = lin + dot(n_ref[:, pl.ds(shard_at(meta, flip, size), size)], weight[:size, :])
    cosine, sine = cos_ref[...], sin_ref[...]
    for head in range(local_heads + 2 * kv_heads):
        part = lin[:, head * head_dim : (head + 1) * head_dim]
        if head < local_heads + kv_heads:
            part = part * cosine + pltpu.roll(part, head_dim // 2, 1) * sine
        if head < local_heads:
            q_ref[0, :, head * head_dim : (head + 1) * head_dim] = part.astype(LOW)
        else:
            at = (head - local_heads) * head_dim
            kv_ref[:, at : at + head_dim] = part.astype(LOW)


def project(meta, inputs, gain, bias, weights, cosine, sine, sizes):
    seq_count, block_len, width = inputs.shape
    local_heads, kv_heads, head_dim, tps = sizes
    own = block_len // tps
    q_cols, kv_cols = local_heads * head_dim, 2 * kv_heads * head_dim

    def row(i, m):
        return (i, 0)

    def device(i, m):
        seq, place = i // tps, i % tps
        return jnp.where(seq % 2 == 0, place, tps - 1 - place), seq, 0

    tokens = seq_count * block_len
    return call(
        functools.partial(project_kernel, local_heads, kv_heads, head_dim),
        (seq_count * tps,),
        [
            pl.BlockSpec((1, own, width), lambda i, m: (i // tps, i % tps, 0)),
            whole(gain), whole(bias), *(whole(w) for w in weights),
            pl.BlockSpec((own, head_dim), row), pl.BlockSpec((own, head_dim), row),
        ],
        [
            pl.BlockSpec((own, width), row),
            pl.BlockSpec((1, own, q_cols), device),
            pl.BlockSpec((own, kv_cols), row),
        ],
        [
            shape((tokens, width), LOW),
            shape((tps, seq_count * own, q_cols), LOW),
            shape((tokens, kv_cols), LOW),
        ],
        cost=pl.CostEstimate(
            flops=2 * tokens * width * (q_cols + kv_cols), bytes_accessed=8 * tokens * width, transcendentals=0
        ),
        name="project",
    )(meta, inputs, gain, bias, *weights, cosine, sine)


def half_block(block, own):
    return block // 2 if block // 2 % own == 0 else block


def fwd_kernel(
    heads, block, parts, meta, *refs
):
    q_refs, (kb_ref, vb_ref, k_ref, v_ref, order_ref, o_ref, lse_ref, qg_ref, acc_ref, m_ref, l_ref) = (
        refs[:parts], refs[parts:]
    )
    own, cols = q_refs[0].shape[1:]
    head_dim = acc_ref.shape[0]
    scale = LOG2E / math.sqrt(head_dim)
    each = cols // head_dim
    for head in range(heads):
        qg_ref[head * own : (head + 1) * own, :] = q_refs[head // each][
            0, :, (head % each) * head_dim : (head % each + 1) * head_dim
        ]
    acc_ref[...] = jnp.zeros_like(acc_ref)
    m_ref[...] = jnp.full_like(m_ref, MASKED)
    l_ref[...] = jnp.zeros_like(l_ref)
    first = meta[PLACE + pl.program_id(0)] * own

    def step(key_ref, value_ref, start, size, masked):
        keys = key_ref[pl.ds(start, size), :]
        values = value_ref[pl.ds(start, size), :]
        logits = inner_cols(keys, qg_ref[...]) * scale
        if masked:
            key_order = (start - first) + lax.broadcasted_iota(jnp.int32, logits.shape, 0)
            logits = jnp.where(key_order <= order_ref[...], logits, MASKED)
        before = m_ref[...]
        peak = jnp.maximum(before, jnp.max(logits, axis=0, keepdims=True))
        weights = jnp.exp2(logits - peak)
        fade = jnp.exp2(before - peak)
        m_ref[...] = peak
        l_ref[...] = l_ref[...] * fade + jnp.sum(weights, axis=0, keepdims=True)
        acc_ref[...] = acc_ref[...] * fade + inner_rows(values, weights.astype(LOW))

    def early(index, carry):
        step(kb_ref, vb_ref, pl.multiple_of(index * block, block), block, False)
        return carry

    lax.fori_loop(0, meta[BEFORE], early, 0)
    short = half_block(block, own)

    @pl.when(first < short)
    def _():
        step(k_ref, v_ref, 0, short, True)

    @pl.when(first >= short)
    def _():
        step(k_ref, v_ref, 0, block, True)

    total = l_ref[...]
    lse_ref[...] = (m_ref[...] + jnp.log2(total)).reshape(lse_ref.shape)
    mixed = jnp.transpose(acc_ref[...] / total)
    for head in range(heads):
        o_ref[:, head * head_dim : (head + 1) * head_dim] = mixed[
            head * own : (head + 1) * own, :
        ].astype(LOW)


def bwd_kernel(heads, block, parts, seq, meta, *refs):
    q_refs, (
        kb_ref, vb_ref, k_ref, v_ref, order_ref, o_ref, g_ref, lse_ref, cos_ref, sin_ref,
        dq_ref, db_ref, dd_ref, qg_ref, gg_ref, both_ref, acc_ref,
    ) = refs[:parts], refs[parts:]
    own, cols = q_refs[0].shape[1:]
    head_dim = acc_ref.shape[0]
    scale = 1.0 / math.sqrt(head_dim)
    each = cols // head_dim
    for head in range(heads):
        rows = slice(head * own, (head + 1) * own)
        at = slice(head * head_dim, (head + 1) * head_dim)
        qg_ref[rows, :] = q_refs[head // each][
            0, :, (head % each) * head_dim : (head % each + 1) * head_dim
        ]
        gg_ref[rows, :] = g_ref[:, at]
        both_ref[rows, :] = g_ref[:, at].astype(jnp.float32) * o_ref[:, at].astype(jnp.float32)
    center = jnp.sum(jnp.transpose(both_ref[...]), axis=0, keepdims=True)
    acc_ref[...] = jnp.zeros_like(acc_ref)
    lse = lse_ref[...].reshape(order_ref.shape)
    first = meta[PLACE + seq] * own

    def step(key_ref, value_ref, out_ref, start, size, masked):
        keys = key_ref[pl.ds(start, size), :]
        values = value_ref[pl.ds(start, size), :]
        logits = inner_cols(keys, qg_ref[...]) * (scale * LOG2E)
        if masked:
            key_order = (start - first) + lax.broadcasted_iota(jnp.int32, logits.shape, 0)
            logits = jnp.where(key_order <= order_ref[...], logits, MASKED)
        probs = jnp.exp2(logits - lse)
        out_ref[1, 0, pl.ds(start, size), :] = dot(probs.astype(LOW), gg_ref[...]).astype(LOW)
        prob_grad = inner_cols(values, gg_ref[...])
        logit_grad = (probs * (prob_grad - center)).astype(LOW)
        out_ref[0, 0, pl.ds(start, size), :] = (dot(logit_grad, qg_ref[...]) * scale).astype(LOW)
        acc_ref[...] += inner_rows(keys, logit_grad)

    def early(index, carry):
        step(kb_ref, vb_ref, db_ref, pl.multiple_of(index * block, block), block, False)
        return carry

    def clear(ref):
        def body(index, carry):
            start = pl.multiple_of(index * block, block)
            ref[:, :, pl.ds(start, block), :] = jnp.zeros((2, 1, block, head_dim), LOW)
            return carry

        return body

    lax.fori_loop(0, meta[BEFORE], early, 0)
    lax.fori_loop(meta[BEFORE], kb_ref.shape[0] // block, clear(db_ref), 0)
    short = half_block(block, own)

    @pl.when(first < short)
    def _():
        step(k_ref, v_ref, dd_ref, 0, short, True)
        if short < block:
            dd_ref[:, :, short:, :] = jnp.zeros((2, 1, block - short, head_dim), LOW)

    @pl.when(first >= short)
    def _():
        step(k_ref, v_ref, dd_ref, 0, block, True)

    both_ref[...] = jnp.transpose(acc_ref[...])
    for head in range(heads):
        grad = both_ref[head * own : (head + 1) * own, :] * scale
        grad = grad * cos_ref[...] - pltpu.roll(grad, head_dim // 2, 1) * sin_ref[...]
        dq_ref[:, head * head_dim : (head + 1) * head_dim] = grad.astype(LOW)


def attention_specs(queries, kv_before, kv_own, sizes, seq=None):
    seq_count, kv_heads, head_dim, tps = sizes
    rows = queries.shape[1] // seq_count
    parts = tps // kv_heads
    heads = queries.shape[2] * parts // head_dim
    before, block_len = kv_before.shape[0] // seq_count, kv_own.shape[0] // seq_count

    def spec(dims, index):
        if seq is None:
            return pl.BlockSpec(dims, index)
        return pl.BlockSpec(dims, lambda g, m: index(seq, g, m))

    def piece(part):
        return spec(
            (1, rows, queries.shape[2]),
            lambda s, g, m: (lax.rem(m[TP] + tps - (g * parts + part), tps), s, 0),
        )

    specs = [piece(part) for part in range(parts)] + [
        spec((before, head_dim), lambda s, g, m: (s, g)),
        spec((before, head_dim), lambda s, g, m: (s, kv_heads + g)),
        spec((block_len, head_dim), lambda s, g, m: (s, g)),
        spec((block_len, head_dim), lambda s, g, m: (s, kv_heads + g)),
        spec((1, heads * rows), lambda s, g, m: (0, 0)),
    ]
    return specs, rows, parts, heads, before, block_len


def attend(meta, queries, kv_before, kv_own, order, block, sizes):
    seq_count, kv_heads, head_dim, tps = sizes
    specs, rows, parts, heads, before, block_len = attention_specs(queries, kv_before, kv_own, sizes)
    width, wide = kv_heads * heads * head_dim, heads * rows
    work = seq_count * rows * width * (before + block_len)
    return call(
        functools.partial(fwd_kernel, heads, block, parts),
        (seq_count, kv_heads),
        specs,
        [
            pl.BlockSpec((rows, heads * head_dim), lambda s, g, m: (s, g)),
            pl.BlockSpec((1, 1, 1, wide), lambda s, g, m: (s, g, 0, 0)),
        ],
        [shape((seq_count * rows, width), LOW), shape((seq_count, kv_heads, 1, wide), jnp.float32)],
        [
            pltpu.VMEM((wide, head_dim), LOW),
            pltpu.VMEM((head_dim, wide), jnp.float32),
            pltpu.VMEM((1, wide), jnp.float32),
            pltpu.VMEM((1, wide), jnp.float32),
        ],
        cost=pl.CostEstimate(flops=8 * work, bytes_accessed=1 << 22, transcendentals=0),
        name="attend",
    )(meta, *([queries] * parts), kv_before, kv_before, kv_own, kv_own, order)


def attend_back(
    meta, seq, queries, kv_before, kv_own, order, mixed, grads, lse, cosine, sine, block, sizes
):
    seq_count, kv_heads, head_dim, tps = sizes
    specs, rows, parts, heads, before, block_len = attention_specs(
        queries, kv_before, kv_own, sizes, seq
    )
    width, wide = kv_heads * heads * head_dim, heads * rows
    work = rows * width * (before + block_len)
    wide_spec = pl.BlockSpec((rows, heads * head_dim), lambda g, m: (seq, g))
    table_spec = pl.BlockSpec((rows, head_dim), lambda g, m: (seq * tps + m[PLACE + seq], 0))
    return call(
        functools.partial(bwd_kernel, heads, block, parts, seq),
        (kv_heads,),
        specs
        + [
            wide_spec,
            wide_spec,
            pl.BlockSpec((1, 1, 1, wide), lambda g, m: (seq, g, 0, 0)),
            table_spec,
            table_spec,
        ],
        [
            pl.BlockSpec((rows, heads * head_dim), lambda g, m: (0, g)),
            pl.BlockSpec((2, 1, before, head_dim), lambda g, m: (0, g, 0, 0)),
            pl.BlockSpec((2, 1, block_len, head_dim), lambda g, m: (0, g, 0, 0)),
        ],
        [
            shape((rows, width), LOW),
            shape((2, kv_heads, before, head_dim), LOW),
            shape((2, kv_heads, block_len, head_dim), LOW),
        ],
        [
            pltpu.VMEM((wide, head_dim), LOW),
            pltpu.VMEM((wide, head_dim), LOW),
            pltpu.VMEM((wide, head_dim), jnp.float32),
            pltpu.VMEM((head_dim, wide), jnp.float32),
        ],
        cost=pl.CostEstimate(flops=16 * work, bytes_accessed=1 << 22, transcendentals=0),
        name="attend_back",
    )(
        meta, *([queries] * parts), kv_before, kv_before, kv_own, kv_own, order,
        mixed, grads, lse, cosine, sine,
    )


def output_pieces(meta, weights, tps):
    own, other, near, far, other_near, other_far = weights
    depth, half = own.shape[0], near.shape[0]
    low = pl.multiple_of(meta[CTX] * (depth - half), 128)
    high = pl.multiple_of((1 - meta[CTX]) * (depth - half), 128)
    pieces = [(0, None, own), (1, None, other)]
    if half == depth:
        return pieces + [(2, None, near), (3, None, other_near)]
    return pieces + [(2, low, near), (2, high, far), (3, low, other_near), (3, high, other_far)]


def merge_kernel(tps, meta, o_ref, x_ref, *refs):
    weights, (gain_ref, h_ref, n_ref, turned_ref) = refs[:6], refs[6:]
    rows, width = h_ref.shape
    size, depth = width // 4, o_ref.shape[1]
    part = depth // tps
    for hop in range(tps):
        turned_ref[:, hop * part : (hop + 1) * part] = o_ref[:, pl.ds(tp_at(meta, hop, tps, part), part)]
    h_ref[...] = x_ref[...].reshape(rows, width).astype(jnp.float32)
    for flip, first, weight in output_pieces(meta, weights, tps):
        left = turned_ref[...] if first is None else turned_ref[:, pl.ds(first, weight.shape[0])]
        h_ref[:, pl.ds(shard_at(meta, flip, size), size)] += dot(left, weight[...])
    hidden = h_ref[...]
    n_ref[...] = (hidden * root_of(hidden) * gain_ref[...]).astype(LOW)


def merge(meta, mixed, inputs, weights, gain, tps):
    seq_count, block_len, width = inputs.shape
    own = block_len // tps
    depth = mixed.shape[1]
    row = pl.BlockSpec((own, width), lambda s, m: (s, 0))
    return call(
        functools.partial(merge_kernel, tps),
        (seq_count,),
        [
            pl.BlockSpec((own, depth), lambda s, m: (s, 0)),
            pl.BlockSpec((1, own, width), lambda s, m: (s, m[PLACE + s], 0)),
            *(whole(w) for w in weights),
            whole(gain),
        ],
        [row, row],
        [shape((seq_count * own, width), jnp.float32), shape((seq_count * own, width), LOW)],
        [pltpu.VMEM((own, depth), LOW)],
        cost=pl.CostEstimate(
            flops=2 * seq_count * own * depth * width, bytes_accessed=1 << 23, transcendentals=0
        ),
        name="merge",
    )(meta, mixed, inputs, *weights, gain)


def turn_kernel(
    tps, meta, a_ref, b_ref, h_ref, c_ref, *refs,
):
    weights, (gain_ref, hg_ref, bg_ref, ag_ref, term_ref, turned_ref) = refs[:6], refs[6:]
    rows, width = h_ref.shape
    size, depth = width // 4, ag_ref.shape[1]
    two_grad = a_ref[...].astype(jnp.float32) + b_ref[...].astype(jnp.float32)
    hidden = h_ref[...]
    root = root_of(hidden)
    term_ref[...] = jnp.sum(two_grad * hidden * root, axis=0, keepdims=True).reshape(term_ref.shape)
    scaled = gain_ref[...] * two_grad
    grad = (
        c_ref[...].reshape(rows, width).astype(jnp.float32)
        + root * scaled
        - hidden * root**3 * jnp.mean(scaled * hidden, axis=-1, keepdims=True)
    )
    hg_ref[...] = grad
    bg_ref[...] = grad.astype(LOW)
    turned_ref[...] = jnp.zeros_like(turned_ref)
    for flip, first, weight in output_pieces(meta, weights, tps):
        at = slice(None) if first is None else pl.ds(first, weight.shape[0])
        turned_ref[:, at] += inner_cols(bg_ref[:, pl.ds(shard_at(meta, flip, size), size)], weight[...])
    part = depth // tps
    for hop in range(tps):
        ag_ref[:, pl.ds(tp_at(meta, hop, tps, part), part)] = turned_ref[
            :, hop * part : (hop + 1) * part
        ].astype(LOW)


def turn(meta, two_own, two_got, hidden, cotangent, weights, gain, depth, tps):
    seq_count, block_len, width = cotangent.shape
    own = block_len // tps
    row = pl.BlockSpec((own, width), lambda s, m: (s, 0))
    tokens = seq_count * own
    return call(
        functools.partial(turn_kernel, tps),
        (seq_count,),
        [
            row, row, row,
            pl.BlockSpec((1, own, width), lambda s, m: (s, m[PLACE + s], 0)),
            *(whole(w) for w in weights),
            whole(gain),
        ],
        [
            row, row,
            pl.BlockSpec((own, depth), lambda s, m: (s, 0)),
            pl.BlockSpec((1, 1, width), lambda s, m: (s, 0, 0)),
        ],
        [
            shape((tokens, width), jnp.float32),
            shape((tokens, width), LOW),
            shape((tokens, depth), LOW),
            shape((seq_count, 1, width), jnp.float32),
        ],
        [pltpu.VMEM((own, depth), jnp.float32)],
        cost=pl.CostEstimate(flops=2 * tokens * depth * width, bytes_accessed=1 << 23, transcendentals=0),
        name="turn",
    )(meta, two_own, two_got, hidden, cotangent, *weights, gain)


def back_through_norm(grad, values, gain):
    root = root_of(values)
    scaled = gain * grad
    term = jnp.sum(grad * values * root, axis=0, keepdims=True)
    return root * scaled - values * root**3 * jnp.mean(scaled * values, axis=-1, keepdims=True), term


def finish_kernel(tps, meta, g_ref, q_ref, x_ref, hg_ref, gain_ref, out_ref, term_ref, turned_ref):
    part = g_ref.shape[1] // tps
    for hop in range(tps):
        turned_ref[:, hop * part : (hop + 1) * part] = g_ref[:, pl.ds(tp_at(meta, hop, tps, part), part)]
    values = x_ref[...].reshape(hg_ref.shape).astype(jnp.float32)
    part, term = back_through_norm(inner_cols(turned_ref[...], q_ref[...]), values, gain_ref[...])
    term_ref[...] = term.reshape(term_ref.shape)
    out_ref[...] = (hg_ref[...] + part).astype(LOW)


def finish(meta, q_grad, q_full, inputs, hidden_grad, gain, tps):
    seq_count, block_len, width = inputs.shape
    own = block_len // tps
    tokens = seq_count * own
    row = pl.BlockSpec((own, width), lambda s, m: (s, 0))
    return call(
        functools.partial(finish_kernel, tps),
        (seq_count,),
        [
            pl.BlockSpec((own, q_grad.shape[1]), lambda s, m: (s, 0)),
            whole(q_full),
            pl.BlockSpec((1, own, width), lambda s, m: (s, m[PLACE + s], 0)),
            row,
            whole(gain),
        ],
        [row, pl.BlockSpec((1, 1, width), lambda s, m: (s, 0, 0))],
        [shape((tokens, width), LOW), shape((seq_count, 1, width), jnp.float32)],
        [pltpu.VMEM((own, q_grad.shape[1]), LOW)],
        cost=pl.CostEstimate(
            flops=2 * tokens * q_grad.shape[1] * width, bytes_accessed=1 << 23, transcendentals=0
        ),
        name="finish",
    )(meta, q_grad, q_full, inputs, hidden_grad, gain)


def one_from_kv(meta, kv_grad, weights, one_ref):
    size = one_ref.shape[1] // 4
    skip = weights[0].shape[1] - kv_grad.shape[1]
    for flip, weight in enumerate(weights):
        one_ref[:, pl.ds(shard_at(meta, flip, size), size)] = inner_cols(
            kv_grad, weight[:size, skip:]
        )
    return one_ref[...]


def kv_kernel(kv_heads, head_dim, meta, a_ref, b_ref, cos_ref, sin_ref, *refs):
    weights, (x_ref, kv_ref, term_ref, one_ref) = refs[:4], refs[4:]
    cosine, sine = cos_ref[...], sin_ref[...]
    for kind in range(2):
        for head in range(kv_heads):
            grad = (
                a_ref[kind, head, 0].astype(jnp.float32) + b_ref[kind, head, 0].astype(jnp.float32)
            )
            if kind == 0:
                grad = grad * cosine - pltpu.roll(grad, head_dim // 2, 1) * sine
            at = (kind * kv_heads + head) * head_dim
            kv_ref[:, at : at + head_dim] = grad.astype(LOW)
    one = one_from_kv(meta, kv_ref[...], weights, one_ref)
    values = x_ref[...].reshape(one.shape).astype(jnp.float32)
    term = jnp.sum(one * values * root_of(values), axis=0, keepdims=True)
    term_ref[...] = term.reshape(term_ref.shape)


def kv_back(meta, kv_mine, kv_got, cosine, sine, weights, inputs, tps):
    seq_count, block_len, width = inputs.shape
    own = block_len // tps
    kv_heads, head_dim = kv_mine.shape[1], kv_mine.shape[4]
    kv_cols = 2 * kv_heads * head_dim
    kv_spec = pl.BlockSpec((2, kv_heads, 1, own, head_dim), lambda s, m: (0, 0, s, 0, 0))
    table_spec = pl.BlockSpec((own, head_dim), lambda s, m: (s * tps + m[PLACE + s], 0))
    return call(
        functools.partial(kv_kernel, kv_heads, head_dim),
        (seq_count,),
        [
            kv_spec, kv_spec, table_spec, table_spec,
            *(whole(w) for w in weights),
            pl.BlockSpec((1, own, width), lambda s, m: (s, m[PLACE + s], 0)),
        ],
        [
            pl.BlockSpec((own, kv_cols), lambda s, m: (s, 0)),
            pl.BlockSpec((1, 1, width), lambda s, m: (s, 0, 0)),
        ],
        [shape((seq_count * own, kv_cols), LOW), shape((seq_count, 1, width), jnp.float32)],
        [pltpu.VMEM((own, width), jnp.float32)],
        cost=pl.CostEstimate(
            flops=2 * seq_count * own * kv_cols * width, bytes_accessed=1 << 22, transcendentals=0
        ),
        name="kv_back",
    )(meta, kv_mine, kv_got, cosine, sine, *weights, inputs)


def last_kernel(tps, meta, *refs):
    blocks, kvs, weights = refs[:tps], refs[tps : 2 * tps], refs[2 * tps : 2 * tps + 4]
    x_ref, gain_ref, out_ref, one_ref = refs[2 * tps + 4 :]
    seq = pl.program_id(0)
    own = blocks[0].shape[0]
    for hop in range(tps):
        device = lax.rem(meta[TP] + tps - hop, tps)
        place = jnp.where(seq % 2 == 0, device, tps - 1 - device)
        at = pl.ds(pl.multiple_of(place * own, own), own)
        one = one_from_kv(meta, kvs[hop][...], weights, one_ref)
        values = x_ref[0, at, :].astype(jnp.float32)
        part, _ = back_through_norm(one, values, gain_ref[...])
        out_ref[0, at, :] = blocks[hop][...].astype(jnp.float32) + part


def last(meta, blocks, kvs, weights, inputs, gain):
    seq_count, block_len, width = inputs.shape
    tps = len(blocks)
    own = block_len // tps
    every = pl.BlockSpec((1, block_len, width), lambda s, m: (s, 0, 0))
    return call(
        functools.partial(last_kernel, tps),
        (seq_count,),
        [pl.BlockSpec((own, width), lambda s, m: (s, 0))] * tps
        + [pl.BlockSpec((own, kvs[0].shape[1]), lambda s, m: (s, 0))] * tps
        + [whole(w) for w in weights]
        + [every, whole(gain)],
        every,
        shape(inputs.shape, jnp.float32),
        [pltpu.VMEM((own, width), jnp.float32)],
        cost=pl.CostEstimate(
            flops=2 * seq_count * block_len * kvs[0].shape[1] * width, bytes_accessed=1 << 24, transcendentals=0
        ),
        name="last",
    )(meta, *blocks, *kvs, *weights, inputs, gain)


def feed_kernel(first, hidden, *refs):
    n_ref, c_ref, wg_ref, wu_ref, wd_ref = refs[1:6]
    act_ref, gg_ref, ug_ref, all_ref, two_ref, mix_ref, two_acc, mix_acc = refs[6 if first else 10 :]
    step, tile = pl.program_id(0), wg_ref.shape[0]
    steps = -(-hidden // tile)

    def body(count):
        gate = inner_cols(n_ref[...], wg_ref[:count, :])
        up_part = inner_cols(n_ref[...], wu_ref[:count, :])
        act_grad = inner_cols(c_ref[...], wd_ref[:count, :])
        sigma = jax.nn.sigmoid(gate)
        silu = gate * sigma
        act = (silu * up_part).astype(LOW)
        gate_grad = (act_grad * up_part * (sigma * (1.0 + gate * (1.0 - sigma)))).astype(LOW)
        up_grad = (act_grad * silu).astype(LOW)
        act_ref[:, :count], gg_ref[:, :count], ug_ref[:, :count] = act, gate_grad, up_grad
        return (
            dot(gate_grad, wg_ref[:count, :]) + dot(up_grad, wu_ref[:count, :]),
            dot(act, wd_ref[:count, :]),
        )

    @pl.when(step == 0)
    def _():
        all_ref[...] = n_ref[...]
        two_acc[...], mix_acc[...] = body(tile)

    @pl.when(jnp.logical_and(step > 0, step < steps - 1))
    def _():
        two, mix = body(tile)
        two_acc[...] += two
        mix_acc[...] += mix

    @pl.when(step == steps - 1)
    def _():
        two, mix = body(hidden - (steps - 1) * tile)
        two_ref[...] = (two_acc[...] + two).astype(LOW)
        mix_ref[...] = (mix_acc[...] + mix).astype(LOW)


def feed(meta, normed, cots, gate_down, up, hop, tps, kept):
    rows, width = normed.shape
    hidden = up.shape[1]
    tile = 768
    assert hidden > tile
    gate_spec = pl.BlockSpec((None, tile, width), lambda j, m: (0, j, 0))
    down_spec = pl.BlockSpec((None, tile, width), lambda j, m: (1, j, 0))
    column = pl.BlockSpec((rows, tile), lambda j, m: (hop, j))
    fixed = pl.BlockSpec((rows, width), lambda j, m: (0, 0))
    first = hop == 0
    wide = shape((tps * rows, hidden), LOW)
    *hiddens, two_part, mixed_part = pl.pallas_call(
        functools.partial(feed_kernel, first, hidden),
        grid_spec=pltpu.PrefetchScalarGridSpec(
            num_scalar_prefetch=1,
            grid=(-(-hidden // tile),),
            in_specs=[fixed, pl.BlockSpec((rows, width), lambda j, m: (hop, 0)), gate_spec, gate_spec, down_spec]
            + ([] if first else [pl.BlockSpec(memory_space=pl.ANY)] * 4),
            out_specs=[
                column, column, column, pl.BlockSpec((rows, width), lambda j, m: (hop, 0)), fixed, fixed
            ],
            scratch_shapes=[pltpu.VMEM((rows, width), jnp.float32)] * 2,
        ),
        out_shape=[
            wide, wide, wide, shape((tps * rows, width), LOW),
            shape((rows, width), LOW), shape((rows, width), LOW),
        ],
        input_output_aliases={} if first else {6: 0, 7: 1, 8: 2, 9: 3},
        compiler_params=pltpu.CompilerParams(vmem_limit_bytes=56 * MIB),
        cost_estimate=pl.CostEstimate(
            flops=12 * rows * width * hidden, bytes_accessed=6 * width * hidden, transcendentals=rows * hidden
        ),
        name="feed",
    )(meta, normed, cots, gate_down, up, gate_down, *(() if first else kept))
    return hiddens, two_part, mixed_part


def assemble_kernel(tiles, meta, own_ref, near_ref, far_ref, o_own_ref, o_near_ref, o_far_ref, out_ref):
    size = own_ref.shape[1]
    is_near = (pl.program_id(0) // tiles) == meta[CTX]
    out_ref[:, pl.ds(shard_at(meta, 0, size), size)] = own_ref[...]
    out_ref[:, pl.ds(shard_at(meta, 1, size), size)] = o_own_ref[...]

    @pl.when(is_near)
    def _():
        out_ref[:, pl.ds(shard_at(meta, 2, size), size)] = near_ref[...]
        out_ref[:, pl.ds(shard_at(meta, 3, size), size)] = o_near_ref[...]

    @pl.when(jnp.logical_not(is_near))
    def _():
        out_ref[:, pl.ds(shard_at(meta, 2, size), size)] = far_ref[...]
        out_ref[:, pl.ds(shard_at(meta, 3, size), size)] = o_far_ref[...]


def assemble(meta, own, near, far, other, other_near, other_far):
    rows, size = own.shape
    tiles = 2 if rows % 64 == 0 else 1
    tile = rows // (2 * tiles)
    every = pl.BlockSpec((tile, size), lambda i, m: (i, 0))
    half = pl.BlockSpec((tile, size), lambda i, m: (i % tiles, 0))
    return call(
        functools.partial(assemble_kernel, tiles),
        (2 * tiles,),
        [every, half, half, every, half, half],
        pl.BlockSpec((tile, 4 * size), lambda i, m: (i, 0)),
        shape((rows, 4 * size), LOW),
        cost=pl.CostEstimate(flops=0, bytes_accessed=16 * rows * size, transcendentals=0),
        name="assemble",
    )(meta, own, near, far, other, other_near, other_far)


def lay_kernel(low_ref, high_ref, out_ref):
    both = jnp.concatenate([low_ref[...], high_ref[...]], axis=0)
    out_ref[...] = jnp.transpose(both.astype(jnp.float32))


def lay(low, high):
    rows, cols = low.shape
    return pl.pallas_call(
        lay_kernel,
        in_specs=[pl.BlockSpec(memory_space=pltpu.VMEM)] * 2,
        out_specs=pl.BlockSpec(memory_space=pltpu.VMEM),
        out_shape=shape((cols, 2 * rows), jnp.float32),
        compiler_params=pltpu.CompilerParams(vmem_limit_bytes=48 * MIB),
        cost_estimate=pl.CostEstimate(flops=0, bytes_accessed=12 * rows * cols, transcendentals=0),
        name="lay",
    )(low, high)


def spread_kernel(tps, meta, *refs):
    out_ref = refs[tps]
    seq_count = out_ref.shape[0]
    own = refs[0].shape[0] // seq_count
    for hop in range(tps):
        device = lax.rem(meta[TP] + tps - hop, tps)
        for s in range(seq_count):
            place = device if s % 2 == 0 else tps - 1 - device
            at = pl.ds(pl.multiple_of(place * own, own), own)
            out_ref[s, at, :] = refs[hop][s * own : (s + 1) * own, :].astype(out_ref.dtype)


def spread_out(meta, blocks, seq_count, kind):
    tps = len(blocks)
    rows, width = blocks[0].shape
    dims = (seq_count, rows // seq_count * tps, width)
    return call(
        functools.partial(spread_kernel, tps),
        (1,),
        [whole(item) for item in blocks],
        pl.BlockSpec(dims, lambda *_: (0, 0, 0)),
        shape(dims, kind),
        cost=pl.CostEstimate(flops=0, bytes_accessed=8 * rows * tps * width, transcendentals=0),
        name="spread",
    )(meta, *blocks)


class Links:
    def __init__(self):
        self.tp, self.ctx, self.fsdp = (lax.axis_index(a) for a in ("tp", "ctx", "fsdp"))
        self.tps, self.ctxs, self.fsdps = (lax.axis_size(a) for a in ("tp", "ctx", "fsdp"))
        self.core, self.x = self.fsdp % 2, self.fsdp // 2
        assert self.fsdps == 4

    def to_core(self, value):
        return lax.ppermute(value, "fsdp", [(0, 1), (1, 0), (2, 3), (3, 2)])

    def to_x(self, value):
        return lax.ppermute(value, "fsdp", [(0, 2), (2, 0), (1, 3), (3, 1)])

    def to_y(self, value):
        return lax.ppermute(value, "ctx", [(0, 1), (1, 0)])

    def hop_tp(self, value, hop=1):
        return lax.ppermute(value, "tp", [(i, (i + hop) % self.tps) for i in range(self.tps)])

    def gather_fsdp(self, shard):
        across = self.to_x(shard)
        return shard, across, self.to_core(jnp.concatenate([shard, across], axis=0))

    def gather_tp(self, block):
        blocks = [block]
        for _ in range(1, self.tps):
            blocks.append(self.hop_tp(blocks[-1]))
        return blocks

    def scatter_tp(self, blocks):
        total = blocks[1]
        for hop in range(1, self.tps):
            got = self.hop_tp(total)
            if hop < self.tps - 1:
                total = add_low(blocks[hop + 1], got)
        return blocks[0], got

    def at(self, hop):
        return (self.tp - hop + self.tps) % self.tps

    def pairs(self, value, axis):
        size = value.shape[axis] // 4

        def pair(core):
            return jnp.concatenate(
                [
                    lax.dynamic_slice_in_dim(value, (2 * x + core) * size, size, axis)
                    for x in range(2)
                ],
                axis,
            )

        return pair(self.core), pair(1 - self.core)

    def scatter_core(self, pairs):
        return add_low(pairs[0], self.to_core(pairs[1]))

    def scatter_x(self, both, axis):
        size = both.shape[axis] // 2
        away = lax.dynamic_slice_in_dim(both, (1 - self.x) * size, size, axis)
        keep = lax.dynamic_slice_in_dim(both, self.x * size, size, axis)
        return add_low(keep, self.to_x(away))

    def sum_ctx(self, value):
        value = lax.optimization_barrier(value.astype(LOW))
        if self.ctxs == 2:
            return value.astype(jnp.float32) + self.to_y(value).astype(jnp.float32)
        return lax.psum(value.astype(jnp.float32), "ctx")

    def reduce_weight(self, term):
        part = lax.psum_scatter(term, ("fsdp", "ctx"), scatter_dimension=0, tiled=True)
        if self.ctxs != 2:
            return lax.all_gather(part, "ctx", axis=0, tiled=True), None
        part = lax.optimization_barrier(part)
        return part, self.to_y(part)

    def lay_weight(self, part, got):
        if got is None:
            return part.astype(jnp.float32).T
        return lay(jnp.where(self.ctx == 0, part, got), jnp.where(self.ctx == 0, got, part))


def local(
    inputs,
    cotangent,
    positions,
    attn_gain,
    query_weight,
    query_bias,
    key_weight,
    key_bias,
    value_weight,
    value_bias,
    output_weight,
    mlp_gain,
    gate_weight,
    up_weight,
    down_weight,
):
    links = Links()
    seq_count, block_len, width = inputs.shape
    tp, tps, ctx, ctxs = links.tp, links.tps, links.ctx, links.ctxs
    fsdp, fsdps = links.fsdp, links.fsdps
    own = block_len // tps
    local_heads, kv_heads = query_bias.shape[0], key_bias.shape[0]
    head_dim = key_weight.shape[1] // kv_heads
    q_cols = local_heads * head_dim
    kv_cols = 2 * kv_heads * head_dim
    depth = q_cols * tps
    shard = width // fsdps
    tokens = seq_count * block_len
    key_block = block_len
    seqs = range(seq_count)

    def place(seq, device):
        return device if seq % 2 == 0 else tps - 1 - device

    def block_rows(value, hop):
        return jnp.concatenate(
            [
                lax.dynamic_slice_in_dim(value[s], place(s, links.at(hop)) * own, own, 0)
                for s in seqs
            ],
            axis=0,
        )

    meta = jnp.stack(
        [fsdp, tp, ctx, ctx * (block_len // key_block)] + [place(s, tp) for s in seqs]
    ).astype(jnp.int32)

    lanes = q_cols + kv_cols
    smalls = jnp.concatenate([b.reshape(-1) for b in (query_bias, key_bias, value_bias)])
    extra = jnp.stack(
        [jnp.pad(row, (0, lanes - row.shape[0])) for row in (attn_gain, mlp_gain, smalls)]
    )
    extra = jnp.pad(extra, ((0, 13), (0, 0)))
    pack = jnp.concatenate(
        [jnp.concatenate([query_weight, key_weight, value_weight], axis=1), extra], axis=0
    )
    pack_core, pack_across = links.to_core(pack), links.to_x(pack)
    qkv = pack, pack_core, pack_across, links.to_core(pack_across)
    o_blocks = links.gather_tp(output_weight)
    up_mine = up_weight.T

    rows = jnp.stack([item[shard : shard + 3] for item in qkv])
    rows = [
        lax.dynamic_index_in_dim(rows, jnp.bitwise_xor(fsdp, j), 0, keepdims=False) for j in range(4)
    ]
    attn_gamma = jnp.concatenate([r[0, :shard] for r in rows])[None].astype(jnp.float32)
    mlp_gamma = jnp.concatenate([r[1, :shard] for r in rows])[None].astype(jnp.float32)
    bias = jnp.concatenate(
        [r[2, : smalls.shape[0]].reshape(-1, head_dim // fsdps) for r in rows], axis=1
    ).reshape(1, lanes).astype(jnp.float32)
    bias = after(bias, o_blocks[1])

    cosine, sine = rope_tables(positions.reshape(tokens), head_dim)
    normed_one, query_blocks, kv_own = project(
        meta, inputs, attn_gamma, bias, qkv, cosine, sine, (local_heads, kv_heads, head_dim, tps)
    )
    if ctxs == 2:
        kv_before = lax.ppermute(kv_own, "ctx", [(0, 1)])
        half = up_mine.shape[0] // 2
        up_near = links.to_x(
            after(lax.dynamic_slice_in_dim(up_mine, ctx * half, half, 0), pack_across)
        )
        up_far = links.to_y(after(up_near, kv_before))
    else:
        kv_before = lax.all_gather(
            kv_own.reshape(seq_count, block_len, kv_cols), "ctx", axis=1, tiled=True
        ).reshape(seq_count * block_len * ctxs, kv_cols)

    def swap(block_of):
        return [block_of(tp)] + [
            links.hop_tp(block_of((tp + hop) % tps), hop) for hop in range(1, tps)
        ]

    queries = jnp.stack(swap(lambda d: lax.dynamic_index_in_dim(query_blocks, d, 0, keepdims=False)))

    def gather_whole(*items):
        return lax.all_gather(after(jnp.stack(items), pack_across), "fsdp", axis=2, tiled=True)

    gate_down = gather_whole(gate_weight.T, down_weight)
    o_blocks = o_blocks[:2] + [after(item, kv_own) for item in o_blocks[2:]]
    o_wide = jnp.concatenate(o_blocks, axis=0)
    q_blocks = links.gather_tp(after(query_weight, queries))
    if ctxs == 2:
        o_near = links.to_x(lax.dynamic_slice_in_dim(o_wide, ctx * (depth // 2), depth // 2, 0))
        o_far = links.to_y(after(o_near, kv_before))
    else:
        o_near = o_far = links.to_x(o_wide)
    o_core = links.to_core(after(o_wide, queries))

    late_cot = after(cotangent, kv_own)
    cot_all = jnp.concatenate([block_rows(late_cot, hop) for hop in range(tps)], axis=0)
    one_all = jnp.concatenate(
        [block_rows(normed_one.reshape(seq_count, block_len, width), hop) for hop in range(tps)], axis=0
    )

    order = jnp.tile(jnp.arange(own, dtype=jnp.int32), depth // head_dim // kv_heads)[None]
    order = after(order, (cot_all, one_all, q_blocks[1], *([up_near] if ctxs == 2 else [])))
    sizes = (seq_count, kv_heads, head_dim, tps)
    mixed, lse = attend(meta, queries, kv_before, kv_own, order, key_block, sizes)
    o_core_near, o_core_far = (
        links.to_core(after(item, (mixed, q_blocks[2]))) for item in (o_near, o_far)
    )
    o_parts = (o_wide, o_core, o_near, o_far, o_core_near, o_core_far)
    hidden, normed_two = merge(meta, mixed, inputs, o_parts, mlp_gamma, tps)
    two_blocks = [normed_two, links.hop_tp(after(normed_two, q_blocks[-1]))]
    if ctxs == 2:
        up_cores = [links.to_core(after(item, mixed)) for item in (up_mine, up_near)]
        up_cores.append(links.to_core(after(up_far, normed_two)))
        up_full = assemble(meta, up_mine, up_near, up_far, *up_cores)[None]
    else:
        up_full = gather_whole(up_mine)

    two_blocks.append(links.hop_tp(after(two_blocks[-1], (gate_down, up_full))))
    two_blocks.append(links.hop_tp(two_blocks[-1]))
    kept, two_parts, mixed_parts, two_total = None, [], [], None
    for hop in range(tps):
        block = two_blocks[hop]
        if hop + 1 < tps:
            block = after(block, two_blocks[hop + 1])
        if two_total is not None:
            block = after(block, two_total)
        kept, two_part, mixed_part = feed(
            meta, block, cot_all, gate_down, up_full, hop, tps, kept
        )
        two_parts.append(two_part)
        mixed_parts.append(mixed_part)
        if hop == 0:
            q_wide = jnp.concatenate(q_blocks, axis=1)
            q_full = lax.all_gather(q_wide, "fsdp", axis=0, tiled=True)
        if hop >= 1:
            two_total = two_part if hop == 1 else add_low(two_part, two_got)
            two_got = links.hop_tp(two_total)
        two_total = two_total if hop >= 2 else None
    two_own = two_parts[0]
    act_all, gate_all, up_all, two_all = kept
    down_term = inner_rows(cot_all, after(act_all, two_total)).astype(LOW)
    two_got = after(two_got, down_term)

    hidden_grad, branch_grad, attended_grad, mlp_term = turn(
        meta, two_own, two_got, hidden, cotangent, o_parts, mlp_gamma, depth, tps
    )
    mixed_got = links.hop_tp(after(mixed_parts[1], two_got))
    q_grads, kv_parts, token = [], [], two_got
    for s in seqs:
        q_grad, grad_before, grad_own = attend_back(
            meta, s, queries, kv_before, kv_own, order, mixed, attended_grad, after(lse, token),
            cosine, sine, key_block, sizes,
        )
        q_grads.append(q_grad)
        if ctxs == 2:
            kv_parts.append((grad_own, lax.ppermute(grad_before, "ctx", [(1, 0)])))
        else:
            wide_grad = lax.dynamic_update_slice_in_dim(grad_before, grad_own, ctx * block_len, 2)
            kv_parts.append((lax.psum_scatter(wide_grad, "ctx", scatter_dimension=2, tiled=True), None))
        token = (mixed_got, q_grad)
    mixed_got = links.hop_tp(add_low(mixed_parts[2], after(mixed_got, q_grads[0])))
    q_grad = jnp.concatenate(q_grads, axis=0)
    shares = swap(lambda d: lax.dynamic_slice_in_dim(q_grad, d * q_cols, q_cols, 1))
    mixed_next = add_low(mixed_parts[3], mixed_got)
    input_low, attn_term = finish(meta, after(q_grad, mixed_next), q_full, inputs, hidden_grad, attn_gamma, tps)
    output_pairs = links.pairs(inner_rows(mixed, after(branch_grad, q_grads[-1])).astype(LOW), 1)
    token = (mixed_got, input_low, kv_parts, shares, output_pairs)
    kv_parts = [
        mine if got is None else add_low(after(mine, token), got) for mine, got in kv_parts
    ]

    def kv_rows(hop):
        return jnp.stack(
            [
                lax.dynamic_slice_in_dim(kv_parts[s], place(s, links.at(hop)) * own, own, 2)
                for s in seqs
            ],
            axis=2,
        )

    def fsdp_rows(value, below):
        return jnp.concatenate(
            [item for j in range(fsdps) for item in (value[j * shard : (j + 1) * shard], below(j))], axis=0
        )

    def output_rows(hop):
        size = output_part.shape[0] // tps
        return lax.dynamic_slice_in_dim(output_part, links.at(hop) * size, size, 0)

    kv_mine, kv_next = kv_rows(0), kv_rows(1)
    mixed_got = links.hop_tp(after(mixed_next, shares))
    kv_got = links.hop_tp(after(kv_next, (input_low, output_pairs)))
    down_weight_grad = links.lay_weight(*links.reduce_weight(after(down_term, kv_next)))
    kv_next = add_low(kv_rows(2), kv_got)
    gate_term = inner_rows(two_all, after(gate_all, kv_next)).astype(LOW)

    in_blocks = [input_low, links.hop_tp(after(input_low, (mixed_got, kv_next, gate_term)))]
    kv_got = links.hop_tp(after(kv_next, mixed_got))
    gate_weight_grad = links.lay_weight(*links.reduce_weight(after(gate_term, mixed_got))).T
    output_both = links.scatter_core(after(output_pairs, mixed_got))
    up_term = inner_rows(two_all, after(up_all, mixed_got)).astype(LOW)
    out_low = hidden + mixed_parts[0].astype(jnp.float32) + mixed_got.astype(jnp.float32)
    out_low = lax.optimization_barrier(out_low.astype(LOW))
    kv_next = add_low(kv_rows(3), after(kv_got, (up_term, out_low)))

    out_blocks = [out_low, links.hop_tp(after(out_low, (in_blocks[1], kv_next)))]
    kv_got = links.hop_tp(after(kv_next, in_blocks[1]))
    up_part, up_got = links.reduce_weight(after(up_term, in_blocks[1]))
    output_part = links.scatter_x(after(output_both, in_blocks[1]), 1)
    grads_all = after(jnp.concatenate(shares, axis=0), kv_got)
    q_bias_row = jnp.sum(grads_all.astype(jnp.float32), axis=0, keepdims=True)
    q_below = jnp.pad(q_bias_row, ((0, 15), (0, 0))).astype(LOW)
    q_pairs = links.pairs(fsdp_rows(inner_rows(one_all, grads_all).astype(LOW), lambda j: q_below), 0)
    kv_grad, kv_term = kv_back(meta, kv_mine, kv_got, cosine, sine, qkv, inputs, tps)
    gain_terms = jnp.concatenate(
        [jnp.sum(attn_term, axis=0) + jnp.sum(kv_term, axis=0), jnp.sum(mlp_term, axis=0)], axis=1
    ).reshape(-1, kv_cols)
    gain_terms = jnp.pad(gain_terms, ((0, 16 - gain_terms.shape[0]), (0, 0))).astype(LOW)
    kv_blocks = [jnp.concatenate([kv_grad, gain_terms], axis=0)]

    in_blocks.append(links.hop_tp(after(in_blocks[1], (out_blocks[1], kv_blocks[0], q_pairs))))
    kv_blocks.append(links.hop_tp(after(kv_blocks[0], out_blocks[1])))
    q_both = links.scatter_core(after(q_pairs, out_blocks[1]))

    out_blocks.append(
        links.hop_tp(
            after(out_blocks[1], (in_blocks[2], kv_blocks[1], q_both))
        )
    )
    kv_blocks.append(links.hop_tp(after(kv_blocks[1], in_blocks[2])))
    q_part = links.scatter_x(after(q_both, in_blocks[2]), 0)
    output_got = links.hop_tp(after(output_rows(1), in_blocks[2]))
    output_next = add_low(output_rows(2), output_got)

    in_blocks.append(
        links.hop_tp(after(in_blocks[2], (out_blocks[2], kv_blocks[2], q_part, output_next)))
    )
    kv_blocks.append(links.hop_tp(after(kv_blocks[2], (out_blocks[2], down_weight_grad))))
    q_total = links.sum_ctx(after(q_part, out_blocks[2]))
    output_got = links.hop_tp(after(output_next, out_blocks[2]))
    output_next = add_low(output_rows(3), output_got)
    output_got = links.hop_tp(after(output_next, in_blocks[3]))
    output_sum = add_low(output_rows(0), output_got)
    own_tokens = seq_count * own
    kv_all = jnp.concatenate([item[:own_tokens] for item in kv_blocks], axis=0)
    gain_rows = sum(
        item[own_tokens : own_tokens + 2 * width // kv_cols].astype(jnp.float32) for item in kv_blocks
    ).reshape(2, width)
    kv_bias_row = jnp.sum(kv_all.astype(jnp.float32), axis=0, keepdims=True)

    def kv_below(j):
        gains = jnp.pad(gain_rows[:, j * shard : (j + 1) * shard], ((0, 0), (0, kv_cols - shard)))
        return jnp.pad(jnp.concatenate([gains, kv_bias_row], axis=0), ((0, 13), (0, 0))).astype(LOW)

    kv_pairs = links.pairs(fsdp_rows(inner_rows(one_all, kv_all).astype(LOW), kv_below), 0)

    out_blocks.append(
        links.hop_tp(
            after(out_blocks[2], (in_blocks[3], kv_pairs))
        )
    )
    kv_both = links.scatter_core(kv_pairs)
    output_weight_grad = links.sum_ctx(output_sum)
    input_grad = last(meta, in_blocks, kv_blocks, qkv, inputs, attn_gamma)
    kv_part = links.scatter_x(after(kv_both, (in_blocks[3], gate_weight_grad)), 0)
    up_part = after(up_part, (input_grad, out_blocks[3]))
    up_weight_grad = links.lay_weight(up_part, up_got).T
    out_blocks[0] = after(out_blocks[0], (output_sum, q_total))
    kv_total = links.sum_ctx(after(kv_part, input_grad))
    outputs = spread_out(meta, out_blocks, seq_count, LOW)
    query_weight_grad = q_total[:shard]
    part = head_dim // fsdps
    query_bias_grad = lax.dynamic_slice_in_dim(
        q_total[shard].reshape(local_heads, head_dim), fsdp * part, part, 1
    )
    kv_weight = kv_total[:shard]
    gains = kv_total[shard : shard + 2, :shard]
    kv_bias = kv_total[shard + 2].reshape(2, kv_heads, head_dim)
    kv_bias = lax.dynamic_slice_in_dim(kv_bias, fsdp * part, part, 2)
    half = kv_cols // 2

    return (
        outputs,
        input_grad,
        gains[0],
        query_weight_grad,
        query_bias_grad,
        kv_weight[:, :half],
        kv_bias[0],
        kv_weight[:, half:],
        kv_bias[1],
        output_weight_grad,
        gains[1],
        gate_weight_grad,
        up_weight_grad,
        down_weight_grad,
    )


def solution(mesh):
    in_specs = (
        P("fsdp", "ctx", None),
        P("fsdp", "ctx", None),
        P("fsdp", "ctx"),
        P("fsdp"),
        P("fsdp", "tp"),
        P("tp", "fsdp"),
        P("fsdp", None),
        P(None, "fsdp"),
        P("fsdp", None),
        P(None, "fsdp"),
        P("tp", "fsdp"),
        P("fsdp"),
        P("fsdp", "tp"),
        P("fsdp", "tp"),
        P("tp", "fsdp"),
    )
    out_specs = (
        P("fsdp", "ctx", None),
        P("fsdp", "ctx", None),
        P("fsdp"),
        P("fsdp", "tp"),
        P("tp", "fsdp"),
        P("fsdp", None),
        P(None, "fsdp"),
        P("fsdp", None),
        P(None, "fsdp"),
        P("tp", "fsdp"),
        P("fsdp"),
        P("fsdp", "tp"),
        P("fsdp", "tp"),
        P("tp", "fsdp"),
    )
    return jax.shard_map(local, mesh=mesh, in_specs=in_specs, out_specs=out_specs, check_vma=False)
```

```python
import functools
import math

import jax
import jax.numpy as jnp
from jax import lax
from jax.experimental import pallas as pl
from jax.experimental.pallas import tpu as pltpu
from jax.sharding import PartitionSpec as P

EPS = 1e-06
THETA = 1000000.0
LOG2E = 1.0 / math.log(2.0)
LOW = jnp.bfloat16
MASKED = -1e30
MIB = 1024 * 1024


def rope_tables(position, width):
    half = width // 2
    freqs = jnp.exp(jnp.arange(half, dtype=jnp.float32) * (-2.0 * math.log(THETA) / width))
    angle = position.astype(jnp.float32)[..., None] * freqs
    cosine, sine = jnp.cos(angle), jnp.sin(angle)
    return (
        jnp.concatenate([cosine, cosine], axis=-1),
        jnp.concatenate([-sine, sine], axis=-1),
    )


def dot(left, right):
    return jnp.dot(left, right, preferred_element_type=jnp.float32)


def inner_rows(left, right):
    return lax.dot_general(
        left, right, (((0,), (0,)), ((), ())), preferred_element_type=jnp.float32
    )


def inner_cols(left, right):
    return lax.dot_general(
        left, right, (((1,), (1,)), ((), ())), preferred_element_type=jnp.float32
    )


def add_low(left, right):
    return (left.astype(jnp.float32) + right.astype(jnp.float32)).astype(LOW)


def after(value, token):
    return lax.optimization_barrier((value, token))[0]


def root_of(values):
    return lax.rsqrt(jnp.mean(values * values, axis=-1, keepdims=True) + EPS)


FSDP, TP, CTX, BEFORE, PLACE = 0, 1, 2, 3, 4


def shard_at(meta, flip, size):
    return pl.multiple_of(jnp.bitwise_xor(meta[FSDP], flip) * size, size)


def tp_at(meta, hop, tps, size):
    return pl.multiple_of(lax.rem(meta[TP] + tps - hop, tps) * size, size)


def call(kernel, grid, in_specs, out_specs, out_shape, scratch=(), cost=None, name=None, vmem=48):
    return pl.pallas_call(
        kernel,
        grid_spec=pltpu.PrefetchScalarGridSpec(
            num_scalar_prefetch=1,
            grid=grid,
            in_specs=in_specs,
            out_specs=out_specs,
            scratch_shapes=list(scratch),
        ),
        out_shape=out_shape,
        compiler_params=pltpu.CompilerParams(vmem_limit_bytes=vmem * MIB),
        cost_estimate=cost,
        name=name,
    )


def whole(array):
    return pl.BlockSpec(array.shape, lambda *_: (0,) * array.ndim)


def shape(dims, kind):
    return jax.ShapeDtypeStruct(dims, kind)


def project_kernel(
    local_heads, kv_heads, head_dim, meta, x_ref, gain_ref, bias_ref, *refs
):
    weights, (cos_ref, sin_ref, n_ref, q_ref, kv_ref) = refs[:4], refs[4:]
    rows = x_ref.shape[1]
    size = n_ref.shape[1] // 4
    values = x_ref[...].reshape(rows, -1).astype(jnp.float32)
    n_ref[...] = (values * root_of(values) * gain_ref[...]).astype(LOW)
    lin = bias_ref[...]
    for flip, weight in enumerate(weights):
        lin = lin + dot(n_ref[:, pl.ds(shard_at(meta, flip, size), size)], weight[:size, :])
    cosine, sine = cos_ref[...], sin_ref[...]
    for head in range(local_heads + 2 * kv_heads):
        part = lin[:, head * head_dim : (head + 1) * head_dim]
        if head < local_heads + kv_heads:
            part = part * cosine + pltpu.roll(part, head_dim // 2, 1) * sine
        if head < local_heads:
            q_ref[0, :, head * head_dim : (head + 1) * head_dim] = part.astype(LOW)
        else:
            at = (head - local_heads) * head_dim
            kv_ref[:, at : at + head_dim] = part.astype(LOW)


def project(meta, inputs, gain, bias, weights, cosine, sine, sizes):
    seq_count, block_len, width = inputs.shape
    local_heads, kv_heads, head_dim, tps = sizes
    own = block_len // tps
    q_cols, kv_cols = local_heads * head_dim, 2 * kv_heads * head_dim

    def row(i, m):
        return (i, 0)

    def device(i, m):
        seq, place = i // tps, i % tps
        return jnp.where(seq % 2 == 0, place, tps - 1 - place), seq, 0

    tokens = seq_count * block_len
    return call(
        functools.partial(project_kernel, local_heads, kv_heads, head_dim),
        (seq_count * tps,),
        [
            pl.BlockSpec((1, own, width), lambda i, m: (i // tps, i % tps, 0)),
            whole(gain), whole(bias), *(whole(w) for w in weights),
            pl.BlockSpec((own, head_dim), row), pl.BlockSpec((own, head_dim), row),
        ],
        [
            pl.BlockSpec((own, width), row),
            pl.BlockSpec((1, own, q_cols), device),
            pl.BlockSpec((own, kv_cols), row),
        ],
        [
            shape((tokens, width), LOW),
            shape((tps, seq_count * own, q_cols), LOW),
            shape((tokens, kv_cols), LOW),
        ],
        cost=pl.CostEstimate(
            flops=2 * tokens * width * (q_cols + kv_cols), bytes_accessed=8 * tokens * width, transcendentals=0
        ),
        name="project",
    )(meta, inputs, gain, bias, *weights, cosine, sine)


def half_block(block, own):
    return block // 2 if block // 2 % own == 0 else block


def fwd_kernel(
    heads, block, parts, meta, *refs
):
    q_refs, (kb_ref, vb_ref, k_ref, v_ref, order_ref, o_ref, lse_ref, qg_ref, acc_ref, m_ref, l_ref) = (
        refs[:parts], refs[parts:]
    )
    own, cols = q_refs[0].shape[1:]
    head_dim = acc_ref.shape[0]
    scale = LOG2E / math.sqrt(head_dim)
    each = cols // head_dim
    for head in range(heads):
        qg_ref[head * own : (head + 1) * own, :] = q_refs[head // each][
            0, :, (head % each) * head_dim : (head % each + 1) * head_dim
        ]
    acc_ref[...] = jnp.zeros_like(acc_ref)
    m_ref[...] = jnp.full_like(m_ref, MASKED)
    l_ref[...] = jnp.zeros_like(l_ref)
    first = meta[PLACE + pl.program_id(0)] * own

    def step(key_ref, value_ref, start, size, masked):
        keys = key_ref[pl.ds(start, size), :]
        values = value_ref[pl.ds(start, size), :]
        logits = inner_cols(keys, qg_ref[...]) * scale
        if masked:
            key_order = (start - first) + lax.broadcasted_iota(jnp.int32, logits.shape, 0)
            logits = jnp.where(key_order <= order_ref[...], logits, MASKED)
        before = m_ref[...]
        peak = jnp.maximum(before, jnp.max(logits, axis=0, keepdims=True))
        weights = jnp.exp2(logits - peak)
        fade = jnp.exp2(before - peak)
        m_ref[...] = peak
        l_ref[...] = l_ref[...] * fade + jnp.sum(weights, axis=0, keepdims=True)
        acc_ref[...] = acc_ref[...] * fade + inner_rows(values, weights.astype(LOW))

    def early(index, carry):
        step(kb_ref, vb_ref, pl.multiple_of(index * block, block), block, False)
        return carry

    lax.fori_loop(0, meta[BEFORE], early, 0)
    short = half_block(block, own)

    @pl.when(first < short)
    def _():
        step(k_ref, v_ref, 0, short, True)

    @pl.when(first >= short)
    def _():
        step(k_ref, v_ref, 0, block, True)

    total = l_ref[...]
    lse_ref[...] = (m_ref[...] + jnp.log2(total)).reshape(lse_ref.shape)
    mixed = jnp.transpose(acc_ref[...] / total)
    for head in range(heads):
        o_ref[:, head * head_dim : (head + 1) * head_dim] = mixed[
            head * own : (head + 1) * own, :
        ].astype(LOW)


def bwd_kernel(heads, block, parts, seq, meta, *refs):
    q_refs, (
        kb_ref, vb_ref, k_ref, v_ref, order_ref, o_ref, g_ref, lse_ref, cos_ref, sin_ref,
        dq_ref, db_ref, dd_ref, qg_ref, gg_ref, both_ref, acc_ref,
    ) = refs[:parts], refs[parts:]
    own, cols = q_refs[0].shape[1:]
    head_dim = acc_ref.shape[0]
    scale = 1.0 / math.sqrt(head_dim)
    each = cols // head_dim
    for head in range(heads):
        rows = slice(head * own, (head + 1) * own)
        at = slice(head * head_dim, (head + 1) * head_dim)
        qg_ref[rows, :] = q_refs[head // each][
            0, :, (head % each) * head_dim : (head % each + 1) * head_dim
        ]
        gg_ref[rows, :] = g_ref[:, at]
        both_ref[rows, :] = g_ref[:, at].astype(jnp.float32) * o_ref[:, at].astype(jnp.float32)
    center = jnp.sum(jnp.transpose(both_ref[...]), axis=0, keepdims=True)
    acc_ref[...] = jnp.zeros_like(acc_ref)
    lse = lse_ref[...].reshape(order_ref.shape)
    first = meta[PLACE + seq] * own

    def step(key_ref, value_ref, out_ref, start, size, masked):
        keys = key_ref[pl.ds(start, size), :]
        values = value_ref[pl.ds(start, size), :]
        logits = inner_cols(keys, qg_ref[...]) * (scale * LOG2E)
        if masked:
            key_order = (start - first) + lax.broadcasted_iota(jnp.int32, logits.shape, 0)
            logits = jnp.where(key_order <= order_ref[...], logits, MASKED)
        probs = jnp.exp2(logits - lse)
        out_ref[1, 0, pl.ds(start, size), :] = dot(probs.astype(LOW), gg_ref[...]).astype(LOW)
        prob_grad = inner_cols(values, gg_ref[...])
        logit_grad = (probs * (prob_grad - center)).astype(LOW)
        out_ref[0, 0, pl.ds(start, size), :] = (dot(logit_grad, qg_ref[...]) * scale).astype(LOW)
        acc_ref[...] += inner_rows(keys, logit_grad)

    def early(index, carry):
        step(kb_ref, vb_ref, db_ref, pl.multiple_of(index * block, block), block, False)
        return carry

    def clear(ref):
        def body(index, carry):
            start = pl.multiple_of(index * block, block)
            ref[:, :, pl.ds(start, block), :] = jnp.zeros((2, 1, block, head_dim), LOW)
            return carry

        return body

    lax.fori_loop(0, meta[BEFORE], early, 0)
    lax.fori_loop(meta[BEFORE], kb_ref.shape[0] // block, clear(db_ref), 0)
    short = half_block(block, own)

    @pl.when(first < short)
    def _():
        step(k_ref, v_ref, dd_ref, 0, short, True)
        if short < block:
            dd_ref[:, :, short:, :] = jnp.zeros((2, 1, block - short, head_dim), LOW)

    @pl.when(first >= short)
    def _():
        step(k_ref, v_ref, dd_ref, 0, block, True)

    both_ref[...] = jnp.transpose(acc_ref[...])
    for head in range(heads):
        grad = both_ref[head * own : (head + 1) * own, :] * scale
        grad = grad * cos_ref[...] - pltpu.roll(grad, head_dim // 2, 1) * sin_ref[...]
        dq_ref[:, head * head_dim : (head + 1) * head_dim] = grad.astype(LOW)


def attention_specs(queries, kv_before, kv_own, sizes, seq=None):
    seq_count, kv_heads, head_dim, tps = sizes
    rows = queries.shape[1] // seq_count
    parts = tps // kv_heads
    heads = queries.shape[2] * parts // head_dim
    before, block_len = kv_before.shape[0] // seq_count, kv_own.shape[0] // seq_count

    def spec(dims, index):
        if seq is None:
            return pl.BlockSpec(dims, index)
        return pl.BlockSpec(dims, lambda g, m: index(seq, g, m))

    def piece(part):
        return spec(
            (1, rows, queries.shape[2]),
            lambda s, g, m: (lax.rem(m[TP] + tps - (g * parts + part), tps), s, 0),
        )

    specs = [piece(part) for part in range(parts)] + [
        spec((before, head_dim), lambda s, g, m: (s, g)),
        spec((before, head_dim), lambda s, g, m: (s, kv_heads + g)),
        spec((block_len, head_dim), lambda s, g, m: (s, g)),
        spec((block_len, head_dim), lambda s, g, m: (s, kv_heads + g)),
        spec((1, heads * rows), lambda s, g, m: (0, 0)),
    ]
    return specs, rows, parts, heads, before, block_len


def attend(meta, queries, kv_before, kv_own, order, block, sizes):
    seq_count, kv_heads, head_dim, tps = sizes
    specs, rows, parts, heads, before, block_len = attention_specs(queries, kv_before, kv_own, sizes)
    width, wide = kv_heads * heads * head_dim, heads * rows
    work = seq_count * rows * width * (before + block_len)
    return call(
        functools.partial(fwd_kernel, heads, block, parts),
        (seq_count, kv_heads),
        specs,
        [
            pl.BlockSpec((rows, heads * head_dim), lambda s, g, m: (s, g)),
            pl.BlockSpec((1, 1, 1, wide), lambda s, g, m: (s, g, 0, 0)),
        ],
        [shape((seq_count * rows, width), LOW), shape((seq_count, kv_heads, 1, wide), jnp.float32)],
        [
            pltpu.VMEM((wide, head_dim), LOW),
            pltpu.VMEM((head_dim, wide), jnp.float32),
            pltpu.VMEM((1, wide), jnp.float32),
            pltpu.VMEM((1, wide), jnp.float32),
        ],
        cost=pl.CostEstimate(flops=8 * work, bytes_accessed=1 << 22, transcendentals=0),
        name="attend",
    )(meta, *([queries] * parts), kv_before, kv_before, kv_own, kv_own, order)


def attend_back(
    meta, seq, queries, kv_before, kv_own, order, mixed, grads, lse, cosine, sine, block, sizes
):
    seq_count, kv_heads, head_dim, tps = sizes
    specs, rows, parts, heads, before, block_len = attention_specs(
        queries, kv_before, kv_own, sizes, seq
    )
    width, wide = kv_heads * heads * head_dim, heads * rows
    work = rows * width * (before + block_len)
    wide_spec = pl.BlockSpec((rows, heads * head_dim), lambda g, m: (seq, g))
    table_spec = pl.BlockSpec((rows, head_dim), lambda g, m: (seq * tps + m[PLACE + seq], 0))
    return call(
        functools.partial(bwd_kernel, heads, block, parts, seq),
        (kv_heads,),
        specs
        + [
            wide_spec,
            wide_spec,
            pl.BlockSpec((1, 1, 1, wide), lambda g, m: (seq, g, 0, 0)),
            table_spec,
            table_spec,
        ],
        [
            pl.BlockSpec((rows, heads * head_dim), lambda g, m: (0, g)),
            pl.BlockSpec((2, 1, before, head_dim), lambda g, m: (0, g, 0, 0)),
            pl.BlockSpec((2, 1, block_len, head_dim), lambda g, m: (0, g, 0, 0)),
        ],
        [
            shape((rows, width), LOW),
            shape((2, kv_heads, before, head_dim), LOW),
            shape((2, kv_heads, block_len, head_dim), LOW),
        ],
        [
            pltpu.VMEM((wide, head_dim), LOW),
            pltpu.VMEM((wide, head_dim), LOW),
            pltpu.VMEM((wide, head_dim), jnp.float32),
            pltpu.VMEM((head_dim, wide), jnp.float32),
        ],
        cost=pl.CostEstimate(flops=16 * work, bytes_accessed=1 << 22, transcendentals=0),
        name="attend_back",
    )(
        meta, *([queries] * parts), kv_before, kv_before, kv_own, kv_own, order,
        mixed, grads, lse, cosine, sine,
    )


def output_pieces(meta, weights, tps):
    own, other, near, far, other_near, other_far = weights
    depth, half = own.shape[0], near.shape[0]
    low = pl.multiple_of(meta[CTX] * (depth - half), 128)
    high = pl.multiple_of((1 - meta[CTX]) * (depth - half), 128)
    pieces = [(0, None, own), (1, None, other)]
    if half == depth:
        return pieces + [(2, None, near), (3, None, other_near)]
    return pieces + [(2, low, near), (2, high, far), (3, low, other_near), (3, high, other_far)]


def merge_kernel(tps, meta, o_ref, x_ref, *refs):
    weights, (gain_ref, h_ref, n_ref, turned_ref) = refs[:6], refs[6:]
    rows, width = h_ref.shape
    size, depth = width // 4, o_ref.shape[1]
    part = depth // tps
    for hop in range(tps):
        turned_ref[:, hop * part : (hop + 1) * part] = o_ref[:, pl.ds(tp_at(meta, hop, tps, part), part)]
    h_ref[...] = x_ref[...].reshape(rows, width).astype(jnp.float32)
    for flip, first, weight in output_pieces(meta, weights, tps):
        left = turned_ref[...] if first is None else turned_ref[:, pl.ds(first, weight.shape[0])]
        h_ref[:, pl.ds(shard_at(meta, flip, size), size)] += dot(left, weight[...])
    hidden = h_ref[...]
    n_ref[...] = (hidden * root_of(hidden) * gain_ref[...]).astype(LOW)


def merge(meta, mixed, inputs, weights, gain, tps):
    seq_count, block_len, width = inputs.shape
    own = block_len // tps
    depth = mixed.shape[1]
    row = pl.BlockSpec((own, width), lambda s, m: (s, 0))
    return call(
        functools.partial(merge_kernel, tps),
        (seq_count,),
        [
            pl.BlockSpec((own, depth), lambda s, m: (s, 0)),
            pl.BlockSpec((1, own, width), lambda s, m: (s, m[PLACE + s], 0)),
            *(whole(w) for w in weights),
            whole(gain),
        ],
        [row, row],
        [shape((seq_count * own, width), jnp.float32), shape((seq_count * own, width), LOW)],
        [pltpu.VMEM((own, depth), LOW)],
        cost=pl.CostEstimate(
            flops=2 * seq_count * own * depth * width, bytes_accessed=1 << 23, transcendentals=0
        ),
        name="merge",
    )(meta, mixed, inputs, *weights, gain)


def turn_kernel(
    tps, meta, a_ref, b_ref, h_ref, c_ref, *refs,
):
    weights, (gain_ref, hg_ref, bg_ref, ag_ref, term_ref, turned_ref) = refs[:6], refs[6:]
    rows, width = h_ref.shape
    size, depth = width // 4, ag_ref.shape[1]
    two_grad = a_ref[...].astype(jnp.float32) + b_ref[...].astype(jnp.float32)
    hidden = h_ref[...]
    root = root_of(hidden)
    term_ref[...] = jnp.sum(two_grad * hidden * root, axis=0, keepdims=True).reshape(term_ref.shape)
    scaled = gain_ref[...] * two_grad
    grad = (
        c_ref[...].reshape(rows, width).astype(jnp.float32)
        + root * scaled
        - hidden * root**3 * jnp.mean(scaled * hidden, axis=-1, keepdims=True)
    )
    hg_ref[...] = grad
    bg_ref[...] = grad.astype(LOW)
    turned_ref[...] = jnp.zeros_like(turned_ref)
    for flip, first, weight in output_pieces(meta, weights, tps):
        at = slice(None) if first is None else pl.ds(first, weight.shape[0])
        turned_ref[:, at] += inner_cols(bg_ref[:, pl.ds(shard_at(meta, flip, size), size)], weight[...])
    part = depth // tps
    for hop in range(tps):
        ag_ref[:, pl.ds(tp_at(meta, hop, tps, part), part)] = turned_ref[
            :, hop * part : (hop + 1) * part
        ].astype(LOW)


def turn(meta, two_own, two_got, hidden, cotangent, weights, gain, depth, tps):
    seq_count, block_len, width = cotangent.shape
    own = block_len // tps
    row = pl.BlockSpec((own, width), lambda s, m: (s, 0))
    tokens = seq_count * own
    return call(
        functools.partial(turn_kernel, tps),
        (seq_count,),
        [
            row, row, row,
            pl.BlockSpec((1, own, width), lambda s, m: (s, m[PLACE + s], 0)),
            *(whole(w) for w in weights),
            whole(gain),
        ],
        [
            row, row,
            pl.BlockSpec((own, depth), lambda s, m: (s, 0)),
            pl.BlockSpec((1, 1, width), lambda s, m: (s, 0, 0)),
        ],
        [
            shape((tokens, width), jnp.float32),
            shape((tokens, width), LOW),
            shape((tokens, depth), LOW),
            shape((seq_count, 1, width), jnp.float32),
        ],
        [pltpu.VMEM((own, depth), jnp.float32)],
        cost=pl.CostEstimate(flops=2 * tokens * depth * width, bytes_accessed=1 << 23, transcendentals=0),
        name="turn",
    )(meta, two_own, two_got, hidden, cotangent, *weights, gain)


def back_through_norm(grad, values, gain):
    root = root_of(values)
    scaled = gain * grad
    term = jnp.sum(grad * values * root, axis=0, keepdims=True)
    return root * scaled - values * root**3 * jnp.mean(scaled * values, axis=-1, keepdims=True), term


def finish_kernel(tps, meta, g_ref, q_ref, x_ref, hg_ref, gain_ref, out_ref, term_ref, turned_ref):
    part = g_ref.shape[1] // tps
    for hop in range(tps):
        turned_ref[:, hop * part : (hop + 1) * part] = g_ref[:, pl.ds(tp_at(meta, hop, tps, part), part)]
    values = x_ref[...].reshape(hg_ref.shape).astype(jnp.float32)
    part, term = back_through_norm(inner_cols(turned_ref[...], q_ref[...]), values, gain_ref[...])
    term_ref[...] = term.reshape(term_ref.shape)
    out_ref[...] = (hg_ref[...] + part).astype(LOW)


def finish(meta, q_grad, q_full, inputs, hidden_grad, gain, tps):
    seq_count, block_len, width = inputs.shape
    own = block_len // tps
    tokens = seq_count * own
    row = pl.BlockSpec((own, width), lambda s, m: (s, 0))
    return call(
        functools.partial(finish_kernel, tps),
        (seq_count,),
        [
            pl.BlockSpec((own, q_grad.shape[1]), lambda s, m: (s, 0)),
            whole(q_full),
            pl.BlockSpec((1, own, width), lambda s, m: (s, m[PLACE + s], 0)),
            row,
            whole(gain),
        ],
        [row, pl.BlockSpec((1, 1, width), lambda s, m: (s, 0, 0))],
        [shape((tokens, width), LOW), shape((seq_count, 1, width), jnp.float32)],
        [pltpu.VMEM((own, q_grad.shape[1]), LOW)],
        cost=pl.CostEstimate(
            flops=2 * tokens * q_grad.shape[1] * width, bytes_accessed=1 << 23, transcendentals=0
        ),
        name="finish",
    )(meta, q_grad, q_full, inputs, hidden_grad, gain)


def one_from_kv(meta, kv_grad, weights, one_ref):
    size = one_ref.shape[1] // 4
    skip = weights[0].shape[1] - kv_grad.shape[1]
    for flip, weight in enumerate(weights):
        one_ref[:, pl.ds(shard_at(meta, flip, size), size)] = inner_cols(
            kv_grad, weight[:size, skip:]
        )
    return one_ref[...]


def kv_kernel(kv_heads, head_dim, meta, a_ref, b_ref, cos_ref, sin_ref, *refs):
    weights, (x_ref, kv_ref, term_ref, one_ref) = refs[:4], refs[4:]
    cosine, sine = cos_ref[...], sin_ref[...]
    for kind in range(2):
        for head in range(kv_heads):
            grad = (
                a_ref[kind, head, 0].astype(jnp.float32) + b_ref[kind, head, 0].astype(jnp.float32)
            )
            if kind == 0:
                grad = grad * cosine - pltpu.roll(grad, head_dim // 2, 1) * sine
            at = (kind * kv_heads + head) * head_dim
            kv_ref[:, at : at + head_dim] = grad.astype(LOW)
    one = one_from_kv(meta, kv_ref[...], weights, one_ref)
    values = x_ref[...].reshape(one.shape).astype(jnp.float32)
    term = jnp.sum(one * values * root_of(values), axis=0, keepdims=True)
    term_ref[...] = term.reshape(term_ref.shape)


def kv_back(meta, kv_mine, kv_got, cosine, sine, weights, inputs, tps):
    seq_count, block_len, width = inputs.shape
    own = block_len // tps
    kv_heads, head_dim = kv_mine.shape[1], kv_mine.shape[4]
    kv_cols = 2 * kv_heads * head_dim
    kv_spec = pl.BlockSpec((2, kv_heads, 1, own, head_dim), lambda s, m: (0, 0, s, 0, 0))
    table_spec = pl.BlockSpec((own, head_dim), lambda s, m: (s * tps + m[PLACE + s], 0))
    return call(
        functools.partial(kv_kernel, kv_heads, head_dim),
        (seq_count,),
        [
            kv_spec, kv_spec, table_spec, table_spec,
            *(whole(w) for w in weights),
            pl.BlockSpec((1, own, width), lambda s, m: (s, m[PLACE + s], 0)),
        ],
        [
            pl.BlockSpec((own, kv_cols), lambda s, m: (s, 0)),
            pl.BlockSpec((1, 1, width), lambda s, m: (s, 0, 0)),
        ],
        [shape((seq_count * own, kv_cols), LOW), shape((seq_count, 1, width), jnp.float32)],
        [pltpu.VMEM((own, width), jnp.float32)],
        cost=pl.CostEstimate(
            flops=2 * seq_count * own * kv_cols * width, bytes_accessed=1 << 22, transcendentals=0
        ),
        name="kv_back",
    )(meta, kv_mine, kv_got, cosine, sine, *weights, inputs)


def last_kernel(tps, meta, *refs):
    blocks, kvs, weights = refs[:tps], refs[tps : 2 * tps], refs[2 * tps : 2 * tps + 4]
    x_ref, gain_ref, out_ref, one_ref = refs[2 * tps + 4 :]
    seq = pl.program_id(0)
    own = blocks[0].shape[0]
    for hop in range(tps):
        device = lax.rem(meta[TP] + tps - hop, tps)
        place = jnp.where(seq % 2 == 0, device, tps - 1 - device)
        at = pl.ds(pl.multiple_of(place * own, own), own)
        one = one_from_kv(meta, kvs[hop][...], weights, one_ref)
        values = x_ref[0, at, :].astype(jnp.float32)
        part, _ = back_through_norm(one, values, gain_ref[...])
        out_ref[0, at, :] = blocks[hop][...].astype(jnp.float32) + part


def last(meta, blocks, kvs, weights, inputs, gain):
    seq_count, block_len, width = inputs.shape
    tps = len(blocks)
    own = block_len // tps
    every = pl.BlockSpec((1, block_len, width), lambda s, m: (s, 0, 0))
    return call(
        functools.partial(last_kernel, tps),
        (seq_count,),
        [pl.BlockSpec((own, width), lambda s, m: (s, 0))] * tps
        + [pl.BlockSpec((own, kvs[0].shape[1]), lambda s, m: (s, 0))] * tps
        + [whole(w) for w in weights]
        + [every, whole(gain)],
        every,
        shape(inputs.shape, jnp.float32),
        [pltpu.VMEM((own, width), jnp.float32)],
        cost=pl.CostEstimate(
            flops=2 * seq_count * block_len * kvs[0].shape[1] * width, bytes_accessed=1 << 24, transcendentals=0
        ),
        name="last",
    )(meta, *blocks, *kvs, *weights, inputs, gain)


def feed_kernel(first, hidden, *refs):
    n_ref, c_ref, wg_ref, wu_ref, wd_ref = refs[1:6]
    act_ref, gg_ref, ug_ref, all_ref, two_ref, mix_ref, two_acc, mix_acc = refs[6 if first else 10 :]
    step, tile = pl.program_id(0), wg_ref.shape[0]
    steps = -(-hidden // tile)

    def body(count):
        gate = inner_cols(n_ref[...], wg_ref[:count, :])
        up_part = inner_cols(n_ref[...], wu_ref[:count, :])
        act_grad = inner_cols(c_ref[...], wd_ref[:count, :])
        sigma = jax.nn.sigmoid(gate)
        silu = gate * sigma
        act = (silu * up_part).astype(LOW)
        gate_grad = (act_grad * up_part * (sigma * (1.0 + gate * (1.0 - sigma)))).astype(LOW)
        up_grad = (act_grad * silu).astype(LOW)
        act_ref[:, :count], gg_ref[:, :count], ug_ref[:, :count] = act, gate_grad, up_grad
        return (
            dot(gate_grad, wg_ref[:count, :]) + dot(up_grad, wu_ref[:count, :]),
            dot(act, wd_ref[:count, :]),
        )

    @pl.when(step == 0)
    def _():
        all_ref[...] = n_ref[...]
        two_acc[...], mix_acc[...] = body(tile)

    @pl.when(jnp.logical_and(step > 0, step < steps - 1))
    def _():
        two, mix = body(tile)
        two_acc[...] += two
        mix_acc[...] += mix

    @pl.when(step == steps - 1)
    def _():
        two, mix = body(hidden - (steps - 1) * tile)
        two_ref[...] = (two_acc[...] + two).astype(LOW)
        mix_ref[...] = (mix_acc[...] + mix).astype(LOW)


def feed(meta, normed, cots, gate_down, up, hop, tps, kept):
    rows, width = normed.shape
    hidden = up.shape[1]
    tile = 768
    assert hidden > tile
    gate_spec = pl.BlockSpec((None, tile, width), lambda j, m: (0, j, 0))
    down_spec = pl.BlockSpec((None, tile, width), lambda j, m: (1, j, 0))
    column = pl.BlockSpec((rows, tile), lambda j, m: (hop, j))
    fixed = pl.BlockSpec((rows, width), lambda j, m: (0, 0))
    first = hop == 0
    wide = shape((tps * rows, hidden), LOW)
    *hiddens, two_part, mixed_part = pl.pallas_call(
        functools.partial(feed_kernel, first, hidden),
        grid_spec=pltpu.PrefetchScalarGridSpec(
            num_scalar_prefetch=1,
            grid=(-(-hidden // tile),),
            in_specs=[fixed, pl.BlockSpec((rows, width), lambda j, m: (hop, 0)), gate_spec, gate_spec, down_spec]
            + ([] if first else [pl.BlockSpec(memory_space=pl.ANY)] * 4),
            out_specs=[
                column, column, column, pl.BlockSpec((rows, width), lambda j, m: (hop, 0)), fixed, fixed
            ],
            scratch_shapes=[pltpu.VMEM((rows, width), jnp.float32)] * 2,
        ),
        out_shape=[
            wide, wide, wide, shape((tps * rows, width), LOW),
            shape((rows, width), LOW), shape((rows, width), LOW),
        ],
        input_output_aliases={} if first else {6: 0, 7: 1, 8: 2, 9: 3},
        compiler_params=pltpu.CompilerParams(vmem_limit_bytes=56 * MIB),
        cost_estimate=pl.CostEstimate(
            flops=12 * rows * width * hidden, bytes_accessed=6 * width * hidden, transcendentals=rows * hidden
        ),
        name="feed",
    )(meta, normed, cots, gate_down, up, gate_down, *(() if first else kept))
    return hiddens, two_part, mixed_part


def assemble_kernel(tiles, meta, own_ref, near_ref, far_ref, o_own_ref, o_near_ref, o_far_ref, out_ref):
    size = own_ref.shape[1]
    is_near = (pl.program_id(0) // tiles) == meta[CTX]
    out_ref[:, pl.ds(shard_at(meta, 0, size), size)] = own_ref[...]
    out_ref[:, pl.ds(shard_at(meta, 1, size), size)] = o_own_ref[...]

    @pl.when(is_near)
    def _():
        out_ref[:, pl.ds(shard_at(meta, 2, size), size)] = near_ref[...]
        out_ref[:, pl.ds(shard_at(meta, 3, size), size)] = o_near_ref[...]

    @pl.when(jnp.logical_not(is_near))
    def _():
        out_ref[:, pl.ds(shard_at(meta, 2, size), size)] = far_ref[...]
        out_ref[:, pl.ds(shard_at(meta, 3, size), size)] = o_far_ref[...]


def assemble(meta, own, near, far, other, other_near, other_far):
    rows, size = own.shape
    tiles = 2 if rows % 64 == 0 else 1
    tile = rows // (2 * tiles)
    every = pl.BlockSpec((tile, size), lambda i, m: (i, 0))
    half = pl.BlockSpec((tile, size), lambda i, m: (i % tiles, 0))
    return call(
        functools.partial(assemble_kernel, tiles),
        (2 * tiles,),
        [every, half, half, every, half, half],
        pl.BlockSpec((tile, 4 * size), lambda i, m: (i, 0)),
        shape((rows, 4 * size), LOW),
        cost=pl.CostEstimate(flops=0, bytes_accessed=16 * rows * size, transcendentals=0),
        name="assemble",
    )(meta, own, near, far, other, other_near, other_far)


def lay_kernel(low_ref, high_ref, out_ref):
    both = jnp.concatenate([low_ref[...], high_ref[...]], axis=0)
    out_ref[...] = jnp.transpose(both.astype(jnp.float32))


def lay(low, high):
    rows, cols = low.shape
    return pl.pallas_call(
        lay_kernel,
        in_specs=[pl.BlockSpec(memory_space=pltpu.VMEM)] * 2,
        out_specs=pl.BlockSpec(memory_space=pltpu.VMEM),
        out_shape=shape((cols, 2 * rows), jnp.float32),
        compiler_params=pltpu.CompilerParams(vmem_limit_bytes=48 * MIB),
        cost_estimate=pl.CostEstimate(flops=0, bytes_accessed=12 * rows * cols, transcendentals=0),
        name="lay",
    )(low, high)


def spread_kernel(tps, meta, *refs):
    out_ref = refs[tps]
    seq_count = out_ref.shape[0]
    own = refs[0].shape[0] // seq_count
    for hop in range(tps):
        device = lax.rem(meta[TP] + tps - hop, tps)
        for s in range(seq_count):
            place = device if s % 2 == 0 else tps - 1 - device
            at = pl.ds(pl.multiple_of(place * own, own), own)
            out_ref[s, at, :] = refs[hop][s * own : (s + 1) * own, :].astype(out_ref.dtype)


def spread_out(meta, blocks, seq_count, kind):
    tps = len(blocks)
    rows, width = blocks[0].shape
    dims = (seq_count, rows // seq_count * tps, width)
    return call(
        functools.partial(spread_kernel, tps),
        (1,),
        [whole(item) for item in blocks],
        pl.BlockSpec(dims, lambda *_: (0, 0, 0)),
        shape(dims, kind),
        cost=pl.CostEstimate(flops=0, bytes_accessed=8 * rows * tps * width, transcendentals=0),
        name="spread",
    )(meta, *blocks)


class Links:
    def __init__(self):
        self.tp, self.ctx, self.fsdp = (lax.axis_index(a) for a in ("tp", "ctx", "fsdp"))
        self.tps, self.ctxs, self.fsdps = (lax.axis_size(a) for a in ("tp", "ctx", "fsdp"))
        self.core, self.x = self.fsdp % 2, self.fsdp // 2
        assert self.fsdps == 4

    def to_core(self, value):
        return lax.ppermute(value, "fsdp", [(0, 1), (1, 0), (2, 3), (3, 2)])

    def to_x(self, value):
        return lax.ppermute(value, "fsdp", [(0, 2), (2, 0), (1, 3), (3, 1)])

    def to_y(self, value):
        return lax.ppermute(value, "ctx", [(0, 1), (1, 0)])

    def hop_tp(self, value, hop=1):
        return lax.ppermute(value, "tp", [(i, (i + hop) % self.tps) for i in range(self.tps)])

    def gather_fsdp(self, shard):
        across = self.to_x(shard)
        return shard, across, self.to_core(jnp.concatenate([shard, across], axis=0))

    def gather_tp(self, block):
        blocks = [block]
        for _ in range(1, self.tps):
            blocks.append(self.hop_tp(blocks[-1]))
        return blocks

    def scatter_tp(self, blocks):
        total = blocks[1]
        for hop in range(1, self.tps):
            got = self.hop_tp(total)
            if hop < self.tps - 1:
                total = add_low(blocks[hop + 1], got)
        return blocks[0], got

    def at(self, hop):
        return (self.tp - hop + self.tps) % self.tps

    def pairs(self, value, axis):
        size = value.shape[axis] // 4

        def pair(core):
            return jnp.concatenate(
                [
                    lax.dynamic_slice_in_dim(value, (2 * x + core) * size, size, axis)
                    for x in range(2)
                ],
                axis,
            )

        return pair(self.core), pair(1 - self.core)

    def scatter_core(self, pairs):
        return add_low(pairs[0], self.to_core(pairs[1]))

    def scatter_x(self, both, axis):
        size = both.shape[axis] // 2
        away = lax.dynamic_slice_in_dim(both, (1 - self.x) * size, size, axis)
        keep = lax.dynamic_slice_in_dim(both, self.x * size, size, axis)
        return add_low(keep, self.to_x(away))

    def sum_ctx(self, value):
        value = lax.optimization_barrier(value.astype(LOW))
        if self.ctxs == 2:
            return value.astype(jnp.float32) + self.to_y(value).astype(jnp.float32)
        return lax.psum(value.astype(jnp.float32), "ctx")

    def reduce_weight(self, term):
        part = lax.psum_scatter(term, ("fsdp", "ctx"), scatter_dimension=0, tiled=True)
        if self.ctxs != 2:
            return lax.all_gather(part, "ctx", axis=0, tiled=True), None
        part = lax.optimization_barrier(part)
        return part, self.to_y(part)

    def lay_weight(self, part, got):
        if got is None:
            return part.astype(jnp.float32).T
        return lay(jnp.where(self.ctx == 0, part, got), jnp.where(self.ctx == 0, got, part))


def local(
    inputs,
    cotangent,
    positions,
    attn_gain,
    query_weight,
    query_bias,
    key_weight,
    key_bias,
    value_weight,
    value_bias,
    output_weight,
    mlp_gain,
    gate_weight,
    up_weight,
    down_weight,
):
    links = Links()
    seq_count, block_len, width = inputs.shape
    tp, tps, ctx, ctxs = links.tp, links.tps, links.ctx, links.ctxs
    fsdp, fsdps = links.fsdp, links.fsdps
    own = block_len // tps
    local_heads, kv_heads = query_bias.shape[0], key_bias.shape[0]
    head_dim = key_weight.shape[1] // kv_heads
    q_cols = local_heads * head_dim
    kv_cols = 2 * kv_heads * head_dim
    depth = q_cols * tps
    shard = width // fsdps
    tokens = seq_count * block_len
    key_block = block_len
    seqs = range(seq_count)

    def place(seq, device):
        return device if seq % 2 == 0 else tps - 1 - device

    def block_rows(value, hop):
        return jnp.concatenate(
            [
                lax.dynamic_slice_in_dim(value[s], place(s, links.at(hop)) * own, own, 0)
                for s in seqs
            ],
            axis=0,
        )

    meta = jnp.stack(
        [fsdp, tp, ctx, ctx * (block_len // key_block)] + [place(s, tp) for s in seqs]
    ).astype(jnp.int32)

    lanes = q_cols + kv_cols
    smalls = jnp.concatenate([b.reshape(-1) for b in (query_bias, key_bias, value_bias)])
    extra = jnp.stack(
        [jnp.pad(row, (0, lanes - row.shape[0])) for row in (attn_gain, mlp_gain, smalls)]
    )
    extra = jnp.pad(extra, ((0, 13), (0, 0)))
    pack = jnp.concatenate(
        [jnp.concatenate([query_weight, key_weight, value_weight], axis=1), extra], axis=0
    )
    pack_core, pack_across = links.to_core(pack), links.to_x(pack)
    qkv = pack, pack_core, pack_across, links.to_core(pack_across)
    o_blocks = links.gather_tp(output_weight)
    up_mine = up_weight.T

    rows = jnp.stack([item[shard : shard + 3] for item in qkv])
    rows = [
        lax.dynamic_index_in_dim(rows, jnp.bitwise_xor(fsdp, j), 0, keepdims=False) for j in range(4)
    ]
    attn_gamma = jnp.concatenate([r[0, :shard] for r in rows])[None].astype(jnp.float32)
    mlp_gamma = jnp.concatenate([r[1, :shard] for r in rows])[None].astype(jnp.float32)
    bias = jnp.concatenate(
        [r[2, : smalls.shape[0]].reshape(-1, head_dim // fsdps) for r in rows], axis=1
    ).reshape(1, lanes).astype(jnp.float32)
    bias = after(bias, o_blocks[1])

    cosine, sine = rope_tables(positions.reshape(tokens), head_dim)
    normed_one, query_blocks, kv_own = project(
        meta, inputs, attn_gamma, bias, qkv, cosine, sine, (local_heads, kv_heads, head_dim, tps)
    )
    if ctxs == 2:
        kv_before = lax.ppermute(kv_own, "ctx", [(0, 1)])
        half = up_mine.shape[0] // 2
        up_near = links.to_x(
            after(lax.dynamic_slice_in_dim(up_mine, ctx * half, half, 0), pack_across)
        )
        up_far = links.to_y(after(up_near, kv_before))
    else:
        kv_before = lax.all_gather(
            kv_own.reshape(seq_count, block_len, kv_cols), "ctx", axis=1, tiled=True
        ).reshape(seq_count * block_len * ctxs, kv_cols)

    def swap(block_of):
        return [block_of(tp)] + [
            links.hop_tp(block_of((tp + hop) % tps), hop) for hop in range(1, tps)
        ]

    queries = jnp.stack(swap(lambda d: lax.dynamic_index_in_dim(query_blocks, d, 0, keepdims=False)))

    def gather_whole(*items):
        return lax.all_gather(after(jnp.stack(items), pack_across), "fsdp", axis=2, tiled=True)

    gate_down = gather_whole(gate_weight.T, down_weight)
    o_blocks = o_blocks[:2] + [after(item, kv_own) for item in o_blocks[2:]]
    o_wide = jnp.concatenate(o_blocks, axis=0)
    q_blocks = links.gather_tp(after(query_weight, queries))
    if ctxs == 2:
        o_near = links.to_x(lax.dynamic_slice_in_dim(o_wide, ctx * (depth // 2), depth // 2, 0))
        o_far = links.to_y(after(o_near, kv_before))
    else:
        o_near = o_far = links.to_x(o_wide)
    o_core = links.to_core(after(o_wide, queries))

    late_cot = after(cotangent, kv_own)
    cot_all = jnp.concatenate([block_rows(late_cot, hop) for hop in range(tps)], axis=0)
    one_all = jnp.concatenate(
        [block_rows(normed_one.reshape(seq_count, block_len, width), hop) for hop in range(tps)], axis=0
    )

    order = jnp.tile(jnp.arange(own, dtype=jnp.int32), depth // head_dim // kv_heads)[None]
    order = after(order, (cot_all, one_all, q_blocks[1], *([up_near] if ctxs == 2 else [])))
    sizes = (seq_count, kv_heads, head_dim, tps)
    mixed, lse = attend(meta, queries, kv_before, kv_own, order, key_block, sizes)
    o_core_near, o_core_far = (
        links.to_core(after(item, (mixed, q_blocks[2]))) for item in (o_near, o_far)
    )
    o_parts = (o_wide, o_core, o_near, o_far, o_core_near, o_core_far)
    hidden, normed_two = merge(meta, mixed, inputs, o_parts, mlp_gamma, tps)
    two_blocks = [normed_two, links.hop_tp(after(normed_two, q_blocks[-1]))]
    if ctxs == 2:
        up_cores = [links.to_core(after(item, mixed)) for item in (up_mine, up_near)]
        up_cores.append(links.to_core(after(up_far, normed_two)))
        up_full = assemble(meta, up_mine, up_near, up_far, *up_cores)[None]
    else:
        up_full = gather_whole(up_mine)

    two_blocks.append(links.hop_tp(after(two_blocks[-1], (gate_down, up_full))))
    two_blocks.append(links.hop_tp(two_blocks[-1]))
    kept, two_parts, mixed_parts, two_total = None, [], [], None
    for hop in range(tps):
        block = two_blocks[hop]
        if hop + 1 < tps:
            block = after(block, two_blocks[hop + 1])
        if two_total is not None:
            block = after(block, two_total)
        kept, two_part, mixed_part = feed(
            meta, block, cot_all, gate_down, up_full, hop, tps, kept
        )
        two_parts.append(two_part)
        mixed_parts.append(mixed_part)
        if hop == 0:
            q_wide = jnp.concatenate(q_blocks, axis=1)
            q_full = lax.all_gather(q_wide, "fsdp", axis=0, tiled=True)
        if hop >= 1:
            two_total = two_part if hop == 1 else add_low(two_part, two_got)
            two_got = links.hop_tp(two_total)
        two_total = two_total if hop >= 2 else None
    two_own = two_parts[0]
    act_all, gate_all, up_all, two_all = kept
    down_term = inner_rows(cot_all, after(act_all, two_total)).astype(LOW)
    two_got = after(two_got, down_term)

    hidden_grad, branch_grad, attended_grad, mlp_term = turn(
        meta, two_own, two_got, hidden, cotangent, o_parts, mlp_gamma, depth, tps
    )
    mixed_got = links.hop_tp(after(mixed_parts[1], two_got))
    q_grads, kv_parts, token = [], [], two_got
    for s in seqs:
        q_grad, grad_before, grad_own = attend_back(
            meta, s, queries, kv_before, kv_own, order, mixed, attended_grad, after(lse, token),
            cosine, sine, key_block, sizes,
        )
        q_grads.append(q_grad)
        if ctxs == 2:
            kv_parts.append((grad_own, lax.ppermute(grad_before, "ctx", [(1, 0)])))
        else:
            wide_grad = lax.dynamic_update_slice_in_dim(grad_before, grad_own, ctx * block_len, 2)
            kv_parts.append((lax.psum_scatter(wide_grad, "ctx", scatter_dimension=2, tiled=True), None))
        token = (mixed_got, q_grad)
    mixed_got = links.hop_tp(add_low(mixed_parts[2], after(mixed_got, q_grads[0])))
    q_grad = jnp.concatenate(q_grads, axis=0)
    shares = swap(lambda d: lax.dynamic_slice_in_dim(q_grad, d * q_cols, q_cols, 1))
    mixed_next = add_low(mixed_parts[3], mixed_got)
    input_low, attn_term = finish(meta, after(q_grad, mixed_next), q_full, inputs, hidden_grad, attn_gamma, tps)
    output_pairs = links.pairs(inner_rows(mixed, after(branch_grad, q_grads[-1])).astype(LOW), 1)
    token = (mixed_got, input_low, kv_parts, shares, output_pairs)
    kv_parts = [(after(mine, token), got) for mine, got in kv_parts]

    def kv_block(seq, hop):
        mine, got = (
            None if item is None
            else lax.dynamic_slice_in_dim(item, place(seq, links.at(hop)) * own, own, 2)
            for item in kv_parts[seq]
        )
        return mine if got is None else add_low(mine, got)

    def kv_rows(hop):
        return jnp.stack([kv_block(s, hop) for s in seqs], axis=2)

    def fsdp_rows(value, below):
        return jnp.concatenate(
            [item for j in range(fsdps) for item in (value[j * shard : (j + 1) * shard], below(j))], axis=0
        )

    def output_rows(hop):
        size = output_part.shape[0] // tps
        return lax.dynamic_slice_in_dim(output_part, links.at(hop) * size, size, 0)

    kv_mine, kv_next = kv_rows(0), kv_rows(1)
    mixed_got = links.hop_tp(after(mixed_next, shares))
    kv_got = links.hop_tp(after(kv_next, (input_low, output_pairs)))
    down_weight_grad = links.lay_weight(*links.reduce_weight(after(down_term, kv_parts[-1])))
    kv_next = add_low(kv_rows(2), kv_got)
    gate_term = inner_rows(two_all, after(gate_all, kv_next)).astype(LOW)

    in_blocks = [input_low, links.hop_tp(after(input_low, (mixed_got, kv_next, gate_term)))]
    kv_got = links.hop_tp(after(kv_next, mixed_got))
    gate_weight_grad = links.lay_weight(*links.reduce_weight(after(gate_term, mixed_got))).T
    output_both = links.scatter_core(after(output_pairs, mixed_got))
    up_term = inner_rows(two_all, after(up_all, mixed_got)).astype(LOW)
    out_low = hidden + mixed_parts[0].astype(jnp.float32) + mixed_got.astype(jnp.float32)
    out_low = lax.optimization_barrier(out_low.astype(LOW))
    kv_next = add_low(kv_rows(3), after(kv_got, (up_term, out_low)))

    out_blocks = [out_low, links.hop_tp(after(out_low, (in_blocks[1], kv_next)))]
    kv_got = links.hop_tp(after(kv_next, in_blocks[1]))
    up_part, up_got = links.reduce_weight(after(up_term, in_blocks[1]))
    output_part = links.scatter_x(after(output_both, in_blocks[1]), 1)
    grads_all = after(jnp.concatenate(shares, axis=0), kv_got)
    q_bias_row = jnp.sum(grads_all.astype(jnp.float32), axis=0, keepdims=True)
    q_below = jnp.pad(q_bias_row, ((0, 15), (0, 0))).astype(LOW)
    q_pairs = links.pairs(fsdp_rows(inner_rows(one_all, grads_all).astype(LOW), lambda j: q_below), 0)
    kv_grad, kv_term = kv_back(meta, kv_mine, kv_got, cosine, sine, qkv, inputs, tps)
    gain_terms = jnp.concatenate(
        [jnp.sum(attn_term, axis=0) + jnp.sum(kv_term, axis=0), jnp.sum(mlp_term, axis=0)], axis=1
    ).reshape(-1, kv_cols)
    gain_terms = jnp.pad(gain_terms, ((0, 16 - gain_terms.shape[0]), (0, 0))).astype(LOW)
    kv_blocks = [jnp.concatenate([kv_grad, gain_terms], axis=0)]

    in_blocks.append(links.hop_tp(after(in_blocks[1], (out_blocks[1], kv_blocks[0], q_pairs))))
    kv_blocks.append(links.hop_tp(after(kv_blocks[0], out_blocks[1])))
    q_both = links.scatter_core(after(q_pairs, out_blocks[1]))

    out_blocks.append(
        links.hop_tp(
            after(out_blocks[1], (in_blocks[2], kv_blocks[1], q_both))
        )
    )
    kv_blocks.append(links.hop_tp(after(kv_blocks[1], in_blocks[2])))
    q_part = links.scatter_x(after(q_both, in_blocks[2]), 0)
    output_got = links.hop_tp(after(output_rows(1), in_blocks[2]))
    output_next = add_low(output_rows(2), output_got)

    in_blocks.append(
        links.hop_tp(after(in_blocks[2], (out_blocks[2], kv_blocks[2], q_part, output_next)))
    )
    kv_blocks.append(links.hop_tp(after(kv_blocks[2], (out_blocks[2], down_weight_grad))))
    q_total = links.sum_ctx(after(q_part, out_blocks[2]))
    output_got = links.hop_tp(after(output_next, out_blocks[2]))
    output_next = add_low(output_rows(3), output_got)
    output_got = links.hop_tp(after(output_next, in_blocks[3]))
    output_sum = add_low(output_rows(0), output_got)
    own_tokens = seq_count * own
    kv_all = jnp.concatenate([item[:own_tokens] for item in kv_blocks], axis=0)
    gain_rows = sum(
        item[own_tokens : own_tokens + 2 * width // kv_cols].astype(jnp.float32) for item in kv_blocks
    ).reshape(2, width)
    kv_bias_row = jnp.sum(kv_all.astype(jnp.float32), axis=0, keepdims=True)

    def kv_below(j):
        gains = jnp.pad(gain_rows[:, j * shard : (j + 1) * shard], ((0, 0), (0, kv_cols - shard)))
        return jnp.pad(jnp.concatenate([gains, kv_bias_row], axis=0), ((0, 13), (0, 0))).astype(LOW)

    kv_pairs = links.pairs(fsdp_rows(inner_rows(one_all, kv_all).astype(LOW), kv_below), 0)

    out_blocks.append(
        links.hop_tp(
            after(out_blocks[2], (in_blocks[3], kv_pairs))
        )
    )
    kv_both = links.scatter_core(kv_pairs)
    output_weight_grad = links.sum_ctx(output_sum)
    input_grad = last(meta, in_blocks, kv_blocks, qkv, inputs, attn_gamma)
    kv_part = links.scatter_x(after(kv_both, (in_blocks[3], gate_weight_grad)), 0)
    up_part = after(up_part, (input_grad, out_blocks[3]))
    up_weight_grad = links.lay_weight(up_part, up_got).T
    out_blocks[0] = after(out_blocks[0], (output_sum, q_total))
    kv_total = links.sum_ctx(after(kv_part, input_grad))
    outputs = spread_out(meta, out_blocks, seq_count, LOW)
    query_weight_grad = q_total[:shard]
    part = head_dim // fsdps
    query_bias_grad = lax.dynamic_slice_in_dim(
        q_total[shard].reshape(local_heads, head_dim), fsdp * part, part, 1
    )
    kv_weight = kv_total[:shard]
    gains = kv_total[shard : shard + 2, :shard]
    kv_bias = kv_total[shard + 2].reshape(2, kv_heads, head_dim)
    kv_bias = lax.dynamic_slice_in_dim(kv_bias, fsdp * part, part, 2)
    half = kv_cols // 2

    return (
        outputs,
        input_grad,
        gains[0],
        query_weight_grad,
        query_bias_grad,
        kv_weight[:, :half],
        kv_bias[0],
        kv_weight[:, half:],
        kv_bias[1],
        output_weight_grad,
        gains[1],
        gate_weight_grad,
        up_weight_grad,
        down_weight_grad,
    )


def solution(mesh):
    in_specs = (
        P("fsdp", "ctx", None),
        P("fsdp", "ctx", None),
        P("fsdp", "ctx"),
        P("fsdp"),
        P("fsdp", "tp"),
        P("tp", "fsdp"),
        P("fsdp", None),
        P(None, "fsdp"),
        P("fsdp", None),
        P(None, "fsdp"),
        P("tp", "fsdp"),
        P("fsdp"),
        P("fsdp", "tp"),
        P("fsdp", "tp"),
        P("tp", "fsdp"),
    )
    out_specs = (
        P("fsdp", "ctx", None),
        P("fsdp", "ctx", None),
        P("fsdp"),
        P("fsdp", "tp"),
        P("tp", "fsdp"),
        P("fsdp", None),
        P(None, "fsdp"),
        P("fsdp", None),
        P(None, "fsdp"),
        P("tp", "fsdp"),
        P("fsdp"),
        P("fsdp", "tp"),
        P("fsdp", "tp"),
        P("tp", "fsdp"),
    )
    return jax.shard_map(local, mesh=mesh, in_specs=in_specs, out_specs=out_specs, check_vma=False)
```
